32 devices in a mesh: dp: 4 (over y, x), ctx: 2 (over core), tensor: 4 (over z).
Axes of the slice: x: 2, y: 2, z: 4, core: 2. Of those that a mesh axis runs over, the one named last changes fastest.
Arguments:
- layer_input: float32 [8, 1024, 768], P('dp', 'ctx'), may hold values from -6 to 6
- segment_ids: int32 [8, 1024], P('dp', 'ctx'), may hold values from 0 to 4, never falling along the last dimension, each value on 1 to 512 neighbouring positions
- mixer_gain: float32 [768], P(('dp', 'ctx')), may hold values from 0.25 to 1.75
- query_weight: float32 [768, 768], P(('dp', 'ctx'), 'tensor'), may hold values from -0.21875 to 0.21875
- key_weight: float32 [768, 768], P(('dp', 'ctx'), 'tensor'), may hold values from -0.21875 to 0.21875
- value_weight: float32 [768, 768], P(('dp', 'ctx'), 'tensor'), may hold values from -0.21875 to 0.21875
- shift_kernel: float32 [4, 768], P(None, ('tensor', 'dp', 'ctx')), may hold values from -3 to 3
- state_decay: float32 [12, 64], P('tensor'), may hold values from 0.95 to 1, as said below
- mixer_weight: float32 [768, 768], P('tensor', ('dp', 'ctx')), may hold values from -0.0017089844 to 0.0017089844
- feed_gain: float32 [768], P(('dp', 'ctx')), may hold values from 0.25 to 1.75
- up_weight: float32 [768, 3072], P(('dp', 'ctx'), 'tensor'), may hold values from -0.21875 to 0.21875
- down_weight: float32 [3072, 768], P('tensor', ('dp', 'ctx')), may hold values from -0.109375 to 0.109375
- cotangent: float32 [8, 1024, 768], P('dp', 'ctx'), may hold values from -6 to 6
Outputs:
- layer_output: float32 [8, 1024, 768], P('dp', 'ctx')
- input_grad: float32 [8, 1024, 768], P('dp', 'ctx')
- mixer_gain_grad: float32 [768], P(('dp', 'ctx'))
- query_weight_grad: float32 [768, 768], P(('dp', 'ctx'), 'tensor')
- key_weight_grad: float32 [768, 768], P(('dp', 'ctx'), 'tensor')
- value_weight_grad: float32 [768, 768], P(('dp', 'ctx'), 'tensor')
- shift_kernel_grad: float32 [4, 768], P(None, ('tensor', 'dp', 'ctx'))
- mixer_weight_grad: float32 [768, 768], P('tensor', ('dp', 'ctx'))
- feed_gain_grad: float32 [768], P(('dp', 'ctx'))
- up_weight_grad: float32 [768, 3072], P(('dp', 'ctx'), 'tensor')
- down_weight_grad: float32 [3072, 768], P('tensor', ('dp', 'ctx'))
The draws below stay inside these ranges and needn't reach their ends.
Inputs may be any that keep to these rules, and one draw needn't show every extreme that they name: `segment_ids`: along each sequence the numbers never fall; a document is one run of equal numbers. `state_decay`: each decay is exp(-1 / r) for a horizon r of 24 positions or more.
All inputs are finite; a program needn't handle non-finite values.
Results may differ from the reference program's by a relative error of at most 0.0003.
Values sent between devices are 32-bit elements; how exact they have to be, the bound alone decides.
No kernel may reach another device: no remote copies, remote signals or barrier semaphores. Data moves between devices by JAX's collectives and lax.ppermute only.
A program may use at most 128 MiB of HBM per device.

```python
import math
import jax
import jax.numpy as jnp
import numpy as np
from jax import lax

D = 768
HEADS = 12
HEAD = 64
FF = 3072
TAPS = 4
SUBBLOCK = 64
SEQ = 1024
SEQUENCES = 8


def draw_state_decay(key, part):
    uniform_draw = jax.random.uniform(key, (HEADS, HEAD), jnp.float32)
    low_end = jnp.log(24.0)
    high_end = jnp.log(32.0 * SEQ)
    horizon = jnp.exp(low_end + (high_end - low_end) * uniform_draw)
    return jnp.exp(-1.0 / horizon)


def block_scale(key, extent, cuts, low, largest):
    def one(dim, parts):
        heights = jax.random.uniform(jax.random.fold_in(jax.random.fold_in(key, 6), dim), (parts,), jnp.float32, low / len(cuts), largest / len(cuts))
        return jnp.repeat(jnp.exp(heights), extent[dim] // parts).reshape((-1,) + (1,) * (len(extent) - dim - 1))

    loudness = one(*cuts[0])
    for cut in cuts[1:]:
        loudness = loudness * one(*cut)
    return loudness


def profile(count, total, bound, skew):
    weights = [(1 << 20) // math.isqrt(rank ** skew) + 1 for rank in range(2, count + 1)]
    spare, counts = total - bound - (count - 1), [1] * (count - 1)
    while spare > 0:
        free = [i for i in range(count - 1) if counts[i] < bound]
        pool, budget = sum([weights[i] for i in free]), spare
        for i in free:
            more = min(bound - counts[i], max(1, budget * weights[i] // pool), spare)
            counts[i] = counts[i] + more
            spare = spare - more
    return np.array([bound] + counts)


def uneven(rng, number_of, total, most, slope):
    if number_of == 2:
        one = jax.random.randint(rng, (), max(1, total - most), min(most, total - 1) + 1)
        return jnp.stack([one, total - one])
    lengths = jnp.asarray(profile(number_of, total, most, slope), jnp.int32)
    couples = (number_of - 1) // 2
    source_of, taker = lengths[1:1 + 2 * couples:2], lengths[2:2 + 2 * couples:2]
    margin = jnp.minimum(source_of - 1, most - taker)
    moved = jax.random.randint(jax.random.fold_in(rng, 1), (couples,), 0, 1 << 20) % (margin + 1)
    lengths = lengths.at[1:1 + 2 * couples:2].set(source_of - moved).at[2:2 + 2 * couples:2].set(taker + moved)
    return lengths[jax.random.permutation(jax.random.fold_in(rng, 2), number_of)]


def gaussian(rng, dims, scale, limit, split=(), kind=jnp.bfloat16):
    values = scale * jax.random.normal(rng, dims, jnp.float32)
    if split:
        values = values * block_scale(rng, dims, split, -0.22, 0.18)
    return jnp.clip(values, -limit, limit).astype(kind)


def setup_inputs(seed: int = 0) -> dict:
    seeds = jax.random.split(jax.random.key(seed), 14)
    return {
        "layer_input": gaussian(seeds[0], (SEQUENCES, SEQ, D), 1.0, 6.0, ((0, 4), (1, 2)), jnp.float32),
        "segment_ids": jax.vmap(lambda own: jnp.searchsorted(jnp.cumsum(uneven(own, SEQ // 512 + 3, SEQ, min(2000, SEQ // 2), 1)), jnp.arange(SEQ), side="right"))(jax.random.split(seeds[1], SEQUENCES)).reshape((SEQUENCES, SEQ)).astype(jnp.int32),
        "mixer_gain": jnp.clip(1.0 + 0.15 * jax.random.normal(seeds[2], (D,), jnp.float32), 0.25, 1.75),
        "query_weight": gaussian(seeds[3], (D, D), D ** -0.5, 0.21875, ((0, 8), (1, 4)), jnp.float32),
        "key_weight": gaussian(seeds[4], (D, D), D ** -0.5, 0.21875, ((0, 8), (1, 4)), jnp.float32),
        "value_weight": gaussian(seeds[5], (D, D), D ** -0.5, 0.21875, ((0, 8), (1, 4)), jnp.float32),
        "shift_kernel": gaussian(seeds[6], (TAPS, D), 0.5, 3.0, ((1, 32),), jnp.float32),
        "state_decay": draw_state_decay(jax.random.fold_in(seeds[13], 71), 0),
        "mixer_weight": gaussian(seeds[8], (D, D), (D * HEAD * 256) ** -0.5, 0.0017089844, ((0, 4), (1, 8)), jnp.float32),
        "feed_gain": jnp.clip(1.0 + 0.15 * jax.random.normal(seeds[9], (D,), jnp.float32), 0.25, 1.75),
        "up_weight": gaussian(seeds[10], (D, FF), D ** -0.5, 0.21875, ((0, 8), (1, 4)), jnp.float32),
        "down_weight": gaussian(seeds[11], (FF, D), FF ** -0.5, 0.109375, ((0, 4), (1, 8)), jnp.float32),
        "cotangent": gaussian(seeds[12], (SEQUENCES, SEQ, D), 1.0, 6.0, ((0, 4), (1, 2)), jnp.float32),
    }


eps = 1e-05
precise = lax.Precision.HIGHEST

@jax.custom_vjp
def low(v):
    return lax.optimization_barrier(v.astype(jnp.bfloat16)).astype(jnp.float32)

@jax.custom_vjp
def low_back(v):
    return v

def low_keep(v):
    return (low(v), None)

def low_pass(kept, grad):
    return (grad,)

def back_keep(v):
    return (v, None)

def back_low(kept, grad):
    return (low(grad),)
low.defvjp(low_keep, low_pass)
low_back.defvjp(back_keep, back_low)

def normalize(inputs, gain):
    centered = inputs - lax.optimization_barrier(jnp.mean(inputs, axis=-1, keepdims=True))
    scaled = centered * lax.rsqrt(lax.optimization_barrier(jnp.mean(centered * centered, axis=-1, keepdims=True)) + eps)
    return scaled * gain

def project(left, right):
    return jnp.dot(left, right, precision=precise, preferred_element_type=left.dtype)

def shift_keys(keys, kernel, segments):
    taps = kernel.shape[0]
    length = keys.shape[0]
    padded = jnp.concatenate([jnp.zeros((taps - 1, keys.shape[1]), keys.dtype), keys], axis=0)
    seg_pad = jnp.concatenate([jnp.full((taps - 1,), -1, jnp.int32), segments.astype(jnp.int32)], axis=0)
    summed = jnp.zeros_like(keys)
    for offset in range(taps):
        begin = taps - 1 - offset
        joined = (seg_pad[begin:begin + length] == segments).astype(keys.dtype)
        summed = summed + kernel[offset] * padded[begin:begin + length] * joined[:, None]
    return summed

def state_mixer(queries, shifted, values, segments, log_decay):
    length = queries.shape[0]
    heads, width = log_decay.shape
    pieces = length // SUBBLOCK
    dtype = queries.dtype
    query_sections = queries.reshape(pieces, SUBBLOCK, heads, width)
    key_sections = shifted.reshape(pieces, SUBBLOCK, heads, width)
    value_sections = values.reshape(pieces, SUBBLOCK, heads, width)
    seg_sections = segments.astype(jnp.int32).reshape(pieces, SUBBLOCK)
    position = jnp.arange(SUBBLOCK).astype(dtype)
    causal = position[:, None] >= position[None, :]
    growing = jnp.exp(position[:, None, None] * log_decay)
    shrinking = jnp.exp(-position[:, None, None] * log_decay)
    step_in = jnp.exp((position + 1.0)[:, None, None] * log_decay)
    closing = jnp.exp((SUBBLOCK - 1.0 - position)[:, None, None] * log_decay)
    full_decay = jnp.exp(SUBBLOCK * log_decay)

    @jax.checkpoint
    def advance(carry, section):
        state, before = carry
        query_part, key_part, value_part, seg_part = section
        allowed = jnp.logical_and(seg_part[:, None] == seg_part[None, :], causal).astype(dtype)
        scores = jnp.einsum('thi,shi->hts', query_part * growing, key_part * shrinking, precision=precise)
        scores = scores * allowed[None]
        within = jnp.einsum('hts,shj->thj', scores, value_part, precision=precise)
        living = (seg_part == before).astype(dtype)
        across = jnp.einsum('thi,hij->thj', query_part * step_in * living[:, None, None], state, precision=precise)
        retained = (seg_part == seg_part[-1]).astype(dtype)
        update = jnp.einsum('thi,thj->hij', key_part * closing * retained[:, None, None], value_part, precision=precise)
        state = (full_decay * living[-1])[:, :, None] * state + update
        return ((state, seg_part[-1]), within + across)
    start = (jnp.zeros((heads, width, width), dtype), jnp.array(-1, jnp.int32))
    _, mixed = lax.scan(advance, start, (query_sections, key_sections, value_sections, seg_sections))
    return mixed.reshape(length, heads * width)

def layer(params, inputs, segments, log_decay):
    mixer_gain, query_weight, key_weight, value_weight, shift_kernel, mixer_weight, feed_gain, up_weight, down_weight = params
    normed = normalize(inputs, mixer_gain)
    queries = project(normed, query_weight)
    keys = project(normed, key_weight)
    values = project(normed, value_weight)
    shifted = shift_keys(keys, shift_kernel, segments)
    mixed = state_mixer(queries, shifted, values, segments, log_decay)
    resid = inputs + project(mixed, mixer_weight)
    normed_feed = normalize(resid, feed_gain)
    activated = jax.nn.gelu(project(normed_feed, up_weight), approximate=True)
    return resid + project(activated, down_weight)

def reference(layer_input, segment_ids, mixer_gain, query_weight, key_weight, value_weight, shift_kernel, state_decay, mixer_weight, feed_gain, up_weight, down_weight, cotangent):
    params = (mixer_gain, query_weight, key_weight, value_weight, shift_kernel, mixer_weight, feed_gain, up_weight, down_weight)
    log_decay = jnp.log(state_decay)
    zeros = jax.tree.map(jnp.zeros_like, params)

    def per_sequence(summed, section):
        inputs, segments, upstream = section

        def run(weights, acts):
            return layer(weights, acts, segments, log_decay)
        result, back = jax.vjp(run, params, inputs)
        grads, in_grad = back(upstream)
        summed = jax.tree.map(jnp.add, summed, grads)
        return (summed, (result, in_grad))
    summed, (outputs, input_grads) = lax.scan(per_sequence, zeros, (layer_input, segment_ids, cotangent))
    return (outputs, input_grads, summed[0], summed[1], summed[2], summed[3], summed[4], summed[5], summed[6], summed[7], summed[8])
```

```python
from functools import partial

import jax
import jax.numpy as jnp
from jax import lax
from jax.experimental import pallas as pl
from jax.experimental.pallas import tpu as pltpu
from jax.sharding import PartitionSpec as P

SUBBLOCK = 64


eps = 1e-05
precise = lax.Precision.HIGHEST


def passed_along(value, axis, steps):
    count = lax.axis_size(axis)
    leading, last = (max(0, -steps), min(count, count - steps))
    return lax.ppermute(value, axis, [(source, source + steps) for source in range(leading, last)])


def carried_in(value, axis, join, neutral, backward):
    count, mine = (lax.axis_size(axis), lax.axis_index(axis))
    pieces = jax.tree.map(lambda part: lax.all_gather(part, axis), value)
    if backward:
        pieces = jax.tree.map(lambda part: part[::-1], pieces)
        mine = count - 1 - mine
    subtotal = jax.tree.map(
        lambda part, zero: jnp.full_like(part, 0) + jnp.asarray(zero, part.dtype), value, neutral
    )

    def step(position, subtotal):
        longer = join(subtotal, jax.tree.map(lambda part: part[position], pieces))
        return jax.tree.map(lambda new, old: jnp.where(position < mine, new, old), longer, subtotal)

    return lax.fori_loop(0, count - 1, step, subtotal)


def normalize(inputs, gain):
    centered = inputs - jnp.mean(inputs, axis=-1, keepdims=True)
    scaled = centered * lax.rsqrt(jnp.mean(centered * centered, axis=-1, keepdims=True) + eps)
    return scaled * gain


def project(left, right):
    return jnp.einsum(
        "btd,df->btf", left, right, precision=precise, preferred_element_type=jnp.float32
    )


def outer_sum(left, right):
    return jnp.einsum(
        "btd,btf->df", left, right, precision=precise, preferred_element_type=jnp.float32
    )


def smooth_gate(inputs):
    return jax.nn.gelu(inputs, approximate=True)


def shift_keys(extended, kernel, seg_ext):
    taps = kernel.shape[0]
    length = extended.shape[1] - taps + 1
    current = seg_ext[:, taps - 1 :]
    summed = jnp.zeros((extended.shape[0], length, extended.shape[2]), jnp.float32)
    for offset in range(taps):
        begin = taps - 1 - offset
        joined = (seg_ext[:, begin : begin + length] == current).astype(jnp.float32)
        summed = summed + kernel[offset] * extended[:, begin : begin + length] * joined[:, :, None]
    return summed


def compose(earlier, later):
    return (earlier[0] * later[0], later[0][..., None] * earlier[1] + later[1])


def geometry(segments, before_block, log_decay):
    rows, length = segments.shape
    pieces = length // SUBBLOCK
    grouped = segments.reshape(rows, pieces, SUBBLOCK)
    before = jnp.concatenate([before_block[:, None], grouped[:, :-1, -1]], axis=1)
    living = (grouped == before[:, :, None]).astype(jnp.float32)
    retained = (grouped == grouped[:, :, -1:]).astype(jnp.float32)
    position = jnp.arange(SUBBLOCK, dtype=jnp.float32)
    causal = position[:, None] >= position[None, :]
    allowed = jnp.logical_and(grouped[:, :, :, None] == grouped[:, :, None, :], causal).astype(
        jnp.float32
    )
    growing = jnp.exp(position[:, None, None] * log_decay)
    shrinking = jnp.exp(-position[:, None, None] * log_decay)
    step_in = growing * jnp.exp(log_decay)
    closing = jnp.exp((SUBBLOCK - 1.0 - position)[:, None, None] * log_decay)
    whole_decay = jnp.exp(SUBBLOCK * log_decay)[None, None] * living[:, :, -1][:, :, None, None]
    running = jnp.ones((rows,) + log_decay.shape, jnp.float32)
    carried = []
    for index in range(pieces):
        carried.append(running)
        running = running * whole_decay[:, index]
    return (
        living,
        retained,
        allowed,
        growing,
        shrinking,
        step_in,
        closing,
        whole_decay,
        jnp.stack(carried, axis=1),
        running,
    )


def local_part(queries, shifted, values, shape_info):
    (
        living,
        retained,
        allowed,
        growing,
        shrinking,
        step_in,
        closing,
        whole_decay,
        carried,
        block_decay,
    ) = shape_info
    scores = jnp.einsum(
        "bncgi,bnsgi->bngcs", queries * growing, shifted * shrinking, precision=precise
    )
    scores = scores * allowed[:, :, None]
    within = jnp.einsum("bngcs,bnsgj->bncgj", scores, values, precision=precise)
    update = jnp.einsum(
        "bncgi,bncgj->bngij",
        shifted * closing * retained[..., None, None],
        values,
        precision=precise,
    )
    running = jnp.zeros_like(update[:, 0])
    starts = []
    for index in range(update.shape[1]):
        starts.append(running)
        running = whole_decay[:, index][..., None] * running + update[:, index]
    return (within, jnp.stack(starts, axis=1), running)


def across(queries, starts, state_in, shape_info):
    (
        living,
        retained,
        allowed,
        growing,
        shrinking,
        step_in,
        closing,
        whole_decay,
        carried,
        block_decay,
    ) = shape_info
    entries = starts + carried[..., None] * state_in[:, None]
    weighted = queries * step_in * living[..., None, None]
    return jnp.einsum("bncgi,bngij->bncgj", weighted, entries, precision=precise)


def on_device(
    layer_input,
    segment_ids,
    mixer_gain,
    query_weight,
    key_weight,
    value_weight,
    shift_kernel,
    state_decay,
    mixer_weight,
    feed_gain,
    up_weight,
    down_weight,
    cotangent,
):
    (
        mixer_gain_all,
        query_all,
        key_all,
        value_all,
        kernel_all,
        mixer_all,
        feed_gain_all,
        up_all,
        down_all,
    ) = (
        lax.all_gather(mixer_gain, ("dp", "ctx"), axis=0, tiled=True),
        lax.all_gather(query_weight, ("dp", "ctx"), axis=0, tiled=True),
        lax.all_gather(key_weight, ("dp", "ctx"), axis=0, tiled=True),
        lax.all_gather(value_weight, ("dp", "ctx"), axis=0, tiled=True),
        lax.all_gather(shift_kernel, ("dp", "ctx"), axis=1, tiled=True),
        lax.all_gather(mixer_weight, ("dp", "ctx"), axis=1, tiled=True),
        lax.all_gather(feed_gain, ("dp", "ctx"), axis=0, tiled=True),
        lax.all_gather(up_weight, ("dp", "ctx"), axis=0, tiled=True),
        lax.all_gather(down_weight, ("dp", "ctx"), axis=1, tiled=True),
    )
    heads, width = state_decay.shape
    log_decay = jnp.log(state_decay)
    taps = kernel_all.shape[0]
    rows, length, model = layer_input.shape
    pieces = length // SUBBLOCK
    features = heads * width
    seg_float = segment_ids.astype(jnp.float32)
    joint_weight = jnp.concatenate([query_all, key_all, value_all], axis=1)
    normed = normalize(layer_input, mixer_gain_all)
    projected = project(normed, joint_weight)
    queries = projected[:, :, :features]
    keys_raw = projected[:, :, features : 2 * features]
    values = projected[:, :, 2 * features :]
    tail_keys, tail_segs = passed_along(
        (keys_raw[:, length - taps + 1 :], seg_float[:, length - taps + 1 :]), "ctx", 1
    )
    extended = jnp.concatenate([tail_keys, keys_raw], axis=1)
    seg_ext = jnp.concatenate([tail_segs, seg_float], axis=1)
    shift_fixed = partial(shift_keys, seg_ext=seg_ext)
    shifted = shift_fixed(extended, kernel_all)
    info = geometry(seg_float, tail_segs[:, -1], log_decay)
    block_decay = info[-1]
    head_q = queries.reshape(rows, pieces, SUBBLOCK, heads, width)
    head_k = shifted.reshape(rows, pieces, SUBBLOCK, heads, width)
    head_v = values.reshape(rows, pieces, SUBBLOCK, heads, width)
    within, starts, local_end = local_part(head_q, head_k, head_v, info)
    identity = (jnp.ones_like(block_decay), jnp.zeros_like(local_end))
    state_in = carried_in((block_decay, local_end), "ctx", compose, identity, False)[1]
    mixed = (within + across(head_q, starts, state_in, info)).reshape(rows, length, features)
    branch = lax.psum(project(mixed, mixer_all), "tensor")
    resid = layer_input + branch
    normed_feed = normalize(resid, feed_gain_all)
    pre_act = project(normed_feed, up_all)
    activated, gelu_back = jax.vjp(smooth_gate, pre_act)
    feed = lax.psum(project(activated, down_all), "tensor")
    layer_output = resid + feed
    act_grad = project(cotangent, down_all.T)
    down_grad = outer_sum(activated, cotangent)
    (pre_grad,) = gelu_back(act_grad)
    up_grad = outer_sum(normed_feed, pre_grad)
    feed_normed_grad = lax.psum(project(pre_grad, up_all.T), "tensor")
    _, feed_norm_back = jax.vjp(normalize, resid, feed_gain_all)
    resid_ln_grad, feed_gain_grad = feed_norm_back(feed_normed_grad)
    resid_grad = cotangent + resid_ln_grad
    mixed_grad = project(resid_grad, mixer_all.T)
    mixer_weight_grad = outer_sum(mixed, resid_grad)
    head_du = mixed_grad.reshape(rows, pieces, SUBBLOCK, heads, width)
    (
        living,
        retained,
        allowed,
        growing,
        shrinking,
        step_in,
        closing,
        whole_decay,
        carried,
        block_decay,
    ) = info
    own_grad = jnp.einsum(
        "bncgi,bncgj,bngi->bgij",
        head_q * step_in * living[..., None, None],
        head_du,
        carried,
        precision=precise,
    )
    identity_grad = (jnp.ones_like(block_decay), jnp.zeros_like(own_grad))
    after = carried_in((block_decay, own_grad), "ctx", compose, identity_grad, True)[1]

    def mixer_full(query_in, key_in, value_in, entering):
        inner, begins, ending = local_part(query_in, key_in, value_in, info)
        output = inner + across(query_in, begins, entering, info)
        return (output, ending + block_decay[..., None] * entering)

    _, mixer_vjp = jax.vjp(mixer_full, head_q, head_k, head_v, state_in)
    query_act_grad, shifted_grad, value_act_grad, _ = mixer_vjp((head_du, after))
    _, shift_back = jax.vjp(shift_fixed, extended, kernel_all)
    ext_grad, kernel_grad = shift_back(shifted_grad.reshape(rows, length, features))
    returned = passed_along(ext_grad[:, : taps - 1], "ctx", -1)
    key_act_grad = ext_grad[:, taps - 1 :] + jnp.pad(
        returned, ((0, 0), (length - taps + 1, 0), (0, 0))
    )
    joint_grad = jnp.concatenate(
        [
            query_act_grad.reshape(rows, length, features),
            key_act_grad,
            value_act_grad.reshape(rows, length, features),
        ],
        axis=2,
    )
    joint_weight_grad = outer_sum(normed, joint_grad)
    normed_grad = lax.psum(project(joint_grad, joint_weight.T), "tensor")
    _, mixer_norm_back = jax.vjp(normalize, layer_input, mixer_gain_all)
    input_ln_grad, mixer_gain_grad = mixer_norm_back(normed_grad)
    input_grad = resid_grad + input_ln_grad
    query_grad = joint_weight_grad[:, :features]
    key_grad = joint_weight_grad[:, features : 2 * features]
    value_grad = joint_weight_grad[:, 2 * features :]
    all_parts = tuple(
        (
            lax.psum_scatter(mixer_gain_grad, ("dp", "ctx"), scatter_dimension=0, tiled=True),
            lax.psum_scatter(query_grad, ("dp", "ctx"), scatter_dimension=0, tiled=True),
            lax.psum_scatter(key_grad, ("dp", "ctx"), scatter_dimension=0, tiled=True),
            lax.psum_scatter(value_grad, ("dp", "ctx"), scatter_dimension=0, tiled=True),
            lax.psum_scatter(kernel_grad, ("dp", "ctx"), scatter_dimension=1, tiled=True),
            lax.psum_scatter(mixer_weight_grad, ("dp", "ctx"), scatter_dimension=1, tiled=True),
            lax.psum_scatter(feed_gain_grad, ("dp", "ctx"), scatter_dimension=0, tiled=True),
            lax.psum_scatter(up_grad, ("dp", "ctx"), scatter_dimension=0, tiled=True),
            lax.psum_scatter(down_grad, ("dp", "ctx"), scatter_dimension=1, tiled=True),
        )
    )
    return (layer_output, input_grad) + all_parts


HIGH = lax.Precision.HIGH
GROUP = 4
C_GELU = 0.7978845608028654


def params(limit=58):
    return pltpu.CompilerParams(vmem_limit_bytes=limit * 2**20)


def mm(left, right):
    return jnp.dot(left, right, precision=HIGH, preferred_element_type=jnp.float32)


def mm_nt(left, right):
    return lax.dot_general(
        left, right, (((1,), (1,)), ((), ())), precision=HIGH, preferred_element_type=jnp.float32
    )


def mm_tn(left, right):
    return lax.dot_general(
        left, right, (((0,), (0,)), ((), ())), precision=HIGH, preferred_element_type=jnp.float32
    )


def norm_parts(v):
    centered = v - jnp.mean(v, axis=-1, keepdims=True)
    r = lax.rsqrt(jnp.mean(centered * centered, axis=-1, keepdims=True) + eps)
    return centered * r, r


def whole(shape):
    return pl.BlockSpec(
        shape, lambda *_: (0,) * len(shape), pipeline_mode=pl.Buffered(buffer_count=1)
    )


def project_kernel(x_ref, gain_ref, w_ref, o_ref, n_ref):
    @pl.when(pl.program_id(0) == 0)
    def _():
        n_ref[...] = norm_parts(x_ref[...])[0] * gain_ref[...]

    o_ref[...] = mm(n_ref[...], w_ref[...])


def run_project(x, gain, w):
    tokens, model = x.shape
    wide = w.shape[1]
    tile = 768
    return pl.pallas_call(
        project_kernel,
        grid=(wide // tile,),
        in_specs=[
            whole((tokens, model)),
            whole((1, model)),
            pl.BlockSpec((model, tile), lambda j: (0, j)),
        ],
        out_specs=pl.BlockSpec((tokens, tile), lambda j: (0, j)),
        out_shape=jax.ShapeDtypeStruct((tokens, wide), jnp.float32),
        scratch_shapes=[pltpu.VMEM((tokens, model), jnp.float32)],
        compiler_params=params(),
        name="project",
    )(x, gain, w)


def split(a):
    high = a.astype(jnp.bfloat16)
    return high, (a - high.astype(jnp.float32)).astype(jnp.bfloat16)


def spread(pair, mask):
    return tuple(jnp.concatenate([p] * GROUP, axis=0) * mask for p in pair)


def d3(left, right, dims):
    dot = partial(
        lax.dot_general, dimension_numbers=(dims, ((), ())), preferred_element_type=jnp.float32
    )
    return dot(left[0], right[0]) + dot(left[1], right[0]) + dot(left[0], right[1])


NN = ((1,), (0,))
NT = ((1,), (1,))
TN = ((0,), (0,))


def shift_forward(k_ref, before, kern_ref, meta, taps):
    keys = k_ref[...]
    extended = jnp.concatenate([before, keys], axis=0)
    size = keys.shape[0]
    moved = [keys]
    for j in range(1, taps):
        moved.append(extended[8 - j : 8 - j + size] * meta[:, 2 + j : 3 + j])
    total = kern_ref[0:1, :] * keys
    for j in range(1, taps):
        total = total + kern_ref[j : j + 1, :] * moved[j]
    return total, moved


def compact(full, mask, width):
    kept = full * mask
    out = kept[0:width]
    for h in range(1, GROUP):
        out = out + kept[h * width : (h + 1) * width]
    return out


def mixer_kernel(
    taps, q_ref, k_ref, v_ref, meta_ref, segrow_ref, kern_ref, grow_ref, shrink_ref,
    dec_ref, end_ref, all_ref, mask_ref, maskf_ref, mixed_ref, state_out_ref, state, tail,
):
    size, model = k_ref.shape
    span = mask_ref.shape[0]
    width = span // GROUP

    @pl.when(pl.program_id(0) == 0)
    def _():
        state[...] = jnp.zeros_like(state)
        tail[...] = jnp.zeros_like(tail)

    meta = meta_ref[...]
    shifted, _ = shift_forward(k_ref, tail[...], kern_ref, meta, taps)
    tail[...] = k_ref[size - 8 :, :]
    rows = lax.broadcasted_iota(jnp.int32, (size, span), 0)
    cols = lax.broadcasted_iota(jnp.int32, (size, span), 1) % size
    living, kept = meta[:, 1:2], meta[:, 2:3]
    allowed = jnp.where(
        jnp.logical_and(rows >= cols, meta[:, 0:1] == segrow_ref[0]), 1.0, 0.0
    )
    mask = mask_ref[...]
    state_out_ref[0] = state[...]
    for g in range(model // span):
        s = slice(g * span, (g + 1) * span)
        qg = split(q_ref[:, s] * grow_ref[:, s])
        kf = shifted[:, s] * shrink_ref[:, s]
        kg = split(kf)
        v = split(v_ref[:, s])
        scores = d3(qg, spread(kg, mask), NT) * allowed
        entering = split(state[:, s] * dec_ref[:, s])
        out = d3(split(scores), spread(v, mask), NN)
        out = out + living * d3(qg, spread(entering, mask), NN)
        mixed_ref[:, s] = out
        update = compact(d3(split(kf * kept), v, TN), maskf_ref[...], width)
        state[:, s] = (
            state[:, s] * (all_ref[:, s] * meta[size - 1 : size, 1:2]) + end_ref[:, s] * update
        )


def run_mixer(proj, meta, segrow, kern, tables):
    tokens = proj.shape[0]
    model = proj.shape[1] // 3
    size = tables["grow"].shape[0]
    steps = tokens // size
    taps = kern.shape[0]

    def col(i):
        return pl.BlockSpec((size, model), lambda c: (c, i))

    return pl.pallas_call(
        partial(mixer_kernel, taps),
        grid=(steps,),
        in_specs=[
            col(0), col(1), col(2),
            pl.BlockSpec((size, meta.shape[1]), lambda c: (c, 0)),
            pl.BlockSpec((1, 1, segrow.shape[2]), lambda c: (c, 0, 0)),
        ]
        + [whole(a.shape) for a in (kern, *tables.values())],
        out_specs=[
            pl.BlockSpec((size, model), lambda c: (c, 0)),
            pl.BlockSpec((1, size, model), lambda c: (c, 0, 0)),
        ],
        out_shape=[
            jax.ShapeDtypeStruct((tokens, model), jnp.float32),
            jax.ShapeDtypeStruct((steps, size, model), jnp.float32),
        ],
        scratch_shapes=[pltpu.VMEM((size, model), jnp.float32), pltpu.VMEM((8, model), jnp.float32)],
        compiler_params=params(),
        name="mixer",
    )(proj, proj, proj, meta, segrow, kern, *tables.values())


def mixer_back_kernel(
    taps, q_ref, k_ref, v_ref, du_ref, before_ref, state_ref, meta_ref, segrow_ref, kern_ref,
    grow_ref, shrink_ref, dec_ref, end_ref, all_ref, mask_ref, maskf_ref,
    dq_ref, dk_ref, dv_ref, dkern_ref, grad, head,
):
    size, model = k_ref.shape
    span = mask_ref.shape[0]
    width = span // GROUP

    @pl.when(pl.program_id(0) == 0)
    def _():
        grad[...] = jnp.zeros_like(grad)
        head[...] = jnp.zeros_like(head)
        dkern_ref[...] = jnp.zeros_like(dkern_ref)

    meta = meta_ref[...]
    shifted, moved = shift_forward(k_ref, before_ref[...], kern_ref, meta, taps)
    rows = lax.broadcasted_iota(jnp.int32, (size, span), 0)
    cols = lax.broadcasted_iota(jnp.int32, (size, span), 1) % size
    same = meta[:, 0:1] == segrow_ref[0]
    living, kept = meta[:, 1:2], meta[:, 2:3]
    allowed = jnp.where(jnp.logical_and(rows >= cols, same), 1.0, 0.0)
    allowed_t = jnp.where(jnp.logical_and(rows <= cols, same), 1.0, 0.0)
    mask = mask_ref[...]
    for g in range(model // span):
        s = slice(g * span, (g + 1) * span)
        qf = q_ref[:, s] * grow_ref[:, s]
        qg = split(qf)
        kg = split(shifted[:, s] * shrink_ref[:, s])
        v = split(v_ref[:, s])
        du = split(du_ref[:, s])
        q_bd, k_bd, v_bd, u_bd = (spread(p, mask) for p in (qg, kg, v, du))
        s_bd = spread(split(state_ref[0, :, s] * dec_ref[:, s]), mask)
        g_bd = spread(split(grad[:, s] * end_ref[:, s]), mask)
        p_t = d3(kg, q_bd, NT) * allowed_t
        dp = d3(du, v_bd, NT) * allowed
        dp_t = d3(v, u_bd, NT) * allowed_t
        dqg = d3(split(dp), k_bd, NN) + living * d3(du, s_bd, NT)
        dkg = d3(split(dp_t), q_bd, NN) + kept * d3(v, g_bd, NT)
        dv_ref[:, s] = d3(split(p_t), u_bd, NN) + kept * d3(kg, g_bd, NN)
        dq_ref[:, s] = dqg * grow_ref[:, s]
        dshift = dkg * shrink_ref[:, s]
        update = compact(d3(split(qf * living), du, TN), maskf_ref[...], width)
        grad[:, s] = (
            grad[:, s] * (all_ref[:, s] * meta[size - 1 : size, 1:2]) + dec_ref[:, s] * update
        )
        total = kern_ref[0:1, s] * dshift
        for j in range(1, taps):
            part = dshift * meta[:, 2 + j : 3 + j]
            extended = jnp.concatenate([part, head[j - 1, :, s]], axis=0)
            total = total + kern_ref[j : j + 1, s] * extended[j : j + size]
            head[j - 1, :, s] = part[0:8]
        dk_ref[:, s] = total
        for j in range(taps):
            dkern_ref[j : j + 1, s] += jnp.sum(dshift * moved[j][:, s], axis=0, keepdims=True)


def run_mixer_back(proj, du, states, meta, segrow, kern, tables):
    tokens = proj.shape[0]
    model = proj.shape[1] // 3
    size = tables["grow"].shape[0]
    steps = tokens // size
    taps = kern.shape[0]
    last = steps - 1

    def col(i):
        return pl.BlockSpec((size, model), lambda c: (last - c, i))

    return pl.pallas_call(
        partial(mixer_back_kernel, taps),
        grid=(steps,),
        in_specs=[
            col(0), col(1), col(2), col(0),
            pl.BlockSpec((8, model), lambda c: (jnp.maximum((last - c) * (size // 8) - 1, 0), 1)),
            pl.BlockSpec((1, size, model), lambda c: (last - c, 0, 0)),
            pl.BlockSpec((size, meta.shape[1]), lambda c: (last - c, 0)),
            pl.BlockSpec((1, 1, segrow.shape[2]), lambda c: (last - c, 0, 0)),
        ]
        + [whole(a.shape) for a in (kern, *tables.values())],
        out_specs=[col(0), col(0), col(0), whole(kern.shape)],
        out_shape=[jax.ShapeDtypeStruct((tokens, model), jnp.float32)] * 3
        + [jax.ShapeDtypeStruct(kern.shape, jnp.float32)],
        scratch_shapes=[
            pltpu.VMEM((size, model), jnp.float32),
            pltpu.VMEM((taps - 1, 8, model), jnp.float32),
        ],
        compiler_params=params(),
        name="mixer_back",
    )(proj, proj, proj, du, proj, states, meta, segrow, kern, *tables.values())


def branch_kernel(x_ref, m_ref, w_ref, gain_ref, resid_ref, n_ref):
    resid = x_ref[...] + mm_nt(m_ref[...], w_ref[...])
    resid_ref[...] = resid
    n_ref[...] = norm_parts(resid)[0] * gain_ref[...]


def run_branch(x, mixed, w, gain):
    tokens, model = x.shape
    tile = 256
    row = pl.BlockSpec((tile, model), lambda i: (i, 0))
    return pl.pallas_call(
        branch_kernel,
        grid=(tokens // tile,),
        in_specs=[row, row, whole(w.shape), whole(gain.shape)],
        out_specs=[row, row],
        out_shape=[jax.ShapeDtypeStruct(x.shape, jnp.float32)] * 2,
        compiler_params=params(),
        name="branch",
    )(x, mixed, w, gain)


def feed_kernel(own, n_ref, ct_ref, resid_ref, up_ref, down_ref, out_ref, fng_ref, dg_ref, ug_ref):
    step = pl.program_id(0)

    @pl.when(step == 0)
    def _():
        out_ref[...] = resid_ref[...]
        fng_ref[...] = jnp.zeros_like(fng_ref)

    pre = mm(n_ref[...], up_ref[...])
    back = mm(ct_ref[...], down_ref[...])
    th = jnp.tanh(C_GELU * (pre + 0.044715 * (pre * pre * pre)))
    act = 0.5 * pre * (1.0 + th)
    slope = 0.5 * (1.0 + th) + (0.5 * C_GELU) * pre * (1.0 - th * th) * (
        1.0 + (3 * 0.044715) * (pre * pre)
    )
    grad = back * slope
    out_ref[...] += mm_nt(act, down_ref[...])
    fng_ref[...] += mm_nt(grad, up_ref[...])

    @pl.when(step < own)
    def _():
        dg_ref[...] = mm_tn(ct_ref[...], act)
        ug_ref[...] = mm_tn(n_ref[...], grad)


def run_feed(n, ct, resid, up, down, own_width):
    tokens, model = n.shape
    hidden = up.shape[1]
    tile = 256
    own = own_width // tile
    wide = pl.BlockSpec((model, tile), lambda j: (0, j))
    mine = pl.BlockSpec((model, tile), lambda j: (0, jnp.minimum(j, own - 1)))
    act = whole((tokens, model))
    return pl.pallas_call(
        partial(feed_kernel, own),
        grid=(hidden // tile,),
        in_specs=[act, act, act, wide, wide],
        out_specs=[act, act, mine, mine],
        out_shape=[jax.ShapeDtypeStruct((tokens, model), jnp.float32)] * 2
        + [jax.ShapeDtypeStruct((model, own_width), jnp.float32)] * 2,
        compiler_params=params(),
        name="feed",
    )(n, ct, resid, up, down)


def norm_back(v, gain, incoming):
    xhat, r = norm_parts(v)
    scaled = incoming * gain
    grad = r * (
        scaled
        - jnp.mean(scaled, axis=-1, keepdims=True)
        - xhat * jnp.mean(scaled * xhat, axis=-1, keepdims=True)
    )
    return grad, jnp.sum(incoming * xhat, axis=0, keepdims=True), xhat


def resid_back_kernel(fng_ref, resid_ref, ct_ref, gain_ref, w_ref, m_ref, rg_ref, mg_ref, gg_ref, wg_ref):
    @pl.when(pl.program_id(0) == 0)
    def _():
        gg_ref[...] = jnp.zeros_like(gg_ref)
        wg_ref[...] = jnp.zeros_like(wg_ref)

    grad, gain_grad, _ = norm_back(resid_ref[...], gain_ref[...], fng_ref[...])
    rg = ct_ref[...] + grad
    rg_ref[...] = rg
    gg_ref[...] += gain_grad
    mg_ref[...] = mm(rg, w_ref[...])
    wg_ref[...] += mm_tn(rg, m_ref[...])


def run_resid_back(fng, resid, ct, gain, w, mixed, own):
    tokens, model = resid.shape
    tile = 256
    row = pl.BlockSpec((tile, model), lambda i: (i, 0))
    return pl.pallas_call(
        resid_back_kernel,
        grid=(tokens // tile,),
        in_specs=[row, row, row, whole(gain.shape), whole(w.shape), pl.BlockSpec((tile, own), lambda i: (i, 0))],
        out_specs=[row, row, whole(gain.shape), whole((model, own))],
        out_shape=[jax.ShapeDtypeStruct(resid.shape, jnp.float32)] * 2
        + [jax.ShapeDtypeStruct(gain.shape, jnp.float32), jax.ShapeDtypeStruct((model, own), jnp.float32)],
        compiler_params=params(),
        name="resid_back",
    )(fng, resid, ct, gain, w, mixed)


def input_back_kernel(x_ref, rg_ref, gain_ref, w_ref, dq_ref, dk_ref, dv_ref, ig_ref, gg_ref, wg_ref):
    @pl.when(pl.program_id(0) == 0)
    def _():
        gg_ref[...] = jnp.zeros_like(gg_ref)
        wg_ref[...] = jnp.zeros_like(wg_ref)

    model = x_ref.shape[1]
    own = wg_ref.shape[1] // 3
    parts = (dq_ref[...], dk_ref[...], dv_ref[...])
    incoming = mm_nt(parts[0], w_ref[:, 0:model])
    incoming = incoming + mm_nt(parts[1], w_ref[:, model : 2 * model])
    incoming = incoming + mm_nt(parts[2], w_ref[:, 2 * model :])
    grad, gain_grad, xhat = norm_back(x_ref[...], gain_ref[...], incoming)
    ig_ref[...] = rg_ref[...] + grad
    gg_ref[...] += gain_grad
    normed = xhat * gain_ref[...]
    for i in range(3):
        wg_ref[:, i * own : (i + 1) * own] += mm_tn(normed, parts[i][:, 0:own])


def run_input_back(x, rg, gain, w, dq, dk, dv, own):
    tokens, model = x.shape
    tile = 256
    row = pl.BlockSpec((tile, model), lambda i: (i, 0))
    return pl.pallas_call(
        input_back_kernel,
        grid=(tokens // tile,),
        in_specs=[row, row, whole(gain.shape), whole(w.shape), row, row, row],
        out_specs=[row, whole(gain.shape), whole((model, 3 * own))],
        out_shape=[
            jax.ShapeDtypeStruct(x.shape, jnp.float32),
            jax.ShapeDtypeStruct(gain.shape, jnp.float32),
            jax.ShapeDtypeStruct((model, 3 * own), jnp.float32),
        ],
        compiler_params=params(),
        name="input_back",
    )(x, rg, gain, w, dq, dk, dv)


def gather_weights(
    mixer_gain, query_weight, key_weight, value_weight, shift_kernel, state_decay, mixer_weight,
    feed_gain, up_weight, down_weight,
):
    plane = ("dp", "ctx")
    rows, own = query_weight.shape
    taps, few = shift_kernel.shape
    heads, width = state_decay.shape
    hidden = up_weight.shape[1]
    lanes = 4 * own
    small = jnp.concatenate(
        [mixer_gain, feed_gain, shift_kernel.reshape(-1), state_decay.reshape(-1)]
    )
    small = jnp.pad(small, (0, lanes - small.shape[0]))[None]
    first = jnp.concatenate(
        [
            jnp.concatenate([query_weight, key_weight, value_weight, mixer_weight.T], axis=1),
            jnp.pad(small, ((0, 7), (0, 0))),
        ],
        axis=0,
    )
    second = jnp.concatenate([up_weight, down_weight.T], axis=1)
    count = lax.axis_size("tensor")
    me = lax.axis_index("tensor")

    def everywhere(block):
        out = lax.all_gather(block, ("tensor",) + plane, axis=0)
        out = out.reshape((count, -1) + block.shape)
        return jnp.stack(
            [lax.dynamic_index_in_dim(out, me ^ i, 0, keepdims=False) for i in range(count)]
        )

    first, second = everywhere(first), everywhere(second)
    blocks = first.shape[1]
    model = blocks * rows
    matrices = first[:, :, :rows].reshape(count, model, 4, own)
    matrices = jnp.transpose(matrices, (2, 1, 0, 3)).reshape(4, model, count * own)
    joint = jnp.concatenate([matrices[0], matrices[1], matrices[2]], axis=1)
    small = first[:, :, rows]
    gains = small[0, :, : 2 * rows].reshape(blocks, 2, rows).transpose(1, 0, 2).reshape(2, 1, model)
    shift = small[:, :, 2 * rows : 2 * rows + taps * few].reshape(count, blocks, taps, few)
    shift = shift.transpose(2, 0, 1, 3).reshape(taps, count * blocks * few)
    begin = 2 * rows + taps * few
    decay = small[:, 0, begin : begin + heads * width].reshape(count * heads, width)
    feed = second.reshape(count, model, 2, hidden).transpose(2, 1, 0, 3).reshape(2, model, count * hidden)
    return gains[0], gains[1], joint, matrices[3], shift, decay, feed[0], feed[1]


def mixer_tables(decay, size):
    heads, width = decay.shape
    log_decay = jnp.log(decay)
    flat = log_decay.reshape(1, heads * width)
    position = jnp.arange(size, dtype=jnp.float32)[:, None]
    column = jnp.repeat(log_decay.T, width, axis=1)
    span = GROUP * width
    which = jnp.arange(span) // width
    mask = (which[:, None] == which[None, :]).astype(jnp.float32)
    return {
        "grow": jnp.exp(position * flat),
        "shrink": jnp.exp(-position * flat),
        "dec": jnp.exp(column),
        "end": jnp.exp((size - 1.0) * column),
        "all": jnp.exp(size * column),
        "mask": mask.astype(jnp.bfloat16),
        "maskf": mask,
    }


def positions(segments, size, taps):
    length = segments.shape[0]
    seg = segments.astype(jnp.float32)
    grouped = seg.reshape(-1, size)
    before = jnp.concatenate([jnp.full((1,), -1.0, jnp.float32), grouped[:-1, -1]])
    columns = [seg, (grouped == before[:, None]).reshape(-1), (grouped == grouped[:, -1:]).reshape(-1)]
    for j in range(1, taps):
        columns.append(jnp.concatenate([jnp.zeros((j,), bool), seg[j:] == seg[:-j]]))
    columns = [c.astype(jnp.float32) for c in columns]
    while len(columns) < 8:
        columns.append(jnp.zeros((length,), jnp.float32))
    return jnp.stack(columns, axis=1), jnp.tile(grouped, (1, GROUP))[:, None]


def swap_in(block):
    me = lax.axis_index("ctx")
    rows, half = block.shape[:2]
    mine = lax.dynamic_index_in_dim(block, me, 0, keepdims=False)
    theirs = lax.dynamic_index_in_dim(block, 1 - me, 0, keepdims=False)
    came = lax.ppermute(theirs, "ctx", [(0, 1), (1, 0)])
    first = jnp.where(me == 0, mine, came)
    second = jnp.where(me == 0, came, mine)
    return jnp.concatenate([first, second], axis=0)


def swap_out(row):
    me = lax.axis_index("ctx")
    half = row.shape[0] // 2
    mine = lax.dynamic_slice_in_dim(row, me * half, half, 0)
    theirs = lax.dynamic_slice_in_dim(row, (1 - me) * half, half, 0)
    came = lax.ppermute(theirs, "ctx", [(0, 1), (1, 0)])
    first = jnp.where(me == 0, mine, came)
    second = jnp.where(me == 0, came, mine)
    return jnp.stack([first, second])


def by_sequence(
    layer_input, segment_ids, mixer_gain, query_weight, key_weight, value_weight, shift_kernel,
    state_decay, mixer_weight, feed_gain, up_weight, down_weight, cotangent,
):
    plane = ("dp", "ctx")
    own = query_weight.shape[1]
    hidden = up_weight.shape[1]
    taps = shift_kernel.shape[0]
    mg, fg, joint, mixer_t, kern, decay, up, down_t = gather_weights(
        mixer_gain, query_weight, key_weight, value_weight, shift_kernel, state_decay,
        mixer_weight, feed_gain, up_weight, down_weight,
    )
    x = swap_in(layer_input)
    ct = swap_in(cotangent)
    seg = swap_in(segment_ids)
    tables = mixer_tables(decay, SUBBLOCK)
    meta, segrow = positions(seg, SUBBLOCK, taps)
    proj = run_project(x, mg, joint)
    mixed, states = run_mixer(proj, meta, segrow, kern, tables)
    resid, n = run_branch(x, mixed, mixer_t, fg)
    out, fng, down_g, up_g = run_feed(n, ct, resid, up, down_t, hidden)
    rg, du, feed_gain_g, mixer_g = run_resid_back(fng, resid, ct, fg, mixer_t, mixed[:, :own], own)
    dq, dk, dv, kern_g = run_mixer_back(proj, du, states, meta, segrow, kern, tables)
    ig, mixer_gain_g, joint_g = run_input_back(x, rg, mg, joint, dq, dk, dv, own)

    def scatter(value, dim):
        return lax.psum_scatter(value, plane, scatter_dimension=dim, tiled=True)

    joint_g = scatter(joint_g, 0)
    return (
        swap_out(out),
        swap_out(ig),
        scatter(mixer_gain_g[0], 0),
        joint_g[:, :own],
        joint_g[:, own : 2 * own],
        joint_g[:, 2 * own :],
        scatter(kern_g[:, :own], 1),
        scatter(mixer_g, 0).T,
        scatter(feed_gain_g[0], 0),
        scatter(up_g, 0),
        scatter(down_g, 0).T,
    )


def solution(mesh):
    shape = mesh.shape

    def chosen(*arrays):
        rows, length, model = arrays[0].shape
        heads, width = arrays[7].shape
        fits = (
            (shape["dp"], shape["ctx"], shape["tensor"]) == (4, 2, 4)
            and rows == 2
            and (heads * shape["tensor"]) % GROUP == 0
            and width == SUBBLOCK
        )
        return (by_sequence if fits else on_device)(*arrays)

    return jax.shard_map(
        chosen,
        mesh=mesh,
        in_specs=(
            P("dp", "ctx", None),
            P("dp", "ctx"),
            P(("dp", "ctx")),
            P(("dp", "ctx"), "tensor"),
            P(("dp", "ctx"), "tensor"),
            P(("dp", "ctx"), "tensor"),
            P(None, ("tensor", "dp", "ctx")),
            P("tensor", None),
            P("tensor", ("dp", "ctx")),
            P(("dp", "ctx")),
            P(("dp", "ctx"), "tensor"),
            P("tensor", ("dp", "ctx")),
            P("dp", "ctx", None),
        ),
        out_specs=(
            P("dp", "ctx", None),
            P("dp", "ctx", None),
            P(("dp", "ctx")),
            P(("dp", "ctx"), "tensor"),
            P(("dp", "ctx"), "tensor"),
            P(("dp", "ctx"), "tensor"),
            P(None, ("tensor", "dp", "ctx")),
            P("tensor", ("dp", "ctx")),
            P(("dp", "ctx")),
            P(("dp", "ctx"), "tensor"),
            P("tensor", ("dp", "ctx")),
        ),
        check_vma=False,
    )
```

```python
from functools import partial

import jax
import jax.numpy as jnp
from jax import lax
from jax.experimental import pallas as pl
from jax.experimental.pallas import tpu as pltpu
from jax.sharding import PartitionSpec as P

SUBBLOCK = 64


eps = 1e-05
precise = lax.Precision.HIGHEST


def passed_along(value, axis, steps):
    count = lax.axis_size(axis)
    leading, last = (max(0, -steps), min(count, count - steps))
    return lax.ppermute(value, axis, [(source, source + steps) for source in range(leading, last)])


def carried_in(value, axis, join, neutral, backward):
    count, mine = (lax.axis_size(axis), lax.axis_index(axis))
    pieces = jax.tree.map(lambda part: lax.all_gather(part, axis), value)
    if backward:
        pieces = jax.tree.map(lambda part: part[::-1], pieces)
        mine = count - 1 - mine
    subtotal = jax.tree.map(
        lambda part, zero: jnp.full_like(part, 0) + jnp.asarray(zero, part.dtype), value, neutral
    )

    def step(position, subtotal):
        longer = join(subtotal, jax.tree.map(lambda part: part[position], pieces))
        return jax.tree.map(lambda new, old: jnp.where(position < mine, new, old), longer, subtotal)

    return lax.fori_loop(0, count - 1, step, subtotal)


def normalize(inputs, gain):
    centered = inputs - jnp.mean(inputs, axis=-1, keepdims=True)
    scaled = centered * lax.rsqrt(jnp.mean(centered * centered, axis=-1, keepdims=True) + eps)
    return scaled * gain


def project(left, right):
    return jnp.einsum(
        "btd,df->btf", left, right, precision=precise, preferred_element_type=jnp.float32
    )


def outer_sum(left, right):
    return jnp.einsum(
        "btd,btf->df", left, right, precision=precise, preferred_element_type=jnp.float32
    )


def smooth_gate(inputs):
    return jax.nn.gelu(inputs, approximate=True)


def shift_keys(extended, kernel, seg_ext):
    taps = kernel.shape[0]
    length = extended.shape[1] - taps + 1
    current = seg_ext[:, taps - 1 :]
    summed = jnp.zeros((extended.shape[0], length, extended.shape[2]), jnp.float32)
    for offset in range(taps):
        begin = taps - 1 - offset
        joined = (seg_ext[:, begin : begin + length] == current).astype(jnp.float32)
        summed = summed + kernel[offset] * extended[:, begin : begin + length] * joined[:, :, None]
    return summed


def compose(earlier, later):
    return (earlier[0] * later[0], later[0][..., None] * earlier[1] + later[1])


def geometry(segments, before_block, log_decay):
    rows, length = segments.shape
    pieces = length // SUBBLOCK
    grouped = segments.reshape(rows, pieces, SUBBLOCK)
    before = jnp.concatenate([before_block[:, None], grouped[:, :-1, -1]], axis=1)
    living = (grouped == before[:, :, None]).astype(jnp.float32)
    retained = (grouped == grouped[:, :, -1:]).astype(jnp.float32)
    position = jnp.arange(SUBBLOCK, dtype=jnp.float32)
    causal = position[:, None] >= position[None, :]
    allowed = jnp.logical_and(grouped[:, :, :, None] == grouped[:, :, None, :], causal).astype(
        jnp.float32
    )
    growing = jnp.exp(position[:, None, None] * log_decay)
    shrinking = jnp.exp(-position[:, None, None] * log_decay)
    step_in = growing * jnp.exp(log_decay)
    closing = jnp.exp((SUBBLOCK - 1.0 - position)[:, None, None] * log_decay)
    whole_decay = jnp.exp(SUBBLOCK * log_decay)[None, None] * living[:, :, -1][:, :, None, None]
    running = jnp.ones((rows,) + log_decay.shape, jnp.float32)
    carried = []
    for index in range(pieces):
        carried.append(running)
        running = running * whole_decay[:, index]
    return (
        living,
        retained,
        allowed,
        growing,
        shrinking,
        step_in,
        closing,
        whole_decay,
        jnp.stack(carried, axis=1),
        running,
    )


def local_part(queries, shifted, values, shape_info):
    (
        living,
        retained,
        allowed,
        growing,
        shrinking,
        step_in,
        closing,
        whole_decay,
        carried,
        block_decay,
    ) = shape_info
    scores = jnp.einsum(
        "bncgi,bnsgi->bngcs", queries * growing, shifted * shrinking, precision=precise
    )
    scores = scores * allowed[:, :, None]
    within = jnp.einsum("bngcs,bnsgj->bncgj", scores, values, precision=precise)
    update = jnp.einsum(
        "bncgi,bncgj->bngij",
        shifted * closing * retained[..., None, None],
        values,
        precision=precise,
    )
    running = jnp.zeros_like(update[:, 0])
    starts = []
    for index in range(update.shape[1]):
        starts.append(running)
        running = whole_decay[:, index][..., None] * running + update[:, index]
    return (within, jnp.stack(starts, axis=1), running)


def across(queries, starts, state_in, shape_info):
    (
        living,
        retained,
        allowed,
        growing,
        shrinking,
        step_in,
        closing,
        whole_decay,
        carried,
        block_decay,
    ) = shape_info
    entries = starts + carried[..., None] * state_in[:, None]
    weighted = queries * step_in * living[..., None, None]
    return jnp.einsum("bncgi,bngij->bncgj", weighted, entries, precision=precise)


def on_device(
    layer_input,
    segment_ids,
    mixer_gain,
    query_weight,
    key_weight,
    value_weight,
    shift_kernel,
    state_decay,
    mixer_weight,
    feed_gain,
    up_weight,
    down_weight,
    cotangent,
):
    (
        mixer_gain_all,
        query_all,
        key_all,
        value_all,
        kernel_all,
        mixer_all,
        feed_gain_all,
        up_all,
        down_all,
    ) = (
        lax.all_gather(mixer_gain, ("dp", "ctx"), axis=0, tiled=True),
        lax.all_gather(query_weight, ("dp", "ctx"), axis=0, tiled=True),
        lax.all_gather(key_weight, ("dp", "ctx"), axis=0, tiled=True),
        lax.all_gather(value_weight, ("dp", "ctx"), axis=0, tiled=True),
        lax.all_gather(shift_kernel, ("dp", "ctx"), axis=1, tiled=True),
        lax.all_gather(mixer_weight, ("dp", "ctx"), axis=1, tiled=True),
        lax.all_gather(feed_gain, ("dp", "ctx"), axis=0, tiled=True),
        lax.all_gather(up_weight, ("dp", "ctx"), axis=0, tiled=True),
        lax.all_gather(down_weight, ("dp", "ctx"), axis=1, tiled=True),
    )
    heads, width = state_decay.shape
    log_decay = jnp.log(state_decay)
    taps = kernel_all.shape[0]
    rows, length, model = layer_input.shape
    pieces = length // SUBBLOCK
    features = heads * width
    seg_float = segment_ids.astype(jnp.float32)
    joint_weight = jnp.concatenate([query_all, key_all, value_all], axis=1)
    normed = normalize(layer_input, mixer_gain_all)
    projected = project(normed, joint_weight)
    queries = projected[:, :, :features]
    keys_raw = projected[:, :, features : 2 * features]
    values = projected[:, :, 2 * features :]
    tail_keys, tail_segs = passed_along(
        (keys_raw[:, length - taps + 1 :], seg_float[:, length - taps + 1 :]), "ctx", 1
    )
    extended = jnp.concatenate([tail_keys, keys_raw], axis=1)
    seg_ext = jnp.concatenate([tail_segs, seg_float], axis=1)
    shift_fixed = partial(shift_keys, seg_ext=seg_ext)
    shifted = shift_fixed(extended, kernel_all)
    info = geometry(seg_float, tail_segs[:, -1], log_decay)
    block_decay = info[-1]
    head_q = queries.reshape(rows, pieces, SUBBLOCK, heads, width)
    head_k = shifted.reshape(rows, pieces, SUBBLOCK, heads, width)
    head_v = values.reshape(rows, pieces, SUBBLOCK, heads, width)
    within, starts, local_end = local_part(head_q, head_k, head_v, info)
    identity = (jnp.ones_like(block_decay), jnp.zeros_like(local_end))
    state_in = carried_in((block_decay, local_end), "ctx", compose, identity, False)[1]
    mixed = (within + across(head_q, starts, state_in, info)).reshape(rows, length, features)
    branch = lax.psum(project(mixed, mixer_all), "tensor")
    resid = layer_input + branch
    normed_feed = normalize(resid, feed_gain_all)
    pre_act = project(normed_feed, up_all)
    activated, gelu_back = jax.vjp(smooth_gate, pre_act)
    feed = lax.psum(project(activated, down_all), "tensor")
    layer_output = resid + feed
    act_grad = project(cotangent, down_all.T)
    down_grad = outer_sum(activated, cotangent)
    (pre_grad,) = gelu_back(act_grad)
    up_grad = outer_sum(normed_feed, pre_grad)
    feed_normed_grad = lax.psum(project(pre_grad, up_all.T), "tensor")
    _, feed_norm_back = jax.vjp(normalize, resid, feed_gain_all)
    resid_ln_grad, feed_gain_grad = feed_norm_back(feed_normed_grad)
    resid_grad = cotangent + resid_ln_grad
    mixed_grad = project(resid_grad, mixer_all.T)
    mixer_weight_grad = outer_sum(mixed, resid_grad)
    head_du = mixed_grad.reshape(rows, pieces, SUBBLOCK, heads, width)
    (
        living,
        retained,
        allowed,
        growing,
        shrinking,
        step_in,
        closing,
        whole_decay,
        carried,
        block_decay,
    ) = info
    own_grad = jnp.einsum(
        "bncgi,bncgj,bngi->bgij",
        head_q * step_in * living[..., None, None],
        head_du,
        carried,
        precision=precise,
    )
    identity_grad = (jnp.ones_like(block_decay), jnp.zeros_like(own_grad))
    after = carried_in((block_decay, own_grad), "ctx", compose, identity_grad, True)[1]

    def mixer_full(query_in, key_in, value_in, entering):
        inner, begins, ending = local_part(query_in, key_in, value_in, info)
        output = inner + across(query_in, begins, entering, info)
        return (output, ending + block_decay[..., None] * entering)

    _, mixer_vjp = jax.vjp(mixer_full, head_q, head_k, head_v, state_in)
    query_act_grad, shifted_grad, value_act_grad, _ = mixer_vjp((head_du, after))
    _, shift_back = jax.vjp(shift_fixed, extended, kernel_all)
    ext_grad, kernel_grad = shift_back(shifted_grad.reshape(rows, length, features))
    returned = passed_along(ext_grad[:, : taps - 1], "ctx", -1)
    key_act_grad = ext_grad[:, taps - 1 :] + jnp.pad(
        returned, ((0, 0), (length - taps + 1, 0), (0, 0))
    )
    joint_grad = jnp.concatenate(
        [
            query_act_grad.reshape(rows, length, features),
            key_act_grad,
            value_act_grad.reshape(rows, length, features),
        ],
        axis=2,
    )
    joint_weight_grad = outer_sum(normed, joint_grad)
    normed_grad = lax.psum(project(joint_grad, joint_weight.T), "tensor")
    _, mixer_norm_back = jax.vjp(normalize, layer_input, mixer_gain_all)
    input_ln_grad, mixer_gain_grad = mixer_norm_back(normed_grad)
    input_grad = resid_grad + input_ln_grad
    query_grad = joint_weight_grad[:, :features]
    key_grad = joint_weight_grad[:, features : 2 * features]
    value_grad = joint_weight_grad[:, 2 * features :]
    all_parts = tuple(
        (
            lax.psum_scatter(mixer_gain_grad, ("dp", "ctx"), scatter_dimension=0, tiled=True),
            lax.psum_scatter(query_grad, ("dp", "ctx"), scatter_dimension=0, tiled=True),
            lax.psum_scatter(key_grad, ("dp", "ctx"), scatter_dimension=0, tiled=True),
            lax.psum_scatter(value_grad, ("dp", "ctx"), scatter_dimension=0, tiled=True),
            lax.psum_scatter(kernel_grad, ("dp", "ctx"), scatter_dimension=1, tiled=True),
            lax.psum_scatter(mixer_weight_grad, ("dp", "ctx"), scatter_dimension=1, tiled=True),
            lax.psum_scatter(feed_gain_grad, ("dp", "ctx"), scatter_dimension=0, tiled=True),
            lax.psum_scatter(up_grad, ("dp", "ctx"), scatter_dimension=0, tiled=True),
            lax.psum_scatter(down_grad, ("dp", "ctx"), scatter_dimension=1, tiled=True),
        )
    )
    return (layer_output, input_grad) + all_parts


PAIR = 2
BLOCK = 128
LANES = 128
LIMIT = 60
TILE = 256
C_GELU = 0.7978845608028654
NN = ((1,), (0,))
NT = ((1,), (1,))
TN = ((0,), (0,))
f32, bf16 = jnp.float32, jnp.bfloat16


def params(limit=LIMIT):
    return pltpu.CompilerParams(vmem_limit_bytes=limit * 2**20)


def cost(flops, moved):
    return pl.CostEstimate(flops=int(flops), bytes_accessed=int(moved), transcendentals=0)


def shaped(shape, dtype=jnp.float32):
    return jax.ShapeDtypeStruct(shape, dtype)


def split(a):
    high = a.astype(bf16)
    return high, (a - high.astype(f32)).astype(bf16)


def d3(left, right, dims):
    dot = partial(lax.dot_general, dimension_numbers=(dims, ((), ())), preferred_element_type=f32)
    return dot(left[0], right[0]) + dot(left[1], right[0]) + dot(left[0], right[1])


def d3_low(left, right, dims):
    dot = partial(lax.dot_general, dimension_numbers=(dims, ((), ())), preferred_element_type=f32)
    rows = left[0].shape[0]
    both = dot(jnp.concatenate(left, axis=0), right[0])
    return both[:rows] + both[rows:] + dot(left[0], right[1])


def tied(arrays):
    specs = [
        pl.BlockSpec((1,) * (a.ndim - 2) + (8, 128), lambda *_, n=a.ndim: (0,) * n) for a in arrays
    ]
    return specs, list(arrays)


def norm_parts(v):
    centered = v - jnp.mean(v, axis=-1, keepdims=True)
    r = lax.rsqrt(jnp.mean(centered * centered, axis=-1, keepdims=True) + eps)
    return centered * r, r


def whole(shape):
    return pl.BlockSpec(
        shape, lambda *_: (0,) * len(shape), pipeline_mode=pl.Buffered(buffer_count=1)
    )


def scalar():
    return pl.BlockSpec(memory_space=pltpu.SMEM)


def pack_mixer_kernel(me_ref, q_ref, k_ref, v_ref, m_ref, mg_ref, fg_ref, kern_ref, decay_ref, o_ref):
    rows, own = q_ref.shape
    taps, few = kern_ref.shape
    heads, width = decay_ref.shape
    o_ref[0:rows, 0:own] = q_ref[...]
    o_ref[0:rows, own : 2 * own] = k_ref[...]
    o_ref[0:rows, 2 * own : 3 * own] = v_ref[...]
    o_ref[0:rows, 3 * own :] = jnp.transpose(m_ref[...])
    o_ref[rows:, :] = jnp.zeros((8, o_ref.shape[1]), f32)
    for b in range(8):

        @pl.when(me_ref[0] == b)
        def _():
            o_ref[rows : rows + 1, b * rows : (b + 1) * rows] = mg_ref[...]
            o_ref[rows + 1 : rows + 2, b * rows : (b + 1) * rows] = fg_ref[...]
            o_ref[rows + 2 : rows + 2 + taps, b * few : (b + 1) * few] = kern_ref[...]

    @pl.when(me_ref[0] == 0)
    def _():
        for h in range(heads):
            at = rows + 2 + taps
            o_ref[at : at + 1, h * width : (h + 1) * width] = decay_ref[h : h + 1, :]


def run_pack_mixer(me, q, k, v, m, mg, fg, kern, decay):
    rows, own = q.shape
    args = (q, k, v, m, mg[None], fg[None], kern, decay)
    return pl.pallas_call(
        pack_mixer_kernel,
        grid=(1,),
        in_specs=[scalar()] + [whole(a.shape) for a in args],
        out_specs=whole((rows + 8, 4 * own)),
        out_shape=shaped((rows + 8, 4 * own)),
        compiler_params=params(),
        cost_estimate=cost(1e6, 2**20),
        name="pack_mixer",
    )(me, *args)


def pack_feed_kernel(up_ref, down_ref, o_ref):
    hidden = up_ref.shape[1]
    o_ref[:, :hidden] = up_ref[...]
    o_ref[:, hidden:] = jnp.transpose(down_ref[...])


def run_pack_feed(up, down):
    return pl.pallas_call(
        pack_feed_kernel,
        grid=(1,),
        in_specs=[whole(up.shape), whole(down.shape)],
        out_specs=whole((up.shape[0], 2 * up.shape[1])),
        out_shape=shaped((up.shape[0], 2 * up.shape[1])),
        compiler_params=params(),
        cost_estimate=cost(1e6, 2 * 2**20),
        name="pack_feed",
    )(up, down)


def sequence_specs(model, order):
    def mine(i, m):
        return (m[0] & 1, order(i, m) % 2, 0)

    def came(i, m):
        return (order(i, m) % 2, 0)

    return [pl.BlockSpec((1, TILE, model), mine), pl.BlockSpec((TILE, model), came)]


def sequence_tile(tile, me_ref, mine_ref, came_ref):
    own = tile // 2 == (me_ref[0] & 1)
    return jnp.where(own, mine_ref[0], came_ref[...])


def project_kernel(me_ref, x_ref, xr_ref, *refs):
    first, second = refs[0:8], refs[8:16]
    o_ref, wh_ref, wl_ref, mh_ref, ml_ref, gains_ref, small_ref = refs[-7:]
    own = first[0].shape[1] // 4
    rows = wh_ref.shape[0] // 8

    @pl.when(pl.program_id(0) == 0)
    def _():
        for r in range(8):
            at = pl.ds(pl.multiple_of((me_ref[0] ^ r) * rows, rows), rows)
            a, b = first[r][0:rows, :], second[r][0:rows, :]
            for i in range(4):
                both = jnp.concatenate(
                    [a[:, i * own : (i + 1) * own], b[:, i * own : (i + 1) * own]], axis=1
                )
                high, low = split(both)
                if i < 3:
                    wh_ref[at, i * 2 * own : (i + 1) * 2 * own] = high
                    wl_ref[at, i * 2 * own : (i + 1) * 2 * own] = low
                else:
                    mh_ref[at, :] = high
                    ml_ref[at, :] = low
        sums = []
        for pieces in (first, second):
            total = pieces[0][rows:, :]
            for r in range(1, 8):
                total = total + pieces[r][rows:, :]
            sums.append(total)
        gains_ref[...] = sums[0]
        small_ref[...] = jnp.concatenate([s[:, :own] for s in sums], axis=1)

    x = sequence_tile(pl.program_id(0), me_ref, x_ref, xr_ref)
    n = split(norm_parts(x)[0] * gains_ref[0:1, :])
    o_ref[...] = d3(n, (wh_ref[...], wl_ref[...]), NN)


def run_project(me, x, first, second, ties=()):
    rows, half, model = x[0].shape
    tokens = rows * half
    own = first[0].shape[1] // 4
    wide = 6 * own
    piece = whole(first[0].shape)
    weights = [(model, wide)] * 2 + [(model, 2 * own)] * 2
    few = [(8, model), (8, 2 * own)]
    tie_specs, tie_args = tied(ties)
    return pl.pallas_call(
        project_kernel,
        grid_spec=pltpu.PrefetchScalarGridSpec(
            num_scalar_prefetch=1,
            grid=(tokens // TILE,),
            in_specs=sequence_specs(model, lambda i, m: i) + [piece] * 16 + tie_specs,
            out_specs=[pl.BlockSpec((TILE, wide), lambda i, m: (i, 0))]
            + [whole(s) for s in weights + few],
        ),
        out_shape=[shaped((tokens, wide))]
        + [shaped(s, bf16) for s in weights]
        + [shaped(s) for s in few],
        compiler_params=params(),
        cost_estimate=cost(6 * tokens * model * wide, 20 * 2**20),
        name="project",
    )(me, *x, *first, *second, *tie_args)


def spread(parts, masks):
    return tuple(jnp.concatenate([p * m for m in masks], axis=0) for p in parts)


def lane_masks(lanes):
    which = lax.broadcasted_iota(jnp.int32, (1, lanes), 1) // (lanes // PAIR)
    return [jnp.where(which == h, 1.0, 0.0).astype(bf16) for h in range(PAIR)]


def square_mask(lanes):
    a = lax.broadcasted_iota(jnp.int32, (lanes, lanes), 0) // (lanes // PAIR)
    b = lax.broadcasted_iota(jnp.int32, (lanes, lanes), 1) // (lanes // PAIR)
    return jnp.where(a == b, 1.0, 0.0)


def fill_tables(decay, grow, shrink, dec, end, full):
    size, model = grow.shape
    lanes = dec.shape[0]
    rates = jnp.log(decay)
    position = lax.broadcasted_iota(jnp.int32, (size, model), 0).astype(f32)
    grow[...] = jnp.exp(position * rates)
    shrink[...] = jnp.exp(-position * rates)
    for p in range(model // lanes):
        s = slice(p * lanes, (p + 1) * lanes)
        column = jnp.transpose(jnp.broadcast_to(rates[:, s], (lanes, lanes)))
        dec[:, s] = jnp.exp(column)
        end[:, s] = jnp.exp((size - 1.0) * column)
        full[:, s] = jnp.exp(float(size) * column)


def joined(extended, size, taps):
    now = extended[8:]
    return [jnp.where(extended[8 - j : 8 - j + size] == now, 1.0, 0.0) for j in range(1, taps)]


def shift_forward(keys, before, kern, same, taps):
    extended = jnp.concatenate([before, keys], axis=0)
    size = keys.shape[0]
    moved = [keys]
    for j in range(1, taps):
        moved.append(extended[8 - j : 8 - j + size] * same[j - 1])
    total = kern[0:1, :] * keys
    for j in range(1, taps):
        total = total + kern[j : j + 1, :] * moved[j]
    return total, moved


def allowed_masks(seg, row):
    size, wide = seg.shape[0], row.shape[1]
    rows = lax.broadcasted_iota(jnp.int32, (size, wide), 0)
    cols = lax.broadcasted_iota(jnp.int32, (size, wide), 1) % size
    same = seg == row
    return (
        jnp.where(jnp.logical_and(rows >= cols, same), 1.0, 0.0),
        jnp.where(jnp.logical_and(rows <= cols, same), 1.0, 0.0),
    )


def pair(a_ref, b_ref):
    return jnp.concatenate([a_ref[...], b_ref[...]], axis=1)


def third_of(refs, rows, i):
    wide = refs[0].shape[1] // 3
    return jnp.concatenate([r[rows, i * wide : (i + 1) * wide] for r in refs], axis=1)


def mixer_kernel(
    taps, me_ref, x_ref, xr_ref, pa_ref, pb_ref, seg_ref, segrow_ref, sa_ref, sb_ref, gains_ref,
    ah_ref, al_ref, bh_ref, bl_ref, own_ref, state_out_ref, resid_ref, nh_ref, nl_ref,
    state, tail, segtail, grow, shrink, dec, end, full, mixed,
):
    size, lanes = grow.shape[0], dec.shape[0]
    projs = (pa_ref, pb_ref)

    @pl.when(pl.program_id(0) == 0)
    def _():
        state[...] = jnp.zeros_like(state)
        tail[...] = jnp.zeros_like(tail)
        segtail[...] = jnp.full_like(segtail, -1.0)
        fill_tables(pair(sa_ref, sb_ref)[2 + taps : 3 + taps], grow, shrink, dec, end, full)

    kern = pair(sa_ref, sb_ref)[2 : 2 + taps]
    masks = lane_masks(lanes)
    square = square_mask(lanes)
    model = state.shape[1]
    groups = [slice(g * lanes, (g + 1) * lanes) for g in range(model // lanes)]
    before_keys, before = tail[...], segtail[...]
    for chunk in range(xr_ref.shape[0] // size):
        here = slice(chunk * size, (chunk + 1) * size)
        seg = seg_ref[here, :]
        extended = jnp.concatenate([before, seg], axis=0)
        living = jnp.where(seg == before[7:8], 1.0, 0.0)
        kept = jnp.where(seg == seg[size - 1 :], 1.0, 0.0)
        goes_on = living[size - 1 :]
        q_all, keys, v_all = (third_of(projs, here, i) for i in range(3))
        shifted, _ = shift_forward(keys, before_keys, kern, joined(extended, size, taps), taps)
        before_keys, before = keys[size - 8 :, :], seg[size - 8 :]
        allowed, _ = allowed_masks(seg, segrow_ref[chunk])
        state_out_ref[chunk] = state[...]
        qg, kf, v, scores = [], [], [], []
        for s in groups:
            qg.append(split(q_all[:, s] * grow[:, s]))
            kf.append(shifted[:, s] * shrink[:, s])
            v.append(split(v_all[:, s]))
            scores.append(d3_low(qg[-1], spread(split(kf[-1]), masks), NT))
        updates = [d3(split(k * kept), w, TN) * square for k, w in zip(kf, v)]
        weights = [split(score * allowed) for score in scores]
        for g, s in enumerate(groups):
            part = d3_low(weights[g], spread(v[g], masks), NN)
            mixed[here, s] = part + living * d3_low(qg[g], split(state[:, s] * dec[:, s]), NN)
        for g, s in enumerate(groups):
            state[:, s] = state[:, s] * (full[:, s] * goes_on) + end[:, s] * updates[g]
    tail[...] = before_keys
    segtail[...] = before
    own_ref[...] = mixed[:, : own_ref.shape[1]]
    third = ah_ref.shape[1]
    resid = (
        sequence_tile(pl.program_id(0), me_ref, x_ref, xr_ref)
        + d3(split(mixed[:, :third]), (ah_ref[...], al_ref[...]), NT)
        + d3(split(mixed[:, third:]), (bh_ref[...], bl_ref[...]), NT)
    )
    resid_ref[...] = resid
    nh_ref[...], nl_ref[...] = split(norm_parts(resid)[0] * gains_ref[1:2, :])


def mixer_scratch(model):
    return [pltpu.VMEM((BLOCK, model), f32)] * 2 + [pltpu.VMEM((LANES, model), f32)] * 3


def run_mixer(me, x, projs, seg, segrow, smalls, gains, a, b, taps):
    tokens, model = projs[0].shape[0], x[0].shape[2]
    act = (tokens, model)
    chunks = TILE // BLOCK
    row = pl.BlockSpec((TILE, model), lambda c, m: (c, 0))
    proj = pl.BlockSpec((TILE, projs[0].shape[1]), lambda c, m: (c, 0))
    states = (tokens // BLOCK, LANES, model)
    return pl.pallas_call(
        partial(mixer_kernel, taps),
        grid_spec=pltpu.PrefetchScalarGridSpec(
        num_scalar_prefetch=1,
        grid=(tokens // TILE,),
        in_specs=sequence_specs(model, lambda i, m: i) + [
            proj, proj,
            pl.BlockSpec((TILE, 1), lambda c, m: (c, 0)),
            pl.BlockSpec((chunks, 1, segrow.shape[2]), lambda c, m: (c, 0, 0)),
            whole(smalls[0].shape), whole(smalls[1].shape), whole(gains.shape),
        ]
        + [whole(a[0].shape)] * 4,
        out_specs=[
            pl.BlockSpec((TILE, 256), lambda c, m: (c, 0)),
            pl.BlockSpec((chunks, LANES, model), lambda c, m: (c, 0, 0)),
            row, row, row,
        ],
        scratch_shapes=[
            pltpu.VMEM((LANES, model), f32), pltpu.VMEM((8, model), f32), pltpu.VMEM((8, 1), f32)
        ]
        + mixer_scratch(model)
        + [pltpu.VMEM((TILE, model), f32)],
        ),
        out_shape=[
            shaped((tokens, 256)), shaped(states), shaped(act),
            shaped(act, bf16), shaped(act, bf16),
        ],
        compiler_params=params(),
        cost_estimate=cost(3e10, 30 * 2**20),
        name="mixer",
    )(me, *x, *projs, seg, segrow, *smalls, gains, *a, *b)


def mixer_back_kernel(
    taps, me_ref, fng_ref, resid_ref, x_ref, xr_ref, ct_ref, cr_ref, pa_ref, pb_ref, ba_ref, bb_ref, state_ref,
    mixed_ref, seg_ref, segb_ref, segrow_ref, sa_ref, sb_ref, gains_ref,
    ah_ref, al_ref, bh_ref, bl_ref, *refs,
):
    (
        rg_ref, dq_ref, dk_ref, dv_ref, gg_ref, dkern_ref, keep_ref, send_ref,
        grad, head, grow, shrink, dec, end, full, du_all, wg,
    ) = refs[-17:]
    size, lanes = grow.shape[0], dec.shape[0]
    step, steps = pl.program_id(0), pl.num_programs(0)
    projs = (pa_ref, pb_ref)

    @pl.when(step == 0)
    def _():
        grad[...] = jnp.zeros_like(grad)
        head[...] = jnp.zeros_like(head)
        dkern_ref[...] = jnp.zeros_like(dkern_ref)
        gg_ref[...] = jnp.zeros_like(gg_ref)
        wg[...] = jnp.zeros_like(wg)
        fill_tables(pair(sa_ref, sb_ref)[2 + taps : 3 + taps], grow, shrink, dec, end, full)

    third = ah_ref.shape[1]
    back, gain_grad, _ = norm_back(resid_ref[...], gains_ref[1:2, :], fng_ref[...])
    tile = steps - 1 - step
    rg = sequence_tile(tile, me_ref, ct_ref, cr_ref) + back
    rg_ref[...] = rg
    gg_ref[...] += gain_grad
    r2 = split(rg)
    du_all[:, :third] = d3(r2, (ah_ref[...], al_ref[...]), NN)
    du_all[:, third:] = d3(r2, (bh_ref[...], bl_ref[...]), NN)

    kern = pair(sa_ref, sb_ref)[2 : 2 + taps]
    masks = lane_masks(lanes)
    square = square_mask(lanes)
    model = grad.shape[1]
    groups = [slice(g * lanes, (g + 1) * lanes) for g in range(model // lanes)]
    count = len(groups)
    chunks = rg.shape[0] // size
    for chunk in reversed(range(chunks)):
        here = slice(chunk * size, (chunk + 1) * size)
        seg = seg_ref[here, :]
        q_all, keys, v_all = (third_of(projs, here, i) for i in range(3))
        if chunk:
            just = slice(chunk * size - 8, chunk * size)
            before, before_keys = seg_ref[just, :], third_of(projs, just, 1)
        else:
            before = jnp.where(step == steps - 1, -1.0, segb_ref[...])
            before_keys = pair(ba_ref, bb_ref)
        extended = jnp.concatenate([before, seg], axis=0)
        living = jnp.where(seg == before[7:8], 1.0, 0.0)
        kept = jnp.where(seg == seg[size - 1 :], 1.0, 0.0)
        goes_on = living[size - 1 :]
        same = joined(extended, size, taps)
        shifted, moved = shift_forward(keys, before_keys, kern, same, taps)
        allowed, allowed_t = allowed_masks(seg, segrow_ref[chunk])
        qf = [q_all[:, s] * grow[:, s] for s in groups]
        qg = [split(q) for q in qf]
        kg = [split(shifted[:, s] * shrink[:, s]) for s in groups]
        v = [split(v_all[:, s]) for s in groups]
        du = [split(du_all[here, s]) for s in groups]
        p_t = [d3_low(kg[g], spread(qg[g], masks), NT) for g in range(count)]
        dp = [d3_low(du[g], spread(v[g], masks), NT) for g in range(count)]
        dp_t = [d3_low(v[g], spread(du[g], masks), NT) for g in range(count)]
        updates = [d3(split(qf[g] * living), du[g], TN) * square for g in range(count)]
        p_t = [split(p * allowed_t) for p in p_t]
        dp = [split(p * allowed) for p in dp]
        dp_t = [split(p * allowed_t) for p in dp_t]
        for g, s in enumerate(groups):
            entering = split(state_ref[chunk, :, s] * dec[:, s])
            leaving = split(grad[:, s] * end[:, s])
            dqg = d3_low(dp[g], spread(kg[g], masks), NN) + living * d3_low(du[g], entering, NT)
            dkg = d3_low(dp_t[g], spread(qg[g], masks), NN) + kept * d3_low(v[g], leaving, NT)
            dv_ref[here, s] = d3_low(p_t[g], spread(du[g], masks), NN) + kept * d3_low(
                kg[g], leaving, NN
            )
            dq_ref[here, s] = dqg * grow[:, s]
            dshift = dkg * shrink[:, s]
            grad[:, s] = grad[:, s] * (full[:, s] * goes_on) + dec[:, s] * updates[g]
            total = kern[0:1, s] * dshift
            for j in range(1, taps):
                part = dshift * same[j - 1]
                longer = jnp.concatenate([part, head[j - 1, :, s]], axis=0)
                total = total + kern[j : j + 1, s] * longer[j : j + size]
                head[j - 1, :, s] = part[0:8]
            dk_ref[here, s] = total
            if g < 2:
                for j in range(taps):
                    dkern_ref[j : j + 1, s] += jnp.sum(
                        dshift * moved[j][:, s], axis=0, keepdims=True
                    )

    own = keep_ref.shape[-1] // 4
    x = sequence_tile(tile, me_ref, x_ref, xr_ref)
    n = split(norm_parts(x)[0] * gains_ref[0:1, :])
    joint = jnp.concatenate([r[:, :own] for r in (dq_ref, dk_ref, dv_ref)], axis=1)
    wg[:, : 3 * own] += d3(n, split(joint), TN)
    wg[:, 3 * own :] += d3(r2, split(mixed_ref[:, :own]), TN)

    @pl.when(step == steps - 1)
    def _():
        store_blocks(me_ref[0], wg, keep_ref, send_ref, 0)


def run_mixer_back(
    me, fng, resid, x, ct, projs, states, mixed, seg, segrow, smalls, gains, a, b, taps, ties=()
):
    tokens, model = resid.shape
    third = projs[0].shape[1] // 3
    own = third // 2
    chunks = TILE // BLOCK
    last = tokens // TILE - 1
    blocks = (1, 4, model // 8, 4 * own)
    tie_specs, tie_args = tied(ties)

    def prior(c):
        return jnp.maximum((last - c) * (TILE // 8) - 1, 0)

    row = pl.BlockSpec((TILE, model), lambda c, m: (last - c, 0))
    proj = pl.BlockSpec((TILE, 3 * third), lambda c, m: (last - c, 0))
    before = pl.BlockSpec((8, third), lambda c, m: (prior(c), 1))
    return pl.pallas_call(
        partial(mixer_back_kernel, taps),
        grid_spec=pltpu.PrefetchScalarGridSpec(
        num_scalar_prefetch=1,
        grid=(last + 1,),
        in_specs=[row, row]
        + sequence_specs(model, lambda c, m: last - c) * 2
        + [
            proj, proj, before, before,
            pl.BlockSpec((chunks, LANES, model), lambda c, m: (last - c, 0, 0)),
            pl.BlockSpec((TILE, 256), lambda c, m: (last - c, 0)),
            pl.BlockSpec((TILE, 1), lambda c, m: (last - c, 0)),
            pl.BlockSpec((8, 1), lambda c, m: (prior(c), 0)),
            pl.BlockSpec((chunks, 1, segrow.shape[2]), lambda c, m: (last - c, 0, 0)),
            whole(smalls[0].shape), whole(smalls[1].shape), whole(gains.shape),
        ]
        + [whole(a[0].shape)] * 4
        + tie_specs,
        out_specs=[row] * 4 + [whole((1, model)), whole((taps, model)), whole(blocks), whole(blocks)],
        scratch_shapes=[
            pltpu.VMEM((LANES, model), f32), pltpu.VMEM((taps - 1, 8, model), f32)
        ]
        + mixer_scratch(model)
        + [pltpu.VMEM((TILE, model), f32), pltpu.VMEM((model, 4 * own), f32)],
        ),
        out_shape=[shaped((tokens, model))] * 4
        + [shaped((1, model)), shaped((taps, model)), shaped(blocks), shaped(blocks)],
        compiler_params=params(),
        cost_estimate=cost(8e10, 50 * 2**20),
        name="mixer_back",
    )(
        me, fng, resid, *x, *ct, *projs, *projs, states, mixed, seg, seg, segrow, *smalls, gains,
        *a, *b, *tie_args,
    )


def gelu_parts(pre, back):
    th = jnp.tanh(pre * (C_GELU + (C_GELU * 0.044715) * (pre * pre)))
    half = 0.5 + 0.5 * th
    act = pre * half
    slope = half + (1.0 - th) * act * (C_GELU + (3 * C_GELU * 0.044715) * (pre * pre))
    return act, back * slope


def store_blocks(me, g, keep_ref, send_ref, i):
    rows = g.shape[0] // 8
    for b in range(8):
        r = me ^ b
        part = g[b * rows : (b + 1) * rows]
        where = r // 2

        @pl.when((r & 1) == 0)
        def _():
            keep_ref[i, where] = part

        @pl.when((r & 1) == 1)
        def _():
            send_ref[i, where] = part


def feed_kernel(own, final, me_ref, nh_ref, nl_ref, ct_ref, cr_ref, out_in, fng_in, w_in, *refs):
    if own:
        out_ref, fng_ref, wg, w = refs[-4:]
    else:
        out_ref, fng_ref, w = refs[-3:]
    step = pl.program_id(0)
    hidden = w.shape[2] // 2

    @pl.when(step == 0)
    def _():
        w[0], w[1] = split(w_in[...].reshape(w.shape[1:]))
        if own:
            wg[...] = jnp.zeros_like(wg)

    tile = theirs_first(step, me_ref)
    n = (nh_ref[...], nl_ref[...])
    ct = split(sequence_tile(tile, me_ref, ct_ref, cr_ref))
    u, d = (w[0, :, :hidden], w[1, :, :hidden]), (w[0, :, hidden:], w[1, :, hidden:])
    act, grad = gelu_parts(d3(n, u, NN), d3(ct, d, NN))
    act, grad = split(act), split(grad)
    out_ref[...] = (out_in[...] + d3(act, d, NT)).reshape(out_ref.shape)
    more = d3(grad, u, NT)
    fng_ref[...] = more if own else fng_in[...] + more
    if own:
        wg[:, :hidden] += d3(n, grad, TN)
        wg[:, hidden:] += d3(ct, act, TN)


def theirs_first(step, me):
    core = me[0] & 1
    return jnp.where(step < 2, 1 - core, core) * 2 + (step & 1)


def run_feed(me, n, ct, out, fng, w, own, final=False, ties=()):
    tokens, model = n[0].shape
    wide = w.shape[1]
    row = pl.BlockSpec((TILE, model), lambda i, m: (theirs_first(i, m), 0))
    tie_specs, tie_args = tied(ties)
    full = shaped((tokens, model))
    last = pl.BlockSpec((1, TILE, model), lambda i, m: (theirs_first(i, m) // 2, i % 2, 0))
    return pl.pallas_call(
        partial(feed_kernel, own, final),
        grid_spec=pltpu.PrefetchScalarGridSpec(
            num_scalar_prefetch=1,
            grid=(tokens // TILE,),
            in_specs=[row] * 2
            + sequence_specs(model, theirs_first)
            + [row] * 2
            + [whole(w.shape)]
            + tie_specs,
            out_specs=[last if final else row, row] + ([whole((model, wide))] if own else []),
            scratch_shapes=[pltpu.VMEM((2, model, wide), bf16)],
        ),
        out_shape=[shaped((2, tokens // 2, model)) if final else full, full]
        + ([shaped((model, wide))] if own else []),
        compiler_params=params(),
        cost_estimate=cost((6 if own else 4) * 3 * tokens * model * wide, 30 * 2**20),
        name="feed_own" if own else "feed",
    )(me, *n, *ct, out, fng, w, *tie_args)


def norm_back(v, gain, incoming):
    xhat, r = norm_parts(v)
    scaled = incoming * gain
    grad = r * (
        scaled
        - jnp.mean(scaled, axis=-1, keepdims=True)
        - xhat * jnp.mean(scaled * xhat, axis=-1, keepdims=True)
    )
    return grad, jnp.sum(incoming * xhat, axis=0, keepdims=True), xhat


def input_back_kernel(
    other, me_ref, x_ref, xr_ref, rg_ref, gains_ref, ah_ref, al_ref, bh_ref, bl_ref,
    dq_ref, dk_ref, dv_ref, *refs,
):
    x = xr_ref[...] if other else x_ref[0]
    third = ah_ref.shape[1] // 3
    parts = (dq_ref, dk_ref, dv_ref)
    left = split(jnp.concatenate([r[:, :third] for r in parts], axis=1))
    right = split(jnp.concatenate([r[:, third:] for r in parts], axis=1))
    incoming = d3(left, (ah_ref[...], al_ref[...]), NT) + d3(right, (bh_ref[...], bl_ref[...]), NT)
    grad = rg_ref[...] + norm_back(x, gains_ref[0:1, :], incoming)[0]
    refs[-1][...] = grad.reshape(refs[-1].shape)


def run_input_back(me, other, x, rg, gains, a, b, dq, dk, dv, ties=()):
    tokens, model = rg.shape
    tie_specs, tie_args = tied(ties)

    def tile(i, m):
        core = m[0] & 1
        return (1 - core if other else core) * 2 + i

    row = pl.BlockSpec((TILE, model), lambda i, m: (tile(i, m), 0))
    return pl.pallas_call(
        partial(input_back_kernel, other),
        grid_spec=pltpu.PrefetchScalarGridSpec(
            num_scalar_prefetch=1,
            grid=(tokens // 2 // TILE,),
            in_specs=sequence_specs(model, tile)
            + [row, whole(gains.shape)]
            + [whole(a[0].shape)] * 4
            + [row, row, row]
            + tie_specs,
            out_specs=pl.BlockSpec((TILE, model), lambda i, m: (i, 0))
            if other
            else pl.BlockSpec((1, TILE, model), lambda i, m: (m[0] & 1, i, 0)),
        ),
        out_shape=shaped((tokens // 2, model) if other else (2, tokens // 2, model)),
        compiler_params=params(),
        cost_estimate=cost(9 * tokens * model * model, 20 * 2**20),
        name="input_back",
    )(me, *x, rg, gains, *a, *b, dq, dk, dv, *tie_args)


def leave_kernel(me_ref, came_ref, whole_ref, o_ref):
    o_ref[0] = came_ref[...]


def run_leave(me, mine, came):
    half, model = came.shape
    return pl.pallas_call(
        leave_kernel,
        grid_spec=pltpu.PrefetchScalarGridSpec(
            num_scalar_prefetch=1,
            grid=(half // TILE,),
            in_specs=[
                pl.BlockSpec((TILE, model), lambda t, m: (t, 0)),
                pl.BlockSpec(memory_space=pl.ANY),
            ],
            out_specs=pl.BlockSpec((1, TILE, model), lambda t, m: (1 - (m[0] & 1), t, 0)),
        ),
        out_shape=shaped((2, half, model)),
        input_output_aliases={2: 0},
        compiler_params=params(),
        cost_estimate=cost(1e6, 4 * 2**20),
        name="leave",
    )(me, came, mine)


def exchange(value, axis, flip):
    count = lax.axis_size(axis)
    return lax.ppermute(value, axis, [(i, i ^ flip) for i in range(count)])


def corner(value):
    pairs = []
    for d in range(4):
        for c in range(2):
            pairs.append((d * 2 + c, (d ^ (2 if c == 0 else 1)) * 2 + c))
    return lax.ppermute(value, ("dp", "ctx"), pairs)


def after(values, *earlier):
    return lax.optimization_barrier((tuple(values), earlier))[0]


def sides(block):
    return [exchange(block, "dp", 1), exchange(block, "dp", 2), exchange(block, "ctx", 1)]


def far(from_x, from_y):
    return corner(jnp.where(lax.axis_index("ctx") == 0, from_x, from_y))


def across_cores(*values):
    return [exchange(v, "ctx", 1) for v in values]


def by_distance(block, near, near_other, diagonal, diagonal_other):
    from_x, from_y, other = near
    return [
        block, other, from_x, near_other[0], from_y, near_other[1], diagonal, diagonal_other
    ]


def scatter_core(keep, send):
    return keep + exchange(send, "ctx", 1)


def scatter_corner(mine):
    core = lax.axis_index("ctx")
    own, to_x, to_y, to_d = (mine[:, i] for i in range(4))
    came = corner(to_d)
    return (
        own,
        jnp.where(core == 0, to_x + came, to_x),
        jnp.where(core == 0, to_y, to_y + came),
    )


def scatter_sides(own, to_x, to_y):
    return own + exchange(to_x, "dp", 1) + exchange(to_y, "dp", 2)


def other_half(block):
    theirs = lax.dynamic_index_in_dim(block, 1 - lax.axis_index("ctx"), 0, keepdims=False)
    return exchange(theirs, "ctx", 1)


def swap_in(block):
    me = lax.axis_index("ctx")
    mine = lax.dynamic_index_in_dim(block, me, 0, keepdims=False)
    came = other_half(block)
    return jnp.where(
        me == 0, jnp.concatenate([mine, came], axis=0), jnp.concatenate([came, mine], axis=0)
    )


def by_sequence(
    layer_input, segment_ids, mixer_gain, query_weight, key_weight, value_weight, shift_kernel,
    state_decay, mixer_weight, feed_gain, up_weight, down_weight, cotangent,
):
    plane = ("dp", "ctx")
    position = lax.axis_index("dp") * 2 + lax.axis_index("ctx")
    me = position.astype(jnp.int32).reshape(1)
    rows, own = query_weight.shape
    taps, few = shift_kernel.shape

    def gathered(block):
        return lax.all_gather(block, plane, axis=0, tiled=True)

    a0 = run_pack_mixer(
        me, query_weight, key_weight, value_weight, mixer_weight, mixer_gain, feed_gain,
        shift_kernel, state_decay,
    )
    a1 = exchange(a0, "tensor", 1)
    near0 = sides(a0)
    up_weight, down_weight, early = after((up_weight, down_weight, layer_input), a0)
    f0 = run_pack_feed(up_weight, down_weight)
    x_came = other_half(early)

    b0, b1, near0 = after((a0, a1, near0), f0)
    a2 = exchange(b0, "tensor", 2)
    far0 = far(*near0[:2])
    near1 = exchange(b1, "dp", 1), exchange(b1, "dp", 2)
    inner = after((*near0[:2], b1), far0)
    other0 = across_cores(*inner[:2], far0)
    other1 = exchange(inner[2], "ctx", 1)

    b0, b2, near1 = after((a0, a2, near1), far0, other0, x_came)
    a3 = exchange(b0, "tensor", 3)
    far1 = far(*near1)
    near2 = exchange(b2, "dp", 1), exchange(b2, "dp", 2)
    inner = after((*near1, b2), far1)
    near1 = (*near1, other1)
    other1 = across_cores(*inner[:2], far1)
    other2 = exchange(inner[2], "ctx", 1)
    seg = swap_in(segment_ids).astype(f32)

    g0, b3, near2 = after((f0, a3, near2), far1, other1)
    w0 = gathered(g0)
    far2 = far(*near2)
    near3 = exchange(b3, "dp", 1), exchange(b3, "dp", 2)
    f1 = exchange(g0, "tensor", 1)
    first0 = by_distance(a0, near0, other0[:2], far0, other0[2])
    first1 = by_distance(a1, near1, other1[:2], far1, other1[2])
    x = (layer_input, x_came)
    proj_a, *wa = run_project(me, x, first0, first1)
    inner = after((*near2, b3, far2), proj_a, near3)
    near2 = (*near2, other2)
    other2 = across_cores(*inner[:2], inner[3])
    other3 = exchange(inner[2], "ctx", 1)

    near3, g0, late = after((near3, f0, cotangent), far2, proj_a)
    far3 = far(*near3)
    f2 = exchange(g0, "tensor", 2)
    inner = after(near3, far3)
    near3 = (*near3, other3)
    other3 = across_cores(*inner, far3)
    ct = (cotangent, other_half(late))
    segrow = jnp.tile(seg.reshape(-1, 1, BLOCK), (1, 1, PAIR))
    seg = seg[:, None]
    first2 = by_distance(a2, near2, other2[:2], far2, other2[2])
    first3 = by_distance(a3, near3, other3[:2], far3, other3[2])
    proj_b, *wb = run_project(me, x, first2, first3)
    f1, g0 = after((f1, f0), proj_b, ct, seg)
    w1 = gathered(f1)
    f3 = exchange(g0, "tensor", 3)

    projs, gains, smalls = (proj_a, proj_b), wa[4], (wa[5], wb[5])
    mixed, states, resid, nh, nl = run_mixer(
        me, x, projs, seg, segrow, smalls, gains, wa[2:4], wb[2:4], taps
    )
    (f2,) = after((f2,), resid)
    w2 = gathered(f2)
    n = (nh, nl)
    out, fng, feed_g = run_feed(me, n, ct, resid, resid, w0, True)
    (f3,) = after((f3,), fng)
    w3 = gathered(f3)
    out, fng = run_feed(me, n, ct, out, fng, w1, False)
    out, fng = run_feed(me, n, ct, out, fng, w2, False)
    halves, fng = run_feed(me, n, ct, out, fng, w3, False, True)
    feed_g = lax.psum_scatter(feed_g, plane, scatter_dimension=0, tiled=True)
    came = other_half(halves)
    rg, dq, dk, dv, feed_gain_g, kern_g, keep, send = run_mixer_back(
        me, fng, resid, x, ct, projs, states, mixed, seg, segrow, smalls, gains, wa[2:4], wb[2:4],
        taps,
    )
    kern_g = kern_g[:, :own].reshape(taps, 8, few).transpose(1, 0, 2).reshape(8, taps * few)
    tiny = jnp.concatenate([feed_gain_g.reshape(8, rows), kern_g], axis=1)
    came_send, came_tiny = exchange(send, "ctx", 1), exchange(tiny, "ctx", 1)
    layer_output = run_leave(me, halves, came)
    keep, came_send, tiny, came_tiny = after((keep, came_send, tiny, came_tiny), layer_output)
    summed = keep + came_send
    tiny = tiny + came_tiny
    diagonal, came_tiny = corner(summed[:, 3]), exchange(tiny, "dp", 1)
    theirs = run_input_back(me, True, x, rg, gains, wa[:2], wb[:2], dq, dk, dv, (summed,))
    diagonal, theirs, came_tiny = after((diagonal, theirs, came_tiny))
    tiny = tiny + came_tiny
    core = lax.axis_index("ctx")
    to_x = exchange(jnp.where(core == 0, summed[:, 1] + diagonal, summed[:, 1]), "dp", 1)
    to_y = exchange(jnp.where(core == 0, summed[:, 2], summed[:, 2] + diagonal), "dp", 2)
    came_tiny = exchange(tiny, "dp", 2)
    came = exchange(theirs, "ctx", 1)
    mine = run_input_back(me, False, x, rg, gains, wa[:2], wb[:2], dq, dk, dv, (theirs,))
    to_x, to_y, came_tiny, came, mine = after((to_x, to_y, came_tiny, came, mine))
    mixer_g = (summed[:, 0] + to_x + to_y)[0]
    tiny = lax.dynamic_index_in_dim(tiny + came_tiny, position, 0, keepdims=False)
    joint = jnp.concatenate([query_weight, key_weight, value_weight], axis=1)
    gain_g = jnp.sum(mixer_g[:, : 3 * own] * joint, axis=1) / mixer_gain
    gain_g = gain_g + exchange(gain_g, "tensor", 1)
    came_gain = exchange(gain_g, "tensor", 2)
    input_grad = run_leave(me, mine, came)
    hidden = up_weight.shape[1]
    return (
        layer_output,
        input_grad,
        gain_g + came_gain,
        mixer_g[:, :own],
        mixer_g[:, own : 2 * own],
        mixer_g[:, 2 * own : 3 * own],
        tiny[rows:].reshape(taps, few),
        mixer_g[:, 3 * own :].T,
        tiny[:rows],
        feed_g[:, :hidden],
        feed_g[:, hidden:].T,
    )


def solution(mesh):
    shape = mesh.shape

    def chosen(*arrays):
        rows, length, model = arrays[0].shape
        heads, width = arrays[7].shape
        fits = (
            (shape["dp"], shape["ctx"], shape["tensor"]) == (4, 2, 4)
            and rows == 2
            and (heads * shape["tensor"]) % (2 * PAIR) == 0
            and PAIR * width == LANES
            and length % (BLOCK // 2) == 0
        )
        return (by_sequence if fits else on_device)(*arrays)

    return jax.shard_map(
        chosen,
        mesh=mesh,
        in_specs=(
            P("dp", "ctx", None),
            P("dp", "ctx"),
            P(("dp", "ctx")),
            P(("dp", "ctx"), "tensor"),
            P(("dp", "ctx"), "tensor"),
            P(("dp", "ctx"), "tensor"),
            P(None, ("tensor", "dp", "ctx")),
            P("tensor", None),
            P("tensor", ("dp", "ctx")),
            P(("dp", "ctx")),
            P(("dp", "ctx"), "tensor"),
            P("tensor", ("dp", "ctx")),
            P("dp", "ctx", None),
        ),
        out_specs=(
            P("dp", "ctx", None),
            P("dp", "ctx", None),
            P(("dp", "ctx")),
            P(("dp", "ctx"), "tensor"),
            P(("dp", "ctx"), "tensor"),
            P(("dp", "ctx"), "tensor"),
            P(None, ("tensor", "dp", "ctx")),
            P("tensor", ("dp", "ctx")),
            P(("dp", "ctx")),
            P(("dp", "ctx"), "tensor"),
            P("tensor", ("dp", "ctx")),
        ),
        check_vma=False,
    )
```

```python
from functools import partial

import jax
import jax.numpy as jnp
from jax import lax
from jax.experimental import pallas as pl
from jax.experimental.pallas import tpu as pltpu
from jax.sharding import PartitionSpec as P

SUBBLOCK = 64


eps = 1e-05
precise = lax.Precision.HIGHEST


def passed_along(value, axis, steps):
    count = lax.axis_size(axis)
    leading, last = (max(0, -steps), min(count, count - steps))
    return lax.ppermute(value, axis, [(source, source + steps) for source in range(leading, last)])


def carried_in(value, axis, join, neutral, backward):
    count, mine = (lax.axis_size(axis), lax.axis_index(axis))
    pieces = jax.tree.map(lambda part: lax.all_gather(part, axis), value)
    if backward:
        pieces = jax.tree.map(lambda part: part[::-1], pieces)
        mine = count - 1 - mine
    subtotal = jax.tree.map(
        lambda part, zero: jnp.full_like(part, 0) + jnp.asarray(zero, part.dtype), value, neutral
    )

    def step(position, subtotal):
        longer = join(subtotal, jax.tree.map(lambda part: part[position], pieces))
        return jax.tree.map(lambda new, old: jnp.where(position < mine, new, old), longer, subtotal)

    return lax.fori_loop(0, count - 1, step, subtotal)


def normalize(inputs, gain):
    centered = inputs - jnp.mean(inputs, axis=-1, keepdims=True)
    scaled = centered * lax.rsqrt(jnp.mean(centered * centered, axis=-1, keepdims=True) + eps)
    return scaled * gain


def project(left, right):
    return jnp.einsum(
        "btd,df->btf", left, right, precision=precise, preferred_element_type=jnp.float32
    )


def outer_sum(left, right):
    return jnp.einsum(
        "btd,btf->df", left, right, precision=precise, preferred_element_type=jnp.float32
    )


def smooth_gate(inputs):
    return jax.nn.gelu(inputs, approximate=True)


def shift_keys(extended, kernel, seg_ext):
    taps = kernel.shape[0]
    length = extended.shape[1] - taps + 1
    current = seg_ext[:, taps - 1 :]
    summed = jnp.zeros((extended.shape[0], length, extended.shape[2]), jnp.float32)
    for offset in range(taps):
        begin = taps - 1 - offset
        joined = (seg_ext[:, begin : begin + length] == current).astype(jnp.float32)
        summed = summed + kernel[offset] * extended[:, begin : begin + length] * joined[:, :, None]
    return summed


def compose(earlier, later):
    return (earlier[0] * later[0], later[0][..., None] * earlier[1] + later[1])


def geometry(segments, before_block, log_decay):
    rows, length = segments.shape
    pieces = length // SUBBLOCK
    grouped = segments.reshape(rows, pieces, SUBBLOCK)
    before = jnp.concatenate([before_block[:, None], grouped[:, :-1, -1]], axis=1)
    living = (grouped == before[:, :, None]).astype(jnp.float32)
    retained = (grouped == grouped[:, :, -1:]).astype(jnp.float32)
    position = jnp.arange(SUBBLOCK, dtype=jnp.float32)
    causal = position[:, None] >= position[None, :]
    allowed = jnp.logical_and(grouped[:, :, :, None] == grouped[:, :, None, :], causal).astype(
        jnp.float32
    )
    growing = jnp.exp(position[:, None, None] * log_decay)
    shrinking = jnp.exp(-position[:, None, None] * log_decay)
    step_in = growing * jnp.exp(log_decay)
    closing = jnp.exp((SUBBLOCK - 1.0 - position)[:, None, None] * log_decay)
    whole_decay = jnp.exp(SUBBLOCK * log_decay)[None, None] * living[:, :, -1][:, :, None, None]
    running = jnp.ones((rows,) + log_decay.shape, jnp.float32)
    carried = []
    for index in range(pieces):
        carried.append(running)
        running = running * whole_decay[:, index]
    return (
        living,
        retained,
        allowed,
        growing,
        shrinking,
        step_in,
        closing,
        whole_decay,
        jnp.stack(carried, axis=1),
        running,
    )


def local_part(queries, shifted, values, shape_info):
    (
        living,
        retained,
        allowed,
        growing,
        shrinking,
        step_in,
        closing,
        whole_decay,
        carried,
        block_decay,
    ) = shape_info
    scores = jnp.einsum(
        "bncgi,bnsgi->bngcs", queries * growing, shifted * shrinking, precision=precise
    )
    scores = scores * allowed[:, :, None]
    within = jnp.einsum("bngcs,bnsgj->bncgj", scores, values, precision=precise)
    update = jnp.einsum(
        "bncgi,bncgj->bngij",
        shifted * closing * retained[..., None, None],
        values,
        precision=precise,
    )
    running = jnp.zeros_like(update[:, 0])
    starts = []
    for index in range(update.shape[1]):
        starts.append(running)
        running = whole_decay[:, index][..., None] * running + update[:, index]
    return (within, jnp.stack(starts, axis=1), running)


def across(queries, starts, state_in, shape_info):
    (
        living,
        retained,
        allowed,
        growing,
        shrinking,
        step_in,
        closing,
        whole_decay,
        carried,
        block_decay,
    ) = shape_info
    entries = starts + carried[..., None] * state_in[:, None]
    weighted = queries * step_in * living[..., None, None]
    return jnp.einsum("bncgi,bngij->bncgj", weighted, entries, precision=precise)


def on_device(
    layer_input,
    segment_ids,
    mixer_gain,
    query_weight,
    key_weight,
    value_weight,
    shift_kernel,
    state_decay,
    mixer_weight,
    feed_gain,
    up_weight,
    down_weight,
    cotangent,
):
    (
        mixer_gain_all,
        query_all,
        key_all,
        value_all,
        kernel_all,
        mixer_all,
        feed_gain_all,
        up_all,
        down_all,
    ) = (
        lax.all_gather(mixer_gain, ("dp", "ctx"), axis=0, tiled=True),
        lax.all_gather(query_weight, ("dp", "ctx"), axis=0, tiled=True),
        lax.all_gather(key_weight, ("dp", "ctx"), axis=0, tiled=True),
        lax.all_gather(value_weight, ("dp", "ctx"), axis=0, tiled=True),
        lax.all_gather(shift_kernel, ("dp", "ctx"), axis=1, tiled=True),
        lax.all_gather(mixer_weight, ("dp", "ctx"), axis=1, tiled=True),
        lax.all_gather(feed_gain, ("dp", "ctx"), axis=0, tiled=True),
        lax.all_gather(up_weight, ("dp", "ctx"), axis=0, tiled=True),
        lax.all_gather(down_weight, ("dp", "ctx"), axis=1, tiled=True),
    )
    heads, width = state_decay.shape
    log_decay = jnp.log(state_decay)
    taps = kernel_all.shape[0]
    rows, length, model = layer_input.shape
    pieces = length // SUBBLOCK
    features = heads * width
    seg_float = segment_ids.astype(jnp.float32)
    joint_weight = jnp.concatenate([query_all, key_all, value_all], axis=1)
    normed = normalize(layer_input, mixer_gain_all)
    projected = project(normed, joint_weight)
    queries = projected[:, :, :features]
    keys_raw = projected[:, :, features : 2 * features]
    values = projected[:, :, 2 * features :]
    tail_keys, tail_segs = passed_along(
        (keys_raw[:, length - taps + 1 :], seg_float[:, length - taps + 1 :]), "ctx", 1
    )
    extended = jnp.concatenate([tail_keys, keys_raw], axis=1)
    seg_ext = jnp.concatenate([tail_segs, seg_float], axis=1)
    shift_fixed = partial(shift_keys, seg_ext=seg_ext)
    shifted = shift_fixed(extended, kernel_all)
    info = geometry(seg_float, tail_segs[:, -1], log_decay)
    block_decay = info[-1]
    head_q = queries.reshape(rows, pieces, SUBBLOCK, heads, width)
    head_k = shifted.reshape(rows, pieces, SUBBLOCK, heads, width)
    head_v = values.reshape(rows, pieces, SUBBLOCK, heads, width)
    within, starts, local_end = local_part(head_q, head_k, head_v, info)
    identity = (jnp.ones_like(block_decay), jnp.zeros_like(local_end))
    state_in = carried_in((block_decay, local_end), "ctx", compose, identity, False)[1]
    mixed = (within + across(head_q, starts, state_in, info)).reshape(rows, length, features)
    branch = lax.psum(project(mixed, mixer_all), "tensor")
    resid = layer_input + branch
    normed_feed = normalize(resid, feed_gain_all)
    pre_act = project(normed_feed, up_all)
    activated, gelu_back = jax.vjp(smooth_gate, pre_act)
    feed = lax.psum(project(activated, down_all), "tensor")
    layer_output = resid + feed
    act_grad = project(cotangent, down_all.T)
    down_grad = outer_sum(activated, cotangent)
    (pre_grad,) = gelu_back(act_grad)
    up_grad = outer_sum(normed_feed, pre_grad)
    feed_normed_grad = lax.psum(project(pre_grad, up_all.T), "tensor")
    _, feed_norm_back = jax.vjp(normalize, resid, feed_gain_all)
    resid_ln_grad, feed_gain_grad = feed_norm_back(feed_normed_grad)
    resid_grad = cotangent + resid_ln_grad
    mixed_grad = project(resid_grad, mixer_all.T)
    mixer_weight_grad = outer_sum(mixed, resid_grad)
    head_du = mixed_grad.reshape(rows, pieces, SUBBLOCK, heads, width)
    (
        living,
        retained,
        allowed,
        growing,
        shrinking,
        step_in,
        closing,
        whole_decay,
        carried,
        block_decay,
    ) = info
    own_grad = jnp.einsum(
        "bncgi,bncgj,bngi->bgij",
        head_q * step_in * living[..., None, None],
        head_du,
        carried,
        precision=precise,
    )
    identity_grad = (jnp.ones_like(block_decay), jnp.zeros_like(own_grad))
    after = carried_in((block_decay, own_grad), "ctx", compose, identity_grad, True)[1]

    def mixer_full(query_in, key_in, value_in, entering):
        inner, begins, ending = local_part(query_in, key_in, value_in, info)
        output = inner + across(query_in, begins, entering, info)
        return (output, ending + block_decay[..., None] * entering)

    _, mixer_vjp = jax.vjp(mixer_full, head_q, head_k, head_v, state_in)
    query_act_grad, shifted_grad, value_act_grad, _ = mixer_vjp((head_du, after))
    _, shift_back = jax.vjp(shift_fixed, extended, kernel_all)
    ext_grad, kernel_grad = shift_back(shifted_grad.reshape(rows, length, features))
    returned = passed_along(ext_grad[:, : taps - 1], "ctx", -1)
    key_act_grad = ext_grad[:, taps - 1 :] + jnp.pad(
        returned, ((0, 0), (length - taps + 1, 0), (0, 0))
    )
    joint_grad = jnp.concatenate(
        [
            query_act_grad.reshape(rows, length, features),
            key_act_grad,
            value_act_grad.reshape(rows, length, features),
        ],
        axis=2,
    )
    joint_weight_grad = outer_sum(normed, joint_grad)
    normed_grad = lax.psum(project(joint_grad, joint_weight.T), "tensor")
    _, mixer_norm_back = jax.vjp(normalize, layer_input, mixer_gain_all)
    input_ln_grad, mixer_gain_grad = mixer_norm_back(normed_grad)
    input_grad = resid_grad + input_ln_grad
    query_grad = joint_weight_grad[:, :features]
    key_grad = joint_weight_grad[:, features : 2 * features]
    value_grad = joint_weight_grad[:, 2 * features :]
    all_parts = tuple(
        (
            lax.psum_scatter(mixer_gain_grad, ("dp", "ctx"), scatter_dimension=0, tiled=True),
            lax.psum_scatter(query_grad, ("dp", "ctx"), scatter_dimension=0, tiled=True),
            lax.psum_scatter(key_grad, ("dp", "ctx"), scatter_dimension=0, tiled=True),
            lax.psum_scatter(value_grad, ("dp", "ctx"), scatter_dimension=0, tiled=True),
            lax.psum_scatter(kernel_grad, ("dp", "ctx"), scatter_dimension=1, tiled=True),
            lax.psum_scatter(mixer_weight_grad, ("dp", "ctx"), scatter_dimension=1, tiled=True),
            lax.psum_scatter(feed_gain_grad, ("dp", "ctx"), scatter_dimension=0, tiled=True),
            lax.psum_scatter(up_grad, ("dp", "ctx"), scatter_dimension=0, tiled=True),
            lax.psum_scatter(down_grad, ("dp", "ctx"), scatter_dimension=1, tiled=True),
        )
    )
    return (layer_output, input_grad) + all_parts


PAIR = 2
BLOCK = 128
LANES = 128
LIMIT = 60
TILE = 256
C_GELU = 0.7978845608028654
NN = ((1,), (0,))
NT = ((1,), (1,))
TN = ((0,), (0,))
f32, bf16 = jnp.float32, jnp.bfloat16


def params(limit=LIMIT):
    return pltpu.CompilerParams(vmem_limit_bytes=limit * 2**20)


def cost(flops, moved):
    return pl.CostEstimate(flops=int(flops), bytes_accessed=int(moved), transcendentals=0)


def shaped(shape, dtype=jnp.float32):
    return jax.ShapeDtypeStruct(shape, dtype)


def split(a):
    high = a.astype(bf16)
    return high, (a - high.astype(f32)).astype(bf16)


def d3(left, right, dims):
    dot = partial(lax.dot_general, dimension_numbers=(dims, ((), ())), preferred_element_type=f32)
    return dot(left[0], right[0]) + dot(left[1], right[0]) + dot(left[0], right[1])


def d3_low(left, right, dims):
    dot = partial(lax.dot_general, dimension_numbers=(dims, ((), ())), preferred_element_type=f32)
    rows = left[0].shape[0]
    both = dot(jnp.concatenate(left, axis=0), right[0])
    return both[:rows] + both[rows:] + dot(left[0], right[1])


def tied(arrays):
    specs = [
        pl.BlockSpec((1,) * (a.ndim - 2) + (8, 128), lambda *_, n=a.ndim: (0,) * n) for a in arrays
    ]
    return specs, list(arrays)


def norm_parts(v):
    centered = v - jnp.mean(v, axis=-1, keepdims=True)
    r = lax.rsqrt(jnp.mean(centered * centered, axis=-1, keepdims=True) + eps)
    return centered * r, r


def whole(shape):
    return pl.BlockSpec(
        shape, lambda *_: (0,) * len(shape), pipeline_mode=pl.Buffered(buffer_count=1)
    )


def scalar():
    return pl.BlockSpec(memory_space=pltpu.SMEM)


def pack_mixer_kernel(me_ref, q_ref, k_ref, v_ref, m_ref, mg_ref, fg_ref, kern_ref, decay_ref, o_ref):
    rows, own = q_ref.shape
    taps, few = kern_ref.shape
    heads, width = decay_ref.shape
    o_ref[0:rows, 0:own] = q_ref[...]
    o_ref[0:rows, own : 2 * own] = k_ref[...]
    o_ref[0:rows, 2 * own : 3 * own] = v_ref[...]
    o_ref[0:rows, 3 * own :] = jnp.transpose(m_ref[...])
    o_ref[rows:, :] = jnp.zeros((8, o_ref.shape[1]), f32)
    for b in range(8):

        @pl.when(me_ref[0] == b)
        def _():
            o_ref[rows : rows + 1, b * rows : (b + 1) * rows] = mg_ref[...]
            o_ref[rows + 1 : rows + 2, b * rows : (b + 1) * rows] = fg_ref[...]
            o_ref[rows + 2 : rows + 2 + taps, b * few : (b + 1) * few] = kern_ref[...]

    @pl.when(me_ref[0] == 0)
    def _():
        for h in range(heads):
            at = rows + 2 + taps
            o_ref[at : at + 1, h * width : (h + 1) * width] = decay_ref[h : h + 1, :]


def run_pack_mixer(me, q, k, v, m, mg, fg, kern, decay):
    rows, own = q.shape
    args = (q, k, v, m, mg[None], fg[None], kern, decay)
    return pl.pallas_call(
        pack_mixer_kernel,
        grid=(1,),
        in_specs=[scalar()] + [whole(a.shape) for a in args],
        out_specs=whole((rows + 8, 4 * own)),
        out_shape=shaped((rows + 8, 4 * own)),
        compiler_params=params(),
        cost_estimate=cost(1e6, 2**20),
        name="pack_mixer",
    )(me, *args)


def pack_feed_kernel(up_ref, down_ref, o_ref):
    hidden = up_ref.shape[1]
    o_ref[:, :hidden] = up_ref[...]
    o_ref[:, hidden:] = jnp.transpose(down_ref[...])


def run_pack_feed(up, down):
    return pl.pallas_call(
        pack_feed_kernel,
        grid=(1,),
        in_specs=[whole(up.shape), whole(down.shape)],
        out_specs=whole((up.shape[0], 2 * up.shape[1])),
        out_shape=shaped((up.shape[0], 2 * up.shape[1])),
        compiler_params=params(),
        cost_estimate=cost(1e6, 2 * 2**20),
        name="pack_feed",
    )(up, down)


def sequence_specs(model, order):
    def mine(i, m):
        return (m[0] & 1, order(i, m) % 2, 0)

    def came(i, m):
        return (order(i, m) % 2, 0)

    return [pl.BlockSpec((1, TILE, model), mine), pl.BlockSpec((TILE, model), came)]


def sequence_tile(tile, me_ref, mine_ref, came_ref):
    own = tile // 2 == (me_ref[0] & 1)
    return jnp.where(own, mine_ref[0], came_ref[...])


def project_kernel(me_ref, x_ref, xr_ref, *refs):
    first, second = refs[0:8], refs[8:16]
    o_ref, wh_ref, wl_ref, mh_ref, ml_ref, gains_ref, small_ref = refs[-7:]
    own = first[0].shape[1] // 4
    rows = wh_ref.shape[0] // 8

    @pl.when(pl.program_id(0) == 0)
    def _():
        for r in range(8):
            at = pl.ds(pl.multiple_of((me_ref[0] ^ r) * rows, rows), rows)
            a, b = first[r][0:rows, :], second[r][0:rows, :]
            for i in range(4):
                both = jnp.concatenate(
                    [a[:, i * own : (i + 1) * own], b[:, i * own : (i + 1) * own]], axis=1
                )
                high, low = split(both)
                if i < 3:
                    wh_ref[at, i * 2 * own : (i + 1) * 2 * own] = high
                    wl_ref[at, i * 2 * own : (i + 1) * 2 * own] = low
                else:
                    mh_ref[at, :] = high
                    ml_ref[at, :] = low
        sums = []
        for pieces in (first, second):
            total = pieces[0][rows:, :]
            for r in range(1, 8):
                total = total + pieces[r][rows:, :]
            sums.append(total)
        gains_ref[...] = sums[0]
        small_ref[...] = jnp.concatenate([s[:, :own] for s in sums], axis=1)

    x = sequence_tile(pl.program_id(0), me_ref, x_ref, xr_ref)
    n = split(norm_parts(x)[0] * gains_ref[0:1, :])
    o_ref[...] = d3(n, (wh_ref[...], wl_ref[...]), NN)


def run_project(me, x, first, second, ties=()):
    rows, half, model = x[0].shape
    tokens = rows * half
    own = first[0].shape[1] // 4
    wide = 6 * own
    piece = whole(first[0].shape)
    weights = [(model, wide)] * 2 + [(model, 2 * own)] * 2
    few = [(8, model), (8, 2 * own)]
    tie_specs, tie_args = tied(ties)
    return pl.pallas_call(
        project_kernel,
        grid_spec=pltpu.PrefetchScalarGridSpec(
            num_scalar_prefetch=1,
            grid=(tokens // TILE,),
            in_specs=sequence_specs(model, lambda i, m: i) + [piece] * 16 + tie_specs,
            out_specs=[pl.BlockSpec((TILE, wide), lambda i, m: (i, 0))]
            + [whole(s) for s in weights + few],
        ),
        out_shape=[shaped((tokens, wide))]
        + [shaped(s, bf16) for s in weights]
        + [shaped(s) for s in few],
        compiler_params=params(),
        cost_estimate=cost(6 * tokens * model * wide, 20 * 2**20),
        name="project",
    )(me, *x, *first, *second, *tie_args)


def spread(parts, masks):
    return tuple(jnp.concatenate([p * m for m in masks], axis=0) for p in parts)


def lane_masks(lanes):
    which = lax.broadcasted_iota(jnp.int32, (1, lanes), 1) // (lanes // PAIR)
    return [jnp.where(which == h, 1.0, 0.0).astype(bf16) for h in range(PAIR)]


def square_mask(lanes):
    a = lax.broadcasted_iota(jnp.int32, (lanes, lanes), 0) // (lanes // PAIR)
    b = lax.broadcasted_iota(jnp.int32, (lanes, lanes), 1) // (lanes // PAIR)
    return jnp.where(a == b, 1.0, 0.0)


def fill_tables(decay, grow, shrink, dec, end, full):
    size, model = grow.shape
    lanes = dec.shape[0]
    rates = jnp.log(decay)
    position = lax.broadcasted_iota(jnp.int32, (size, model), 0).astype(f32)
    grow[...] = jnp.exp(position * rates)
    shrink[...] = jnp.exp(-position * rates)
    for p in range(model // lanes):
        s = slice(p * lanes, (p + 1) * lanes)
        column = jnp.transpose(jnp.broadcast_to(rates[:, s], (lanes, lanes)))
        dec[:, s] = jnp.exp(column)
        end[:, s] = jnp.exp((size - 1.0) * column)
        full[:, s] = jnp.exp(float(size) * column)


def joined(extended, size, taps):
    now = extended[8:]
    return [jnp.where(extended[8 - j : 8 - j + size] == now, 1.0, 0.0) for j in range(1, taps)]


def shift_forward(keys, before, kern, same, taps):
    extended = jnp.concatenate([before, keys], axis=0)
    size = keys.shape[0]
    moved = [keys]
    for j in range(1, taps):
        moved.append(extended[8 - j : 8 - j + size] * same[j - 1])
    total = kern[0:1, :] * keys
    for j in range(1, taps):
        total = total + kern[j : j + 1, :] * moved[j]
    return total, moved


def allowed_masks(seg, row):
    size, wide = seg.shape[0], row.shape[1]
    rows = lax.broadcasted_iota(jnp.int32, (size, wide), 0)
    cols = lax.broadcasted_iota(jnp.int32, (size, wide), 1) % size
    same = seg == row
    return (
        jnp.where(jnp.logical_and(rows >= cols, same), 1.0, 0.0),
        jnp.where(jnp.logical_and(rows <= cols, same), 1.0, 0.0),
    )


def pair(a_ref, b_ref):
    return jnp.concatenate([a_ref[...], b_ref[...]], axis=1)


def third_of(refs, rows, i):
    wide = refs[0].shape[1] // 3
    return jnp.concatenate([r[rows, i * wide : (i + 1) * wide] for r in refs], axis=1)


def mixer_kernel(taps, last, me_ref, proj_ref, seg_ref, segrow_ref, small_ref, *refs):
    if last:
        x_ref, xr_ref, other_ref, gains_ref, ah_ref, al_ref, bh_ref, bl_ref = refs[:8]
        state_out_ref, resid_ref, nh_ref, nl_ref = refs[8:12]
    else:
        state_out_ref, mixed_ref = refs[:2]
    state, tail, segtail, grow, shrink, dec, end, full, mixed = refs[-9:]
    size, lanes = grow.shape[0], dec.shape[0]
    projs = (proj_ref,)

    @pl.when(pl.program_id(0) == 0)
    def _():
        state[...] = jnp.zeros_like(state)
        tail[...] = jnp.zeros_like(tail)
        segtail[...] = jnp.full_like(segtail, -1.0)
        fill_tables(small_ref[2 + taps : 3 + taps], grow, shrink, dec, end, full)

    kern = small_ref[2 : 2 + taps]
    masks = lane_masks(lanes)
    square = square_mask(lanes)
    groups = [slice(g * lanes, (g + 1) * lanes) for g in range(state.shape[1] // lanes)]
    before_keys, before = tail[...], segtail[...]
    for chunk in range(proj_ref.shape[0] // size):
        here = slice(chunk * size, (chunk + 1) * size)
        seg = seg_ref[here, :]
        extended = jnp.concatenate([before, seg], axis=0)
        living = jnp.where(seg == before[7:8], 1.0, 0.0)
        kept = jnp.where(seg == seg[size - 1 :], 1.0, 0.0)
        goes_on = living[size - 1 :]
        q_all, keys, v_all = (third_of(projs, here, i) for i in range(3))
        shifted, _ = shift_forward(keys, before_keys, kern, joined(extended, size, taps), taps)
        before_keys, before = keys[size - 8 :, :], seg[size - 8 :]
        allowed, _ = allowed_masks(seg, segrow_ref[chunk])
        state_out_ref[chunk] = state[...]
        qg, kf, v, scores = [], [], [], []
        for s in groups:
            qg.append(split(q_all[:, s] * grow[:, s]))
            kf.append(shifted[:, s] * shrink[:, s])
            v.append(split(v_all[:, s]))
            scores.append(d3_low(qg[-1], spread(split(kf[-1]), masks), NT))
        updates = [d3(split(k * kept), w, TN) * square for k, w in zip(kf, v)]
        weights = [split(score * allowed) for score in scores]
        for g, s in enumerate(groups):
            part = d3_low(weights[g], spread(v[g], masks), NN)
            mixed[here, s] = part + living * d3_low(qg[g], split(state[:, s] * dec[:, s]), NN)
        for g, s in enumerate(groups):
            state[:, s] = state[:, s] * (full[:, s] * goes_on) + end[:, s] * updates[g]
    tail[...] = before_keys
    segtail[...] = before
    if not last:
        mixed_ref[...] = mixed[...]
        return
    resid = (
        sequence_tile(pl.program_id(0), me_ref, x_ref, xr_ref)
        + d3(split(other_ref[...]), (ah_ref[...], al_ref[...]), NT)
        + d3(split(mixed[...]), (bh_ref[...], bl_ref[...]), NT)
    )
    resid_ref[...] = resid
    nh_ref[...], nl_ref[...] = split(norm_parts(resid)[0] * gains_ref[1:2, :])


def mixer_scratch(model):
    return [pltpu.VMEM((BLOCK, model), f32)] * 2 + [pltpu.VMEM((LANES, model), f32)] * 3


def run_mixer(me, proj, seg, segrow, small, taps, more=(), ties=()):
    tokens, third = proj.shape[0], proj.shape[1] // 3
    chunks = TILE // BLOCK

    def row(width):
        return pl.BlockSpec((TILE, width), lambda c, m: (c, 0))

    extra_specs, extra = [], []
    outs = [(row(third), shaped((tokens, third)))]
    if more:
        x, other, gains, a, b = more
        model = x[0].shape[2]
        extra_specs = sequence_specs(model, lambda i, m: i) + [row(third), whole(gains.shape)]
        extra_specs = extra_specs + [whole(a[0].shape)] * 4
        extra = [*x, other, gains, *a, *b]
        outs = [(row(model), shaped((tokens, model), t)) for t in (f32, bf16, bf16)]
    states = pl.BlockSpec((chunks, LANES, third), lambda c, m: (c, 0, 0))
    tie_specs, tie_args = tied(ties)
    return pl.pallas_call(
        partial(mixer_kernel, taps, bool(more)),
        grid_spec=pltpu.PrefetchScalarGridSpec(
            num_scalar_prefetch=1,
            grid=(tokens // TILE,),
            in_specs=[
                row(3 * third),
                row(1),
                pl.BlockSpec((chunks, 1, segrow.shape[2]), lambda c, m: (c, 0, 0)),
                whole(small.shape),
            ]
            + extra_specs
            + tie_specs,
            out_specs=[states] + [spec for spec, _ in outs],
            scratch_shapes=[
                pltpu.VMEM((LANES, third), f32),
                pltpu.VMEM((8, third), f32),
                pltpu.VMEM((8, 1), f32),
            ]
            + mixer_scratch(third)
            + [pltpu.VMEM((TILE, third), f32)],
        ),
        out_shape=[shaped((tokens // BLOCK, LANES, third))] + [shape for _, shape in outs],
        compiler_params=params(),
        cost_estimate=cost(6e9 + (7e9 if more else 0), 10 * 2**20),
        name="mixer_out" if more else "mixer",
    )(me, proj, seg, segrow, small, *extra, *tie_args)


def mixer_back_kernel(
    taps, me_ref, fng_ref, resid_ref, x_ref, xr_ref, ct_ref, cr_ref, pa_ref, pb_ref, ba_ref, bb_ref,
    ta_ref, tb_ref, mixed_ref, seg_ref, segb_ref, segrow_ref, sa_ref, sb_ref, gains_ref,
    ah_ref, al_ref, bh_ref, bl_ref, qah_ref, qal_ref, qbh_ref, qbl_ref, *refs,
):
    (
        ig_ref, gg_ref, g2_ref, dkern_ref, keep_ref, send_ref,
        grad, head, grow, shrink, dec, end, full, du_all, da, db, wg,
    ) = refs[-17:]
    size, lanes = grow.shape[0], dec.shape[0]
    step, steps = pl.program_id(0), pl.num_programs(0)
    projs = (pa_ref, pb_ref)

    @pl.when(step == 0)
    def _():
        grad[...] = jnp.zeros_like(grad)
        head[...] = jnp.zeros_like(head)
        dkern_ref[...] = jnp.zeros_like(dkern_ref)
        gg_ref[...] = jnp.zeros_like(gg_ref)
        g2_ref[...] = jnp.zeros_like(g2_ref)
        wg[...] = jnp.zeros_like(wg)
        fill_tables(pair(sa_ref, sb_ref)[2 + taps : 3 + taps], grow, shrink, dec, end, full)

    third = ah_ref.shape[1]
    tile = steps - 1 - step
    back, gain_grad, _ = norm_back(resid_ref[...], gains_ref[1:2, :], fng_ref[...])
    rg = sequence_tile(tile, me_ref, ct_ref, cr_ref) + back
    g2_ref[...] += gain_grad
    r2 = split(rg)
    du_all[:, :third] = d3(r2, (ah_ref[...], al_ref[...]), NN)
    du_all[:, third:] = d3(r2, (bh_ref[...], bl_ref[...]), NN)

    kern = pair(sa_ref, sb_ref)[2 : 2 + taps]
    masks = lane_masks(lanes)
    square = square_mask(lanes)
    model = grad.shape[1]
    groups = [slice(g * lanes, (g + 1) * lanes) for g in range(model // lanes)]
    count = len(groups)
    chunks = rg.shape[0] // size
    for chunk in reversed(range(chunks)):
        here = slice(chunk * size, (chunk + 1) * size)
        seg = seg_ref[here, :]
        q_all, keys, v_all = (third_of(projs, here, i) for i in range(3))
        if chunk:
            just = slice(chunk * size - 8, chunk * size)
            before, before_keys = seg_ref[just, :], third_of(projs, just, 1)
        else:
            before = jnp.where(step == steps - 1, -1.0, segb_ref[...])
            before_keys = pair(ba_ref, bb_ref)
        extended = jnp.concatenate([before, seg], axis=0)
        living = jnp.where(seg == before[7:8], 1.0, 0.0)
        kept = jnp.where(seg == seg[size - 1 :], 1.0, 0.0)
        goes_on = living[size - 1 :]
        same = joined(extended, size, taps)
        shifted, moved = shift_forward(keys, before_keys, kern, same, taps)
        allowed, allowed_t = allowed_masks(seg, segrow_ref[chunk])
        qf = [q_all[:, s] * grow[:, s] for s in groups]
        qg = [split(q) for q in qf]
        kg = [split(shifted[:, s] * shrink[:, s]) for s in groups]
        v = [split(v_all[:, s]) for s in groups]
        du = [split(du_all[here, s]) for s in groups]
        p_t = [d3_low(kg[g], spread(qg[g], masks), NT) for g in range(count)]
        dp = [d3_low(du[g], spread(v[g], masks), NT) for g in range(count)]
        dp_t = [d3_low(v[g], spread(du[g], masks), NT) for g in range(count)]
        updates = [d3(split(qf[g] * living), du[g], TN) * square for g in range(count)]
        p_t = [split(p * allowed_t) for p in p_t]
        dp = [split(p * allowed) for p in dp]
        dp_t = [split(p * allowed_t) for p in dp_t]
        for g, s in enumerate(groups):
            first = s.start < third
            at = s.start - (0 if first else third)
            to = da if first else db
            states = (ta_ref if first else tb_ref)[chunk, :, at : at + lanes]
            entering = split(states * dec[:, s])
            leaving = split(grad[:, s] * end[:, s])
            dqg = d3_low(dp[g], spread(kg[g], masks), NN) + living * d3_low(du[g], entering, NT)
            dkg = d3_low(dp_t[g], spread(qg[g], masks), NN) + kept * d3_low(v[g], leaving, NT)
            dv = d3_low(p_t[g], spread(du[g], masks), NN) + kept * d3_low(kg[g], leaving, NN)
            to[here, 2 * third + at : 2 * third + at + lanes] = dv
            to[here, at : at + lanes] = dqg * grow[:, s]
            dshift = dkg * shrink[:, s]
            grad[:, s] = grad[:, s] * (full[:, s] * goes_on) + dec[:, s] * updates[g]
            total = kern[0:1, s] * dshift
            for j in range(1, taps):
                part = dshift * same[j - 1]
                longer = jnp.concatenate([part, head[j - 1, :, s]], axis=0)
                total = total + kern[j : j + 1, s] * longer[j : j + size]
                head[j - 1, :, s] = part[0:8]
            to[here, third + at : third + at + lanes] = total
            if g < 2:
                for j in range(taps):
                    dkern_ref[j : j + 1, s] += jnp.sum(
                        dshift * moved[j][:, s], axis=0, keepdims=True
                    )

    own = keep_ref.shape[-1] // 4
    x = sequence_tile(tile, me_ref, x_ref, xr_ref)
    left, right = split(da[...]), split(db[...])
    incoming = d3(left, (qah_ref[...], qal_ref[...]), NT)
    incoming = incoming + d3(right, (qbh_ref[...], qbl_ref[...]), NT)
    back, gain_grad, xhat = norm_back(x, gains_ref[0:1, :], incoming)
    ig_ref[0] = rg + back
    gg_ref[...] += gain_grad
    n = split(xhat * gains_ref[0:1, :])
    joint = tuple(
        jnp.concatenate([p[:, i * third : i * third + own] for i in range(3)], axis=1) for p in left
    )
    wg[:, : 3 * own] += d3(n, joint, TN)
    wg[:, 3 * own :] += d3(r2, split(mixed_ref[:, :own]), TN)

    @pl.when(step == steps - 1)
    def _():
        store_blocks(me_ref[0], wg, keep_ref, send_ref, 0)


def run_mixer_back(
    me, fng, resid, x, ct, projs, states, mixed, seg, segrow, smalls, gains, a, b, qa, qb, taps
):
    tokens, model = resid.shape
    third = projs[0].shape[1] // 3
    own = third // 2
    chunks = TILE // BLOCK
    last = tokens // TILE - 1
    blocks = (1, 4, model // 8, 4 * own)

    def prior(c):
        return jnp.maximum((last - c) * (TILE // 8) - 1, 0)

    row = pl.BlockSpec((TILE, model), lambda c, m: (last - c, 0))
    proj = pl.BlockSpec((TILE, 3 * third), lambda c, m: (last - c, 0))
    before = pl.BlockSpec((8, third), lambda c, m: (prior(c), 1))
    state = pl.BlockSpec((chunks, LANES, third), lambda c, m: (last - c, 0, 0))
    halves = pl.BlockSpec((1, TILE, model), lambda c, m: ((last - c) // 2, (last - c) % 2, 0))
    return pl.pallas_call(
        partial(mixer_back_kernel, taps),
        grid_spec=pltpu.PrefetchScalarGridSpec(
            num_scalar_prefetch=1,
            grid=(last + 1,),
            in_specs=[row, row]
            + sequence_specs(model, lambda c, m: last - c) * 2
            + [proj, proj, before, before, state, state]
            + [
                pl.BlockSpec((TILE, third), lambda c, m: (last - c, 0)),
                pl.BlockSpec((TILE, 1), lambda c, m: (last - c, 0)),
                pl.BlockSpec((8, 1), lambda c, m: (prior(c), 0)),
                pl.BlockSpec((chunks, 1, segrow.shape[2]), lambda c, m: (last - c, 0, 0)),
                whole(smalls[0].shape),
                whole(smalls[1].shape),
                whole(gains.shape),
            ]
            + [whole(a[0].shape)] * 4
            + [whole(qa[0].shape)] * 4,
            out_specs=[halves, whole((1, model)), whole((1, model)), whole((taps, model))]
            + [whole(blocks), whole(blocks)],
            scratch_shapes=[
                pltpu.VMEM((LANES, model), f32),
                pltpu.VMEM((taps - 1, 8, model), f32),
            ]
            + mixer_scratch(model)
            + [pltpu.VMEM((TILE, model), f32)]
            + [pltpu.VMEM((TILE, 3 * third), f32)] * 2
            + [pltpu.VMEM((model, 4 * own), f32)],
        ),
        out_shape=[shaped((2, tokens // 2, model)), shaped((1, model)), shaped((1, model))]
        + [shaped((taps, model)), shaped(blocks), shaped(blocks)],
        compiler_params=params(),
        cost_estimate=cost(1e11, 60 * 2**20),
        name="mixer_back",
    )(
        me, fng, resid, *x, *ct, *projs, *projs, *states, mixed, seg, seg, segrow, *smalls, gains,
        *a, *b, *qa, *qb,
    )


def gelu_parts(pre, back):
    th = jnp.tanh(pre * (C_GELU + (C_GELU * 0.044715) * (pre * pre)))
    half = 0.5 + 0.5 * th
    act = pre * half
    slope = half + (1.0 - th) * act * (C_GELU + (3 * C_GELU * 0.044715) * (pre * pre))
    return act, back * slope


def store_blocks(me, g, keep_ref, send_ref, i):
    rows = g.shape[0] // 8
    for b in range(8):
        r = me ^ b
        part = g[b * rows : (b + 1) * rows]
        where = r // 2

        @pl.when((r & 1) == 0)
        def _():
            keep_ref[i, where] = part

        @pl.when((r & 1) == 1)
        def _():
            send_ref[i, where] = part


def feed_kernel(own, final, me_ref, nh_ref, nl_ref, ct_ref, cr_ref, out_in, fng_in, w_in, *refs):
    if own:
        out_ref, fng_ref, wg, w = refs[-4:]
    else:
        out_ref, fng_ref, w = refs[-3:]
    step = pl.program_id(0)
    hidden = w.shape[2] // 2

    @pl.when(step == 0)
    def _():
        w[0], w[1] = split(w_in[...].reshape(w.shape[1:]))
        if own:
            wg[...] = jnp.zeros_like(wg)

    tile = theirs_first(step, me_ref)
    n = (nh_ref[...], nl_ref[...])
    ct = split(sequence_tile(tile, me_ref, ct_ref, cr_ref))
    u, d = (w[0, :, :hidden], w[1, :, :hidden]), (w[0, :, hidden:], w[1, :, hidden:])
    act, grad = gelu_parts(d3(n, u, NN), d3(ct, d, NN))
    act, grad = split(act), split(grad)
    out_ref[...] = (out_in[...] + d3(act, d, NT)).reshape(out_ref.shape)
    more = d3(grad, u, NT)
    fng_ref[...] = more if own else fng_in[...] + more
    if own:
        wg[:, :hidden] += d3(n, grad, TN)
        wg[:, hidden:] += d3(ct, act, TN)


def theirs_first(step, me):
    core = me[0] & 1
    return jnp.where(step < 2, 1 - core, core) * 2 + (step & 1)


def run_feed(me, n, ct, out, fng, w, slot, slots, own, final=False, ties=()):
    tokens, model = n[0].shape
    wide = w.shape[1] // slots
    part = pl.BlockSpec(
        (model, wide), lambda *_: (0, slot), pipeline_mode=pl.Buffered(buffer_count=1)
    )
    row = pl.BlockSpec((TILE, model), lambda i, m: (theirs_first(i, m), 0))
    tie_specs, tie_args = tied(ties)
    full = shaped((tokens, model))
    last = pl.BlockSpec((1, TILE, model), lambda i, m: (theirs_first(i, m) // 2, i % 2, 0))
    return pl.pallas_call(
        partial(feed_kernel, own, final),
        grid_spec=pltpu.PrefetchScalarGridSpec(
            num_scalar_prefetch=1,
            grid=(tokens // TILE,),
            in_specs=[row] * 2
            + sequence_specs(model, theirs_first)
            + [row] * 2
            + [part]
            + tie_specs,
            out_specs=[last if final else row, row] + ([whole((model, wide))] if own else []),
            scratch_shapes=[pltpu.VMEM((2, model, wide), bf16)],
        ),
        out_shape=[shaped((2, tokens // 2, model)) if final else full, full]
        + ([shaped((model, wide))] if own else []),
        compiler_params=params(),
        cost_estimate=cost((6 if own else 4) * 3 * tokens * model * wide, 30 * 2**20),
        name="feed_own" if own else "feed",
    )(me, *n, *ct, out, fng, w, *tie_args)


def norm_back(v, gain, incoming):
    xhat, r = norm_parts(v)
    scaled = incoming * gain
    grad = r * (
        scaled
        - jnp.mean(scaled, axis=-1, keepdims=True)
        - xhat * jnp.mean(scaled * xhat, axis=-1, keepdims=True)
    )
    return grad, jnp.sum(incoming * xhat, axis=0, keepdims=True), xhat


def leave_kernel(me_ref, came_ref, whole_ref, o_ref):
    o_ref[0] = came_ref[...]


def run_leave(me, mine, came):
    half, model = came.shape
    return pl.pallas_call(
        leave_kernel,
        grid_spec=pltpu.PrefetchScalarGridSpec(
            num_scalar_prefetch=1,
            grid=(half // TILE,),
            in_specs=[
                pl.BlockSpec((TILE, model), lambda t, m: (t, 0)),
                pl.BlockSpec(memory_space=pl.ANY),
            ],
            out_specs=pl.BlockSpec((1, TILE, model), lambda t, m: (1 - (m[0] & 1), t, 0)),
        ),
        out_shape=shaped((2, half, model)),
        input_output_aliases={2: 0},
        compiler_params=params(),
        cost_estimate=cost(1e6, 4 * 2**20),
        name="leave",
    )(me, came, mine)


def exchange(value, axis, flip):
    count = lax.axis_size(axis)
    return lax.ppermute(value, axis, [(i, i ^ flip) for i in range(count)])


def corner(value):
    pairs = []
    for d in range(4):
        for c in range(2):
            pairs.append((d * 2 + c, (d ^ (2 if c == 0 else 1)) * 2 + c))
    return lax.ppermute(value, ("dp", "ctx"), pairs)


def after(values, *earlier):
    return lax.optimization_barrier((tuple(values), earlier))[0]


def sides(block):
    return [exchange(block, "dp", 1), exchange(block, "dp", 2), exchange(block, "ctx", 1)]


def far(from_x, from_y):
    return corner(jnp.where(lax.axis_index("ctx") == 0, from_x, from_y))


def across_cores(*values):
    return [exchange(v, "ctx", 1) for v in values]


def by_distance(block, near, near_other, diagonal, diagonal_other):
    from_x, from_y, other = near
    return [
        block, other, from_x, near_other[0], from_y, near_other[1], diagonal, diagonal_other
    ]


def scatter_core(keep, send):
    return keep + exchange(send, "ctx", 1)


def scatter_corner(mine):
    core = lax.axis_index("ctx")
    own, to_x, to_y, to_d = (mine[:, i] for i in range(4))
    came = corner(to_d)
    return (
        own,
        jnp.where(core == 0, to_x + came, to_x),
        jnp.where(core == 0, to_y, to_y + came),
    )


def scatter_sides(own, to_x, to_y):
    return own + exchange(to_x, "dp", 1) + exchange(to_y, "dp", 2)


def other_half(block):
    theirs = lax.dynamic_index_in_dim(block, 1 - lax.axis_index("ctx"), 0, keepdims=False)
    return exchange(theirs, "ctx", 1)


def swap_in(block):
    me = lax.axis_index("ctx")
    mine = lax.dynamic_index_in_dim(block, me, 0, keepdims=False)
    came = other_half(block)
    return jnp.where(
        me == 0, jnp.concatenate([mine, came], axis=0), jnp.concatenate([came, mine], axis=0)
    )


def by_sequence(
    layer_input, segment_ids, mixer_gain, query_weight, key_weight, value_weight, shift_kernel,
    state_decay, mixer_weight, feed_gain, up_weight, down_weight, cotangent,
):
    plane = ("dp", "ctx")
    position = lax.axis_index("dp") * 2 + lax.axis_index("ctx")
    me = position.astype(jnp.int32).reshape(1)
    rows, own = query_weight.shape
    taps, few = shift_kernel.shape

    def gathered(block):
        return lax.all_gather(block, plane, axis=0, tiled=True)

    a0 = run_pack_mixer(
        me, query_weight, key_weight, value_weight, mixer_weight, mixer_gain, feed_gain,
        shift_kernel, state_decay,
    )
    a1 = exchange(a0, "tensor", 1)
    near0 = sides(a0)
    f0 = run_pack_feed(*after((up_weight, down_weight), a0))
    x_came = other_half(after((layer_input,), a0)[0])

    b0, b1, near0 = after((a0, a1, near0), f0)
    a2 = exchange(b0, "tensor", 2)
    far0 = far(*near0[:2])
    near1 = exchange(b1, "dp", 1), exchange(b1, "dp", 2)
    inner = after((*near0[:2], b1), far0)
    other0 = across_cores(*inner[:2], far0)
    other1 = exchange(inner[2], "ctx", 1)

    b0, b2, near1 = after((a0, a2, near1), far0, other0, x_came)
    a3 = exchange(b0, "tensor", 3)
    far1 = far(*near1)
    near2 = exchange(b2, "dp", 1), exchange(b2, "dp", 2)
    inner = after((*near1, b2), far1)
    near1 = (*near1, other1)
    other1 = across_cores(*inner[:2], far1)
    other2 = exchange(inner[2], "ctx", 1)
    seg = swap_in(segment_ids).astype(f32)

    g0, b3, near2 = after((f0, a3, near2), far1, other1)
    w0 = gathered(g0)
    far2 = far(*near2)
    near3 = exchange(b3, "dp", 1), exchange(b3, "dp", 2)
    f1 = exchange(g0, "tensor", 1)
    f2 = exchange(g0, "tensor", 2)
    first0 = by_distance(a0, near0, other0[:2], far0, other0[2])
    first1 = by_distance(a1, near1, other1[:2], far1, other1[2])
    x = (layer_input, x_came)
    proj_a, *wa = run_project(me, x, first0, first1)
    inner = after((*near2, b3, far2), proj_a, near3)
    near2 = (*near2, other2)
    other2 = across_cores(*inner[:2], inner[3])
    other3 = exchange(inner[2], "ctx", 1)

    near3, late = after((near3, cotangent), far2, proj_a)
    far3 = far(*near3)
    ct = (cotangent, other_half(late))
    segrow = jnp.tile(seg.reshape(-1, 1, BLOCK), (1, 1, PAIR))
    seg = seg[:, None]
    states_a, mixed_a = run_mixer(me, proj_a, seg, segrow, wa[5], taps)
    f1, f2, far3, g0 = after((f1, f2, far3, f0), mixed_a)
    w12 = gathered(jnp.concatenate([f1, f2], axis=1))
    inner = after(near3, far3)
    near3 = (*near3, other3)
    other3 = across_cores(*inner, far3)
    first2 = by_distance(a2, near2, other2[:2], far2, other2[2])
    first3 = by_distance(a3, near3, other3[:2], far3, other3[2])
    proj_b, *wb = run_project(me, x, first2, first3)
    (g0,) = after((g0,), proj_b, ct)
    f3 = exchange(g0, "tensor", 3)

    projs, gains, smalls = (proj_a, proj_b), wa[4], (wa[5], wb[5])
    more = (x, mixed_a, gains, wa[2:4], wb[2:4])
    states_b, resid, nh, nl = run_mixer(me, proj_b, seg, segrow, wb[5], taps, more)
    n = (nh, nl)
    out, fng, feed_g = run_feed(me, n, ct, resid, resid, w0, 0, 1, True)
    (f3,) = after((f3,), fng)
    w3 = gathered(f3)
    out, fng = run_feed(me, n, ct, out, fng, w12, 0, 2, False)
    out, fng = run_feed(me, n, ct, out, fng, w12, 1, 2, False)
    out_halves, fng = run_feed(me, n, ct, out, fng, w3, 0, 1, False, True)
    feed_g = lax.psum_scatter(feed_g, plane, scatter_dimension=0, tiled=True)
    came = other_half(out_halves)
    halves, mixer_gain_g, feed_gain_g, kern_g, keep, send = run_mixer_back(
        me, fng, resid, x, ct, projs, (states_a, states_b), mixed_a, seg, segrow, smalls, gains,
        wa[2:4], wb[2:4], wa[:2], wb[:2], taps,
    )
    layer_output = run_leave(me, out_halves, came)
    core = lax.axis_index("ctx")
    came_send = exchange(send, "ctx", 1)
    diagonal = keep[:, 3] + came_send[:, 3]
    keep, came_send = after((keep, came_send), diagonal)
    kern_g = kern_g[:, :own].reshape(taps, 8, few).transpose(1, 0, 2).reshape(8, taps * few)
    gains_g = [g.reshape(8, rows) for g in (mixer_gain_g, feed_gain_g)]
    tiny = jnp.concatenate(gains_g + [kern_g], axis=1)
    diagonal = corner(diagonal)
    tiny = tiny + exchange(tiny, "ctx", 1)
    came = other_half(halves)
    to_own, to_x, to_y = (keep[:, i] + came_send[:, i] for i in range(3))
    diagonal, to_own, to_x, to_y, tiny, came = after((diagonal, to_own, to_x, to_y, tiny, came))
    came_x = exchange(jnp.where(core == 0, to_x + diagonal, to_x), "dp", 1)
    came_y = exchange(jnp.where(core == 0, to_y, to_y + diagonal), "dp", 2)
    tiny = tiny + exchange(tiny, "dp", 1)
    input_grad = run_leave(me, halves, came)
    tiny = tiny + exchange(tiny, "dp", 2)
    mixer_g = (to_own + came_x + came_y)[0]
    tiny = lax.dynamic_index_in_dim(tiny, position, 0, keepdims=False)
    hidden = up_weight.shape[1]
    return (
        layer_output,
        input_grad,
        tiny[:rows],
        mixer_g[:, :own],
        mixer_g[:, own : 2 * own],
        mixer_g[:, 2 * own : 3 * own],
        tiny[2 * rows :].reshape(taps, few),
        mixer_g[:, 3 * own :].T,
        tiny[rows : 2 * rows],
        feed_g[:, :hidden],
        feed_g[:, hidden:].T,
    )


def solution(mesh):
    shape = mesh.shape

    def chosen(*arrays):
        rows, length, model = arrays[0].shape
        heads, width = arrays[7].shape
        fits = (
            (shape["dp"], shape["ctx"], shape["tensor"]) == (4, 2, 4)
            and (rows, length) == (2, 2 * TILE)
            and PAIR * width == LANES
            and 2 * heads * width % LANES == 0
        )
        return (by_sequence if fits else on_device)(*arrays)

    return jax.shard_map(
        chosen,
        mesh=mesh,
        in_specs=(
            P("dp", "ctx", None),
            P("dp", "ctx"),
            P(("dp", "ctx")),
            P(("dp", "ctx"), "tensor"),
            P(("dp", "ctx"), "tensor"),
            P(("dp", "ctx"), "tensor"),
            P(None, ("tensor", "dp", "ctx")),
            P("tensor", None),
            P("tensor", ("dp", "ctx")),
            P(("dp", "ctx")),
            P(("dp", "ctx"), "tensor"),
            P("tensor", ("dp", "ctx")),
            P("dp", "ctx", None),
        ),
        out_specs=(
            P("dp", "ctx", None),
            P("dp", "ctx", None),
            P(("dp", "ctx")),
            P(("dp", "ctx"), "tensor"),
            P(("dp", "ctx"), "tensor"),
            P(("dp", "ctx"), "tensor"),
            P(None, ("tensor", "dp", "ctx")),
            P("tensor", ("dp", "ctx")),
            P(("dp", "ctx")),
            P(("dp", "ctx"), "tensor"),
            P("tensor", ("dp", "ctx")),
        ),
        check_vma=False,
    )
```

```python
from functools import partial

import jax
import jax.numpy as jnp
from jax import lax
from jax.experimental import pallas as pl
from jax.experimental.pallas import tpu as pltpu
from jax.sharding import PartitionSpec as P

SUBBLOCK = 64


eps = 1e-05
precise = lax.Precision.HIGHEST


def passed_along(value, axis, steps):
    count = lax.axis_size(axis)
    leading, last = (max(0, -steps), min(count, count - steps))
    return lax.ppermute(value, axis, [(source, source + steps) for source in range(leading, last)])


def carried_in(value, axis, join, neutral, backward):
    count, mine = (lax.axis_size(axis), lax.axis_index(axis))
    pieces = jax.tree.map(lambda part: lax.all_gather(part, axis), value)
    if backward:
        pieces = jax.tree.map(lambda part: part[::-1], pieces)
        mine = count - 1 - mine
    subtotal = jax.tree.map(
        lambda part, zero: jnp.full_like(part, 0) + jnp.asarray(zero, part.dtype), value, neutral
    )

    def step(position, subtotal):
        longer = join(subtotal, jax.tree.map(lambda part: part[position], pieces))
        return jax.tree.map(lambda new, old: jnp.where(position < mine, new, old), longer, subtotal)

    return lax.fori_loop(0, count - 1, step, subtotal)


def normalize(inputs, gain):
    centered = inputs - jnp.mean(inputs, axis=-1, keepdims=True)
    scaled = centered * lax.rsqrt(jnp.mean(centered * centered, axis=-1, keepdims=True) + eps)
    return scaled * gain


def project(left, right):
    return jnp.einsum(
        "btd,df->btf", left, right, precision=precise, preferred_element_type=jnp.float32
    )


def outer_sum(left, right):
    return jnp.einsum(
        "btd,btf->df", left, right, precision=precise, preferred_element_type=jnp.float32
    )


def smooth_gate(inputs):
    return jax.nn.gelu(inputs, approximate=True)


def shift_keys(extended, kernel, seg_ext):
    taps = kernel.shape[0]
    length = extended.shape[1] - taps + 1
    current = seg_ext[:, taps - 1 :]
    summed = jnp.zeros((extended.shape[0], length, extended.shape[2]), jnp.float32)
    for offset in range(taps):
        begin = taps - 1 - offset
        joined = (seg_ext[:, begin : begin + length] == current).astype(jnp.float32)
        summed = summed + kernel[offset] * extended[:, begin : begin + length] * joined[:, :, None]
    return summed


def compose(earlier, later):
    return (earlier[0] * later[0], later[0][..., None] * earlier[1] + later[1])


def geometry(segments, before_block, log_decay):
    rows, length = segments.shape
    pieces = length // SUBBLOCK
    grouped = segments.reshape(rows, pieces, SUBBLOCK)
    before = jnp.concatenate([before_block[:, None], grouped[:, :-1, -1]], axis=1)
    living = (grouped == before[:, :, None]).astype(jnp.float32)
    retained = (grouped == grouped[:, :, -1:]).astype(jnp.float32)
    position = jnp.arange(SUBBLOCK, dtype=jnp.float32)
    causal = position[:, None] >= position[None, :]
    allowed = jnp.logical_and(grouped[:, :, :, None] == grouped[:, :, None, :], causal).astype(
        jnp.float32
    )
    growing = jnp.exp(position[:, None, None] * log_decay)
    shrinking = jnp.exp(-position[:, None, None] * log_decay)
    step_in = growing * jnp.exp(log_decay)
    closing = jnp.exp((SUBBLOCK - 1.0 - position)[:, None, None] * log_decay)
    whole_decay = jnp.exp(SUBBLOCK * log_decay)[None, None] * living[:, :, -1][:, :, None, None]
    running = jnp.ones((rows,) + log_decay.shape, jnp.float32)
    carried = []
    for index in range(pieces):
        carried.append(running)
        running = running * whole_decay[:, index]
    return (
        living,
        retained,
        allowed,
        growing,
        shrinking,
        step_in,
        closing,
        whole_decay,
        jnp.stack(carried, axis=1),
        running,
    )


def local_part(queries, shifted, values, shape_info):
    (
        living,
        retained,
        allowed,
        growing,
        shrinking,
        step_in,
        closing,
        whole_decay,
        carried,
        block_decay,
    ) = shape_info
    scores = jnp.einsum(
        "bncgi,bnsgi->bngcs", queries * growing, shifted * shrinking, precision=precise
    )
    scores = scores * allowed[:, :, None]
    within = jnp.einsum("bngcs,bnsgj->bncgj", scores, values, precision=precise)
    update = jnp.einsum(
        "bncgi,bncgj->bngij",
        shifted * closing * retained[..., None, None],
        values,
        precision=precise,
    )
    running = jnp.zeros_like(update[:, 0])
    starts = []
    for index in range(update.shape[1]):
        starts.append(running)
        running = whole_decay[:, index][..., None] * running + update[:, index]
    return (within, jnp.stack(starts, axis=1), running)


def across(queries, starts, state_in, shape_info):
    (
        living,
        retained,
        allowed,
        growing,
        shrinking,
        step_in,
        closing,
        whole_decay,
        carried,
        block_decay,
    ) = shape_info
    entries = starts + carried[..., None] * state_in[:, None]
    weighted = queries * step_in * living[..., None, None]
    return jnp.einsum("bncgi,bngij->bncgj", weighted, entries, precision=precise)


def on_device(
    layer_input,
    segment_ids,
    mixer_gain,
    query_weight,
    key_weight,
    value_weight,
    shift_kernel,
    state_decay,
    mixer_weight,
    feed_gain,
    up_weight,
    down_weight,
    cotangent,
):
    (
        mixer_gain_all,
        query_all,
        key_all,
        value_all,
        kernel_all,
        mixer_all,
        feed_gain_all,
        up_all,
        down_all,
    ) = (
        lax.all_gather(mixer_gain, ("dp", "ctx"), axis=0, tiled=True),
        lax.all_gather(query_weight, ("dp", "ctx"), axis=0, tiled=True),
        lax.all_gather(key_weight, ("dp", "ctx"), axis=0, tiled=True),
        lax.all_gather(value_weight, ("dp", "ctx"), axis=0, tiled=True),
        lax.all_gather(shift_kernel, ("dp", "ctx"), axis=1, tiled=True),
        lax.all_gather(mixer_weight, ("dp", "ctx"), axis=1, tiled=True),
        lax.all_gather(feed_gain, ("dp", "ctx"), axis=0, tiled=True),
        lax.all_gather(up_weight, ("dp", "ctx"), axis=0, tiled=True),
        lax.all_gather(down_weight, ("dp", "ctx"), axis=1, tiled=True),
    )
    heads, width = state_decay.shape
    log_decay = jnp.log(state_decay)
    taps = kernel_all.shape[0]
    rows, length, model = layer_input.shape
    pieces = length // SUBBLOCK
    features = heads * width
    seg_float = segment_ids.astype(jnp.float32)
    joint_weight = jnp.concatenate([query_all, key_all, value_all], axis=1)
    normed = normalize(layer_input, mixer_gain_all)
    projected = project(normed, joint_weight)
    queries = projected[:, :, :features]
    keys_raw = projected[:, :, features : 2 * features]
    values = projected[:, :, 2 * features :]
    tail_keys, tail_segs = passed_along(
        (keys_raw[:, length - taps + 1 :], seg_float[:, length - taps + 1 :]), "ctx", 1
    )
    extended = jnp.concatenate([tail_keys, keys_raw], axis=1)
    seg_ext = jnp.concatenate([tail_segs, seg_float], axis=1)
    shift_fixed = partial(shift_keys, seg_ext=seg_ext)
    shifted = shift_fixed(extended, kernel_all)
    info = geometry(seg_float, tail_segs[:, -1], log_decay)
    block_decay = info[-1]
    head_q = queries.reshape(rows, pieces, SUBBLOCK, heads, width)
    head_k = shifted.reshape(rows, pieces, SUBBLOCK, heads, width)
    head_v = values.reshape(rows, pieces, SUBBLOCK, heads, width)
    within, starts, local_end = local_part(head_q, head_k, head_v, info)
    identity = (jnp.ones_like(block_decay), jnp.zeros_like(local_end))
    state_in = carried_in((block_decay, local_end), "ctx", compose, identity, False)[1]
    mixed = (within + across(head_q, starts, state_in, info)).reshape(rows, length, features)
    branch = lax.psum(project(mixed, mixer_all), "tensor")
    resid = layer_input + branch
    normed_feed = normalize(resid, feed_gain_all)
    pre_act = project(normed_feed, up_all)
    activated, gelu_back = jax.vjp(smooth_gate, pre_act)
    feed = lax.psum(project(activated, down_all), "tensor")
    layer_output = resid + feed
    act_grad = project(cotangent, down_all.T)
    down_grad = outer_sum(activated, cotangent)
    (pre_grad,) = gelu_back(act_grad)
    up_grad = outer_sum(normed_feed, pre_grad)
    feed_normed_grad = lax.psum(project(pre_grad, up_all.T), "tensor")
    _, feed_norm_back = jax.vjp(normalize, resid, feed_gain_all)
    resid_ln_grad, feed_gain_grad = feed_norm_back(feed_normed_grad)
    resid_grad = cotangent + resid_ln_grad
    mixed_grad = project(resid_grad, mixer_all.T)
    mixer_weight_grad = outer_sum(mixed, resid_grad)
    head_du = mixed_grad.reshape(rows, pieces, SUBBLOCK, heads, width)
    (
        living,
        retained,
        allowed,
        growing,
        shrinking,
        step_in,
        closing,
        whole_decay,
        carried,
        block_decay,
    ) = info
    own_grad = jnp.einsum(
        "bncgi,bncgj,bngi->bgij",
        head_q * step_in * living[..., None, None],
        head_du,
        carried,
        precision=precise,
    )
    identity_grad = (jnp.ones_like(block_decay), jnp.zeros_like(own_grad))
    after = carried_in((block_decay, own_grad), "ctx", compose, identity_grad, True)[1]

    def mixer_full(query_in, key_in, value_in, entering):
        inner, begins, ending = local_part(query_in, key_in, value_in, info)
        output = inner + across(query_in, begins, entering, info)
        return (output, ending + block_decay[..., None] * entering)

    _, mixer_vjp = jax.vjp(mixer_full, head_q, head_k, head_v, state_in)
    query_act_grad, shifted_grad, value_act_grad, _ = mixer_vjp((head_du, after))
    _, shift_back = jax.vjp(shift_fixed, extended, kernel_all)
    ext_grad, kernel_grad = shift_back(shifted_grad.reshape(rows, length, features))
    returned = passed_along(ext_grad[:, : taps - 1], "ctx", -1)
    key_act_grad = ext_grad[:, taps - 1 :] + jnp.pad(
        returned, ((0, 0), (length - taps + 1, 0), (0, 0))
    )
    joint_grad = jnp.concatenate(
        [
            query_act_grad.reshape(rows, length, features),
            key_act_grad,
            value_act_grad.reshape(rows, length, features),
        ],
        axis=2,
    )
    joint_weight_grad = outer_sum(normed, joint_grad)
    normed_grad = lax.psum(project(joint_grad, joint_weight.T), "tensor")
    _, mixer_norm_back = jax.vjp(normalize, layer_input, mixer_gain_all)
    input_ln_grad, mixer_gain_grad = mixer_norm_back(normed_grad)
    input_grad = resid_grad + input_ln_grad
    query_grad = joint_weight_grad[:, :features]
    key_grad = joint_weight_grad[:, features : 2 * features]
    value_grad = joint_weight_grad[:, 2 * features :]
    all_parts = tuple(
        (
            lax.psum_scatter(mixer_gain_grad, ("dp", "ctx"), scatter_dimension=0, tiled=True),
            lax.psum_scatter(query_grad, ("dp", "ctx"), scatter_dimension=0, tiled=True),
            lax.psum_scatter(key_grad, ("dp", "ctx"), scatter_dimension=0, tiled=True),
            lax.psum_scatter(value_grad, ("dp", "ctx"), scatter_dimension=0, tiled=True),
            lax.psum_scatter(kernel_grad, ("dp", "ctx"), scatter_dimension=1, tiled=True),
            lax.psum_scatter(mixer_weight_grad, ("dp", "ctx"), scatter_dimension=1, tiled=True),
            lax.psum_scatter(feed_gain_grad, ("dp", "ctx"), scatter_dimension=0, tiled=True),
            lax.psum_scatter(up_grad, ("dp", "ctx"), scatter_dimension=0, tiled=True),
            lax.psum_scatter(down_grad, ("dp", "ctx"), scatter_dimension=1, tiled=True),
        )
    )
    return (layer_output, input_grad) + all_parts


PAIR = 2
BLOCK = 128
LANES = 128
LIMIT = 60
TILE = 256
C_GELU = 0.7978845608028654
NN = ((1,), (0,))
NT = ((1,), (1,))
TN = ((0,), (0,))
f32, bf16 = jnp.float32, jnp.bfloat16


def params(limit=LIMIT):
    return pltpu.CompilerParams(vmem_limit_bytes=limit * 2**20)


def cost(flops, moved):
    return pl.CostEstimate(flops=int(flops), bytes_accessed=int(moved), transcendentals=0)


def shaped(shape, dtype=jnp.float32):
    return jax.ShapeDtypeStruct(shape, dtype)


def split(a):
    high = a.astype(bf16)
    return high, (a - high.astype(f32)).astype(bf16)


def d3(left, right, dims):
    dot = partial(lax.dot_general, dimension_numbers=(dims, ((), ())), preferred_element_type=f32)
    return dot(left[0], right[0]) + dot(left[1], right[0]) + dot(left[0], right[1])


def d3_low(left, right, dims):
    dot = partial(lax.dot_general, dimension_numbers=(dims, ((), ())), preferred_element_type=f32)
    rows = left[0].shape[0]
    both = dot(jnp.concatenate(left, axis=0), right[0])
    return both[:rows] + both[rows:] + dot(left[0], right[1])


def tied(arrays):
    specs = [
        pl.BlockSpec((1,) * (a.ndim - 2) + (8, 128), lambda *_, n=a.ndim: (0,) * n) for a in arrays
    ]
    return specs, list(arrays)


def norm_parts(v):
    centered = v - jnp.mean(v, axis=-1, keepdims=True)
    r = lax.rsqrt(jnp.mean(centered * centered, axis=-1, keepdims=True) + eps)
    return centered * r, r


def whole(shape):
    return pl.BlockSpec(
        shape, lambda *_: (0,) * len(shape), pipeline_mode=pl.Buffered(buffer_count=1)
    )


def scalar():
    return pl.BlockSpec(memory_space=pltpu.SMEM)


def pack_mixer_kernel(me_ref, q_ref, k_ref, v_ref, m_ref, mg_ref, fg_ref, kern_ref, decay_ref, o_ref):
    rows, own = q_ref.shape
    taps, few = kern_ref.shape
    heads, width = decay_ref.shape
    o_ref[0:rows, 0:own] = q_ref[...]
    o_ref[0:rows, own : 2 * own] = k_ref[...]
    o_ref[0:rows, 2 * own : 3 * own] = v_ref[...]
    o_ref[0:rows, 3 * own :] = jnp.transpose(m_ref[...])
    o_ref[rows:, :] = jnp.zeros((8, o_ref.shape[1]), f32)
    for b in range(8):

        @pl.when(me_ref[0] == b)
        def _():
            o_ref[rows : rows + 1, b * rows : (b + 1) * rows] = mg_ref[...]
            o_ref[rows + 1 : rows + 2, b * rows : (b + 1) * rows] = fg_ref[...]
            o_ref[rows + 2 : rows + 2 + taps, b * few : (b + 1) * few] = kern_ref[...]

    @pl.when(me_ref[0] == 0)
    def _():
        for h in range(heads):
            at = rows + 2 + taps
            o_ref[at : at + 1, h * width : (h + 1) * width] = decay_ref[h : h + 1, :]


def run_pack_mixer(me, q, k, v, m, mg, fg, kern, decay):
    rows, own = q.shape
    args = (q, k, v, m, mg[None], fg[None], kern, decay)
    return pl.pallas_call(
        pack_mixer_kernel,
        grid=(1,),
        in_specs=[scalar()] + [whole(a.shape) for a in args],
        out_specs=whole((rows + 8, 4 * own)),
        out_shape=shaped((rows + 8, 4 * own)),
        compiler_params=params(),
        cost_estimate=cost(1e6, 2**20),
        name="pack_mixer",
    )(me, *args)


def pack_feed_kernel(up_ref, down_ref, o_ref):
    hidden = up_ref.shape[1]
    o_ref[:, :hidden] = up_ref[...]
    o_ref[:, hidden:] = jnp.transpose(down_ref[...])


def run_pack_feed(up, down):
    return pl.pallas_call(
        pack_feed_kernel,
        grid=(1,),
        in_specs=[whole(up.shape), whole(down.shape)],
        out_specs=whole((up.shape[0], 2 * up.shape[1])),
        out_shape=shaped((up.shape[0], 2 * up.shape[1])),
        compiler_params=params(),
        cost_estimate=cost(1e6, 2 * 2**20),
        name="pack_feed",
    )(up, down)


def sequence_specs(model, order):
    def mine(i, m):
        return (m[0] & 1, order(i, m) % 2, 0)

    return [pl.BlockSpec((1, TILE, model), mine)] * 2


def sequence_tile(tile, me_ref, mine_ref, came_ref):
    own = tile // 2 == (me_ref[0] & 1)
    return jnp.where(own, mine_ref[0], came_ref[0])


def project_kernel(me_ref, x_ref, xr_ref, *refs):
    first, second = refs[0:8], refs[8:16]
    o_ref, wh_ref, wl_ref, mh_ref, ml_ref, gains_ref, small_ref = refs[-7:]
    own = first[0].shape[1] // 4
    rows = wh_ref.shape[0] // 8

    @pl.when(pl.program_id(0) == 0)
    def _():
        for r in range(8):
            at = pl.ds(pl.multiple_of((me_ref[0] ^ r) * rows, rows), rows)
            a, b = first[r][0:rows, :], second[r][0:rows, :]
            for i in range(4):
                both = jnp.concatenate(
                    [a[:, i * own : (i + 1) * own], b[:, i * own : (i + 1) * own]], axis=1
                )
                high, low = split(both)
                if i < 3:
                    wh_ref[at, i * 2 * own : (i + 1) * 2 * own] = high
                    wl_ref[at, i * 2 * own : (i + 1) * 2 * own] = low
                else:
                    mh_ref[at, :] = high
                    ml_ref[at, :] = low
        sums = []
        for pieces in (first, second):
            total = pieces[0][rows:, :]
            for r in range(1, 8):
                total = total + pieces[r][rows:, :]
            sums.append(total)
        gains_ref[...] = sums[0]
        small_ref[...] = jnp.concatenate([s[:, :own] for s in sums], axis=1)

    x = sequence_tile(pl.program_id(0), me_ref, x_ref, xr_ref)
    n = split(norm_parts(x)[0] * gains_ref[0:1, :])
    o_ref[...] = d3(n, (wh_ref[...], wl_ref[...]), NN)


def run_project(me, x, first, second, ties=()):
    rows, half, model = x[0].shape
    tokens = rows * half
    own = first[0].shape[1] // 4
    wide = 6 * own
    piece = whole(first[0].shape)
    weights = [(model, wide)] * 2 + [(model, 2 * own)] * 2
    few = [(8, model), (8, 2 * own)]
    tie_specs, tie_args = tied(ties)
    return pl.pallas_call(
        project_kernel,
        grid_spec=pltpu.PrefetchScalarGridSpec(
            num_scalar_prefetch=1,
            grid=(tokens // TILE,),
            in_specs=sequence_specs(model, lambda i, m: i) + [piece] * 16 + tie_specs,
            out_specs=[pl.BlockSpec((TILE, wide), lambda i, m: (i, 0))]
            + [whole(s) for s in weights + few],
        ),
        out_shape=[shaped((tokens, wide))]
        + [shaped(s, bf16) for s in weights]
        + [shaped(s) for s in few],
        compiler_params=params(),
        cost_estimate=cost(6 * tokens * model * wide, 20 * 2**20),
        name="project",
    )(me, *x, *first, *second, *tie_args)


def spread(parts, masks):
    return tuple(jnp.concatenate([p * m for m in masks], axis=0) for p in parts)


def lane_masks(lanes):
    which = lax.broadcasted_iota(jnp.int32, (1, lanes), 1) // (lanes // PAIR)
    return [jnp.where(which == h, 1.0, 0.0).astype(bf16) for h in range(PAIR)]


def square_mask(lanes):
    a = lax.broadcasted_iota(jnp.int32, (lanes, lanes), 0) // (lanes // PAIR)
    b = lax.broadcasted_iota(jnp.int32, (lanes, lanes), 1) // (lanes // PAIR)
    return jnp.where(a == b, 1.0, 0.0)


def fill_tables(decay, grow, shrink, dec, end, full):
    size, model = grow.shape
    lanes = dec.shape[0]
    rates = jnp.log(decay)
    position = lax.broadcasted_iota(jnp.int32, (size, model), 0).astype(f32)
    grow[...] = jnp.exp(position * rates)
    shrink[...] = jnp.exp(-position * rates)
    for p in range(model // lanes):
        s = slice(p * lanes, (p + 1) * lanes)
        column = jnp.transpose(jnp.broadcast_to(rates[:, s], (lanes, lanes)))
        dec[:, s] = jnp.exp(column)
        end[:, s] = jnp.exp((size - 1.0) * column)
        full[:, s] = jnp.exp(float(size) * column)


def joined(extended, size, taps):
    now = extended[8:]
    return [jnp.where(extended[8 - j : 8 - j + size] == now, 1.0, 0.0) for j in range(1, taps)]


def shift_forward(keys, before, kern, same, taps):
    extended = jnp.concatenate([before, keys], axis=0)
    size = keys.shape[0]
    moved = [keys]
    for j in range(1, taps):
        moved.append(extended[8 - j : 8 - j + size] * same[j - 1])
    total = kern[0:1, :] * keys
    for j in range(1, taps):
        total = total + kern[j : j + 1, :] * moved[j]
    return total, moved


def allowed_masks(seg, row):
    size, wide = seg.shape[0], row.shape[1]
    rows = lax.broadcasted_iota(jnp.int32, (size, wide), 0)
    cols = lax.broadcasted_iota(jnp.int32, (size, wide), 1) % size
    same = seg == row
    return (
        jnp.where(jnp.logical_and(rows >= cols, same), 1.0, 0.0),
        jnp.where(jnp.logical_and(rows <= cols, same), 1.0, 0.0),
    )


def pair(a_ref, b_ref):
    return jnp.concatenate([a_ref[...], b_ref[...]], axis=1)


def third_of(refs, rows, i):
    wide = refs[0].shape[1] // 3
    return jnp.concatenate([r[rows, i * wide : (i + 1) * wide] for r in refs], axis=1)


def mixer_kernel(taps, last, me_ref, proj_ref, seg_ref, segrow_ref, small_ref, *refs):
    if last:
        x_ref, xr_ref, other_ref, gains_ref, ah_ref, al_ref, bh_ref, bl_ref = refs[:8]
        state_out_ref, resid_ref, nh_ref, nl_ref = refs[8:12]
    else:
        state_out_ref, mixed_ref = refs[:2]
    state, tail, segtail, grow, shrink, dec, end, full, mixed = refs[-9:]
    size, lanes = grow.shape[0], dec.shape[0]
    projs = (proj_ref,)

    @pl.when(pl.program_id(0) == 0)
    def _():
        state[...] = jnp.zeros_like(state)
        tail[...] = jnp.zeros_like(tail)
        segtail[...] = jnp.full_like(segtail, -1.0)
        fill_tables(small_ref[2 + taps : 3 + taps], grow, shrink, dec, end, full)

    kern = small_ref[2 : 2 + taps]
    masks = lane_masks(lanes)
    square = square_mask(lanes)
    groups = [slice(g * lanes, (g + 1) * lanes) for g in range(state.shape[1] // lanes)]
    before_keys, before = tail[...], segtail[...]
    for chunk in range(proj_ref.shape[0] // size):
        here = slice(chunk * size, (chunk + 1) * size)
        seg = seg_ref[here, :]
        extended = jnp.concatenate([before, seg], axis=0)
        living = jnp.where(seg == before[7:8], 1.0, 0.0)
        kept = jnp.where(seg == seg[size - 1 :], 1.0, 0.0)
        goes_on = living[size - 1 :]
        q_all, keys, v_all = (third_of(projs, here, i) for i in range(3))
        shifted, _ = shift_forward(keys, before_keys, kern, joined(extended, size, taps), taps)
        before_keys, before = keys[size - 8 :, :], seg[size - 8 :]
        allowed, _ = allowed_masks(seg, segrow_ref[chunk])
        state_out_ref[chunk] = state[...]
        qg, kf, v, scores = [], [], [], []
        for s in groups:
            qg.append(split(q_all[:, s] * grow[:, s]))
            kf.append(shifted[:, s] * shrink[:, s])
            v.append(split(v_all[:, s]))
            scores.append(d3_low(qg[-1], spread(split(kf[-1]), masks), NT))
        updates = [d3(split(k * kept), w, TN) * square for k, w in zip(kf, v)]
        weights = [split(score * allowed) for score in scores]
        for g, s in enumerate(groups):
            part = d3_low(weights[g], spread(v[g], masks), NN)
            mixed[here, s] = part + living * d3_low(qg[g], split(state[:, s] * dec[:, s]), NN)
        for g, s in enumerate(groups):
            state[:, s] = state[:, s] * (full[:, s] * goes_on) + end[:, s] * updates[g]
    tail[...] = before_keys
    segtail[...] = before
    if not last:
        mixed_ref[...] = mixed[...]
        return
    resid = (
        sequence_tile(pl.program_id(0), me_ref, x_ref, xr_ref)
        + d3(split(other_ref[...]), (ah_ref[...], al_ref[...]), NT)
        + d3(split(mixed[...]), (bh_ref[...], bl_ref[...]), NT)
    )
    resid_ref[...] = resid
    nh_ref[...], nl_ref[...] = split(norm_parts(resid)[0] * gains_ref[1:2, :])


def mixer_scratch(model):
    return [pltpu.VMEM((BLOCK, model), f32)] * 2 + [pltpu.VMEM((LANES, model), f32)] * 3


def run_mixer(me, proj, seg, segrow, small, taps, more=(), ties=()):
    tokens, third = proj.shape[0], proj.shape[1] // 3
    chunks = TILE // BLOCK

    def row(width):
        return pl.BlockSpec((TILE, width), lambda c, m: (c, 0))

    extra_specs, extra = [], []
    outs = [(row(third), shaped((tokens, third)))]
    if more:
        x, other, gains, a, b = more
        model = x[0].shape[2]
        extra_specs = sequence_specs(model, lambda i, m: i) + [row(third), whole(gains.shape)]
        extra_specs = extra_specs + [whole(a[0].shape)] * 4
        extra = [*x, other, gains, *a, *b]
        outs = [(row(model), shaped((tokens, model), t)) for t in (f32, bf16, bf16)]
    states = pl.BlockSpec((chunks, LANES, third), lambda c, m: (c, 0, 0))
    tie_specs, tie_args = tied(ties)
    return pl.pallas_call(
        partial(mixer_kernel, taps, bool(more)),
        grid_spec=pltpu.PrefetchScalarGridSpec(
            num_scalar_prefetch=1,
            grid=(tokens // TILE,),
            in_specs=[
                row(3 * third),
                row(1),
                pl.BlockSpec((chunks, 1, segrow.shape[2]), lambda c, m: (c, 0, 0)),
                whole(small.shape),
            ]
            + extra_specs
            + tie_specs,
            out_specs=[states] + [spec for spec, _ in outs],
            scratch_shapes=[
                pltpu.VMEM((LANES, third), f32),
                pltpu.VMEM((8, third), f32),
                pltpu.VMEM((8, 1), f32),
            ]
            + mixer_scratch(third)
            + [pltpu.VMEM((TILE, third), f32)],
        ),
        out_shape=[shaped((tokens // BLOCK, LANES, third))] + [shape for _, shape in outs],
        compiler_params=params(),
        cost_estimate=cost(6e9 + (7e9 if more else 0), 10 * 2**20),
        name="mixer_out" if more else "mixer",
    )(me, proj, seg, segrow, small, *extra, *tie_args)


def mixer_back_kernel(
    taps, me_ref, fng_ref, resid_ref, x_ref, xr_ref, ct_ref, cr_ref, pa_ref, pb_ref, ba_ref, bb_ref,
    ta_ref, tb_ref, mixed_ref, seg_ref, segb_ref, segrow_ref, sa_ref, sb_ref, gains_ref,
    ah_ref, al_ref, bh_ref, bl_ref, qah_ref, qal_ref, qbh_ref, qbl_ref, *refs,
):
    (
        theirs_ref, ig_ref, keep_ref, send_ref, gg, g2, dkern,
        grad, head, grow, shrink, dec, end, full, du_all, da, db, wg,
    ) = refs[-18:]
    size, lanes = grow.shape[0], dec.shape[0]
    step, steps = pl.program_id(0), pl.num_programs(0)
    projs = (pa_ref, pb_ref)

    @pl.when(step == 0)
    def _():
        grad[...] = jnp.zeros_like(grad)
        head[...] = jnp.zeros_like(head)
        dkern[...] = jnp.zeros_like(dkern)
        gg[...] = jnp.zeros_like(gg)
        g2[...] = jnp.zeros_like(g2)
        wg[...] = jnp.zeros_like(wg)
        fill_tables(pair(sa_ref, sb_ref)[2 + taps : 3 + taps], grow, shrink, dec, end, full)

    third = ah_ref.shape[1]
    tile = steps - 1 - step
    back, gain_grad, _ = norm_back(resid_ref[...], gains_ref[1:2, :], fng_ref[...])
    rg = sequence_tile(tile, me_ref, ct_ref, cr_ref) + back
    g2[...] += gain_grad
    r2 = split(rg)
    du_all[:, :third] = d3(r2, (ah_ref[...], al_ref[...]), NN)
    du_all[:, third:] = d3(r2, (bh_ref[...], bl_ref[...]), NN)

    kern = pair(sa_ref, sb_ref)[2 : 2 + taps]
    masks = lane_masks(lanes)
    square = square_mask(lanes)
    model = grad.shape[1]
    groups = [slice(g * lanes, (g + 1) * lanes) for g in range(model // lanes)]
    count = len(groups)
    chunks = rg.shape[0] // size
    for chunk in reversed(range(chunks)):
        here = slice(chunk * size, (chunk + 1) * size)
        seg = seg_ref[here, :]
        q_all, keys, v_all = (third_of(projs, here, i) for i in range(3))
        if chunk:
            just = slice(chunk * size - 8, chunk * size)
            before, before_keys = seg_ref[just, :], third_of(projs, just, 1)
        else:
            before = jnp.where(step == steps - 1, -1.0, segb_ref[...])
            before_keys = pair(ba_ref, bb_ref)
        extended = jnp.concatenate([before, seg], axis=0)
        living = jnp.where(seg == before[7:8], 1.0, 0.0)
        kept = jnp.where(seg == seg[size - 1 :], 1.0, 0.0)
        goes_on = living[size - 1 :]
        same = joined(extended, size, taps)
        shifted, moved = shift_forward(keys, before_keys, kern, same, taps)
        allowed, allowed_t = allowed_masks(seg, segrow_ref[chunk])
        qf = [q_all[:, s] * grow[:, s] for s in groups]
        qg = [split(q) for q in qf]
        kg = [split(shifted[:, s] * shrink[:, s]) for s in groups]
        v = [split(v_all[:, s]) for s in groups]
        du = [split(du_all[here, s]) for s in groups]
        p_t = [d3_low(kg[g], spread(qg[g], masks), NT) for g in range(count)]
        dp = [d3_low(du[g], spread(v[g], masks), NT) for g in range(count)]
        dp_t = [d3_low(v[g], spread(du[g], masks), NT) for g in range(count)]
        updates = [d3(split(qf[g] * living), du[g], TN) * square for g in range(count)]
        p_t = [split(p * allowed_t) for p in p_t]
        dp = [split(p * allowed) for p in dp]
        dp_t = [split(p * allowed_t) for p in dp_t]
        for g, s in enumerate(groups):
            first = s.start < third
            at = s.start - (0 if first else third)
            to = da if first else db
            states = (ta_ref if first else tb_ref)[chunk, :, at : at + lanes]
            entering = split(states * dec[:, s])
            leaving = split(grad[:, s] * end[:, s])
            dqg = d3_low(dp[g], spread(kg[g], masks), NN) + living * d3_low(du[g], entering, NT)
            dkg = d3_low(dp_t[g], spread(qg[g], masks), NN) + kept * d3_low(v[g], leaving, NT)
            dv = d3_low(p_t[g], spread(du[g], masks), NN) + kept * d3_low(kg[g], leaving, NN)
            to[here, 2 * third + at : 2 * third + at + lanes] = dv
            to[here, at : at + lanes] = dqg * grow[:, s]
            dshift = dkg * shrink[:, s]
            grad[:, s] = grad[:, s] * (full[:, s] * goes_on) + dec[:, s] * updates[g]
            total = kern[0:1, s] * dshift
            for j in range(1, taps):
                part = dshift * same[j - 1]
                longer = jnp.concatenate([part, head[j - 1, :, s]], axis=0)
                total = total + kern[j : j + 1, s] * longer[j : j + size]
                head[j - 1, :, s] = part[0:8]
            to[here, third + at : third + at + lanes] = total
            if g < 2:
                for j in range(taps):
                    dkern[j : j + 1, s] += jnp.sum(
                        dshift * moved[j][:, s], axis=0, keepdims=True
                    )

    own = keep_ref.shape[-1] // 4
    x = sequence_tile(tile, me_ref, x_ref, xr_ref)
    left, right = split(da[...]), split(db[...])
    incoming = d3(left, (qah_ref[...], qal_ref[...]), NT)
    incoming = incoming + d3(right, (qbh_ref[...], qbl_ref[...]), NT)
    back, gain_grad, xhat = norm_back(x, gains_ref[0:1, :], incoming)
    ig_ref[0] = rg + back
    gg[...] += gain_grad
    n = split(xhat * gains_ref[0:1, :])
    joint = tuple(
        jnp.concatenate([p[:, i * third : i * third + own] for i in range(3)], axis=1) for p in left
    )
    wg[:, : 3 * own] += d3(n, joint, TN)
    wg[:, 3 * own :] += d3(r2, split(mixed_ref[:, :own]), TN)

    @pl.when(tile // 2 != (me_ref[0] & 1))
    def _():
        theirs_ref[...] = ig_ref[0]

    @pl.when(step == steps - 1)
    def _():
        few = (gg[...], g2[...], dkern[:, :own])
        store_blocks(me_ref[0], wg, few, keep_ref, send_ref)


def run_mixer_back(
    me, fng, resid, x, ct, projs, states, mixed, seg, segrow, smalls, gains, a, b, qa, qb, taps
):
    tokens, model = resid.shape
    third = projs[0].shape[1] // 3
    own = third // 2
    chunks = TILE // BLOCK
    last = tokens // TILE - 1
    blocks = (1, 4, model // 8 + 8, 4 * own)

    def prior(c):
        return jnp.maximum((last - c) * (TILE // 8) - 1, 0)

    row = pl.BlockSpec((TILE, model), lambda c, m: (last - c, 0))
    proj = pl.BlockSpec((TILE, 3 * third), lambda c, m: (last - c, 0))
    before = pl.BlockSpec((8, third), lambda c, m: (prior(c), 1))
    state = pl.BlockSpec((chunks, LANES, third), lambda c, m: (last - c, 0, 0))
    halves = pl.BlockSpec((1, TILE, model), lambda c, m: ((last - c) // 2, (last - c) % 2, 0))

    def for_other(c, m):
        core, tile = m[0] & 1, last - c
        return (jnp.where(tile // 2 == 1 - core, tile % 2, core), 0)

    theirs = pl.BlockSpec((TILE, model), for_other)
    return pl.pallas_call(
        partial(mixer_back_kernel, taps),
        grid_spec=pltpu.PrefetchScalarGridSpec(
            num_scalar_prefetch=1,
            grid=(last + 1,),
            in_specs=[row, row]
            + sequence_specs(model, lambda c, m: last - c) * 2
            + [proj, proj, before, before, state, state]
            + [
                pl.BlockSpec((TILE, third), lambda c, m: (last - c, 0)),
                pl.BlockSpec((TILE, 1), lambda c, m: (last - c, 0)),
                pl.BlockSpec((8, 1), lambda c, m: (prior(c), 0)),
                pl.BlockSpec((chunks, 1, segrow.shape[2]), lambda c, m: (last - c, 0, 0)),
                whole(smalls[0].shape),
                whole(smalls[1].shape),
                whole(gains.shape),
            ]
            + [whole(a[0].shape)] * 4
            + [whole(qa[0].shape)] * 4,
            out_specs=[theirs, halves, whole(blocks), whole(blocks)],
            scratch_shapes=[
                pltpu.VMEM((1, model), f32),
                pltpu.VMEM((1, model), f32),
                pltpu.VMEM((taps, model), f32),
                pltpu.VMEM((LANES, model), f32),
                pltpu.VMEM((taps - 1, 8, model), f32),
            ]
            + mixer_scratch(model)
            + [pltpu.VMEM((TILE, model), f32)]
            + [pltpu.VMEM((TILE, 3 * third), f32)] * 2
            + [pltpu.VMEM((model, 4 * own), f32)],
        ),
        out_shape=[shaped((tokens // 2, model)), shaped((2, tokens // 2, model))]
        + [shaped(blocks), shaped(blocks)],
        compiler_params=params(),
        cost_estimate=cost(1e11, 60 * 2**20),
        name="mixer_back",
    )(
        me, fng, resid, *x, *ct, *projs, *projs, *states, mixed, seg, seg, segrow, *smalls, gains,
        *a, *b, *qa, *qb,
    )


def gelu_parts(pre, back):
    th = jnp.tanh(pre * (C_GELU + (C_GELU * 0.044715) * (pre * pre)))
    half = 0.5 + 0.5 * th
    act = pre * half
    slope = half + (1.0 - th) * act * (C_GELU + (3 * C_GELU * 0.044715) * (pre * pre))
    return act, back * slope


def store_blocks(me, g, few, keep_ref, send_ref):
    rows = g.shape[0] // 8
    for b in range(8):
        r = me ^ b
        where = r // 2
        short = [f[:, b * (f.shape[1] // 8) : (b + 1) * (f.shape[1] // 8)] for f in few]

        def put(ref):
            ref[0, where, 0:rows, :] = g[b * rows : (b + 1) * rows]
            ref[0, where, rows:, :] = jnp.zeros((ref.shape[2] - rows, ref.shape[3]), f32)
            at = rows
            for part in short:
                ref[0, where, at : at + part.shape[0], 0 : part.shape[1]] = part
                at = at + part.shape[0]

        @pl.when((r & 1) == 0)
        def _():
            put(keep_ref)

        @pl.when((r & 1) == 1)
        def _():
            put(send_ref)


def feed_kernel(own, slots, final, me_ref, nh_ref, nl_ref, ct_ref, cr_ref, out_in, fng_in, w_in, *refs):
    if own:
        out_ref, fng_ref, wg, w = refs[-4:]
    else:
        out_ref, fng_ref, w = refs[-3:]
    step = pl.program_id(0)
    hidden = w.shape[2] // (2 * slots)

    @pl.when(step == 0)
    def _():
        w[0], w[1] = split(w_in[...])
        if own:
            wg[...] = jnp.zeros_like(wg)

    tile = theirs_first(step, me_ref)
    n = (nh_ref[...], nl_ref[...])
    ct = split(sequence_tile(tile, me_ref, ct_ref, cr_ref))
    out, fng = out_in[...], None if own else fng_in[...]
    for t in range(slots):
        a, b = (slice((2 * t + i) * hidden, (2 * t + i + 1) * hidden) for i in range(2))
        u, d = (w[0, :, a], w[1, :, a]), (w[0, :, b], w[1, :, b])
        act, grad = gelu_parts(d3(n, u, NN), d3(ct, d, NN))
        act, grad = split(act), split(grad)
        out = out + d3(act, d, NT)
        more = d3(grad, u, NT)
        fng = more if fng is None else fng + more
    out_ref[...] = out.reshape(out_ref.shape)
    fng_ref[...] = fng
    if own:
        wg[:, :hidden] += d3(n, grad, TN)
        wg[:, hidden:] += d3(ct, act, TN)
    if final:

        @pl.when(step < 2)
        def _():
            refs[0][...] = out_ref[0]


def theirs_first(step, me):
    core = me[0] & 1
    return jnp.where(step < 2, 1 - core, core) * 2 + (step & 1)


def run_feed(me, n, ct, out, fng, w, slots, own, final=False):
    tokens, model = n[0].shape
    wide = w.shape[1]
    row = pl.BlockSpec((TILE, model), lambda i, m: (theirs_first(i, m), 0))
    full = shaped((tokens, model))
    last = pl.BlockSpec((1, TILE, model), lambda i, m: (theirs_first(i, m) // 2, i % 2, 0))
    theirs = pl.BlockSpec((TILE, model), lambda i, m: (jnp.minimum(i, 1), 0))
    return pl.pallas_call(
        partial(feed_kernel, own, slots, final),
        grid_spec=pltpu.PrefetchScalarGridSpec(
            num_scalar_prefetch=1,
            grid=(tokens // TILE,),
            in_specs=[row] * 2
            + sequence_specs(model, theirs_first)
            + [row] * 2
            + [whole(w.shape)],
            out_specs=[theirs] * final
            + [last if final else row, row]
            + ([whole((model, wide))] if own else []),
            scratch_shapes=[pltpu.VMEM((2, model, wide), bf16)],
        ),
        out_shape=[shaped((tokens // 2, model))] * final
        + [shaped((2, tokens // 2, model)) if final else full, full]
        + ([shaped((model, wide))] if own else []),
        compiler_params=params(),
        cost_estimate=cost((6 if own else 4) * 3 * tokens * model * wide, 30 * 2**20),
        name="feed_own" if own else "feed",
    )(me, *n, *ct, out, fng, w)


def norm_back(v, gain, incoming):
    xhat, r = norm_parts(v)
    scaled = incoming * gain
    grad = r * (
        scaled
        - jnp.mean(scaled, axis=-1, keepdims=True)
        - xhat * jnp.mean(scaled * xhat, axis=-1, keepdims=True)
    )
    return grad, jnp.sum(incoming * xhat, axis=0, keepdims=True), xhat


def leave_kernel(me_ref, came_ref, whole_ref, o_ref):
    o_ref[0] = came_ref[...]


def run_leave(me, mine, came):
    half, model = came.shape
    return pl.pallas_call(
        leave_kernel,
        grid_spec=pltpu.PrefetchScalarGridSpec(
            num_scalar_prefetch=1,
            grid=(half // TILE,),
            in_specs=[
                pl.BlockSpec((TILE, model), lambda t, m: (t, 0)),
                pl.BlockSpec(memory_space=pl.ANY),
            ],
            out_specs=pl.BlockSpec((1, TILE, model), lambda t, m: (1 - (m[0] & 1), t, 0)),
        ),
        out_shape=shaped((2, half, model)),
        input_output_aliases={2: 0},
        compiler_params=params(),
        cost_estimate=cost(1e6, 4 * 2**20),
        name="leave",
    )(me, came, mine)


def exchange(value, axis, flip):
    count = lax.axis_size(axis)
    return lax.ppermute(value, axis, [(i, i ^ flip) for i in range(count)])


def corner(value):
    pairs = []
    for d in range(4):
        for c in range(2):
            pairs.append((d * 2 + c, (d ^ (2 if c == 0 else 1)) * 2 + c))
    return lax.ppermute(value, ("dp", "ctx"), pairs)


def after(values, *earlier):
    return lax.optimization_barrier((tuple(values), earlier))[0]


def sides(block):
    return [exchange(block, "dp", 1), exchange(block, "dp", 2), exchange(block, "ctx", 1)]


def far(from_x, from_y):
    return corner(jnp.where(lax.axis_index("ctx") == 0, from_x, from_y))


def across_cores(*values):
    return [exchange(v, "ctx", 1) for v in values]


def by_distance(block, near, near_other, diagonal, diagonal_other):
    from_x, from_y, other = near
    return [
        block, other, from_x, near_other[0], from_y, near_other[1], diagonal, diagonal_other
    ]


def scatter_core(keep, send):
    return keep + exchange(send, "ctx", 1)


def scatter_corner(mine):
    core = lax.axis_index("ctx")
    own, to_x, to_y, to_d = (mine[:, i] for i in range(4))
    came = corner(to_d)
    return (
        own,
        jnp.where(core == 0, to_x + came, to_x),
        jnp.where(core == 0, to_y, to_y + came),
    )


def scatter_sides(own, to_x, to_y):
    return own + exchange(to_x, "dp", 1) + exchange(to_y, "dp", 2)


def swap_in(block):
    me = lax.axis_index("ctx")
    mine = lax.dynamic_index_in_dim(block, me, 0, keepdims=False)
    came = lax.dynamic_index_in_dim(exchange(block, "ctx", 1), me, 0, keepdims=False)
    return jnp.where(
        me == 0, jnp.concatenate([mine, came], axis=0), jnp.concatenate([came, mine], axis=0)
    )


def by_sequence(
    layer_input, segment_ids, mixer_gain, query_weight, key_weight, value_weight, shift_kernel,
    state_decay, mixer_weight, feed_gain, up_weight, down_weight, cotangent,
):
    plane = ("dp", "ctx")
    position = lax.axis_index("dp") * 2 + lax.axis_index("ctx")
    me = position.astype(jnp.int32).reshape(1)
    rows, own = query_weight.shape
    taps, few = shift_kernel.shape

    def gathered(block):
        return lax.all_gather(block, plane, axis=0, tiled=True)

    a0 = run_pack_mixer(
        me, query_weight, key_weight, value_weight, mixer_weight, mixer_gain, feed_gain,
        shift_kernel, state_decay,
    )
    a1 = exchange(a0, "tensor", 1)
    near0 = sides(a0)
    f0 = run_pack_feed(*after((up_weight, down_weight), a0))
    x_came = exchange(after((layer_input,), a0)[0], "ctx", 1)
    seg = swap_in(segment_ids).astype(f32)

    b0, b1, near0 = after((a0, a1, near0), f0)
    a2 = exchange(b0, "tensor", 2)
    far0 = far(*near0[:2])
    near1 = exchange(b1, "dp", 1), exchange(b1, "dp", 2)
    inner = after((*near0[:2], b1), far0)
    other0 = across_cores(*inner[:2], far0)
    other1 = exchange(inner[2], "ctx", 1)

    b0, b2, near1, seg = after((a0, a2, near1, seg), far0, other0, x_came)
    a3 = exchange(b0, "tensor", 3)
    far1 = far(*near1)
    near2 = exchange(b2, "dp", 1), exchange(b2, "dp", 2)
    inner = after((*near1, b2), far1)
    near1 = (*near1, other1)
    other1 = across_cores(*inner[:2], far1)
    other2 = exchange(inner[2], "ctx", 1)

    g0, b3, near2 = after((f0, a3, near2), far1, other1)
    w0 = gathered(g0)
    far2 = far(*near2)
    near3 = exchange(b3, "dp", 1), exchange(b3, "dp", 2)
    f1 = exchange(g0, "tensor", 1)
    f2 = exchange(g0, "tensor", 2)
    first0 = by_distance(a0, near0, other0[:2], far0, other0[2])
    first1 = by_distance(a1, near1, other1[:2], far1, other1[2])
    x = (layer_input, x_came)
    proj_a, *wa = run_project(me, x, first0, first1)
    inner = after((*near2, b3, far2), proj_a, near3)
    near2 = (*near2, other2)
    other2 = across_cores(*inner[:2], inner[3])
    other3 = exchange(inner[2], "ctx", 1)

    near3, late = after((near3, cotangent), far2, proj_a)
    far3 = far(*near3)
    ct = (cotangent, exchange(late, "ctx", 1))
    segrow = jnp.tile(seg.reshape(-1, 1, BLOCK), (1, 1, PAIR))
    seg = seg[:, None]
    states_a, mixed_a = run_mixer(me, proj_a, seg, segrow, wa[5], taps)
    f1, f2, far3, g0 = after((f1, f2, far3, f0), mixed_a)
    w12 = gathered(jnp.concatenate([f1, f2], axis=1))
    inner = after(near3, far3)
    near3 = (*near3, other3)
    other3 = across_cores(*inner, far3)
    first2 = by_distance(a2, near2, other2[:2], far2, other2[2])
    first3 = by_distance(a3, near3, other3[:2], far3, other3[2])
    proj_b, *wb = run_project(me, x, first2, first3)
    (g0,) = after((g0,), proj_b, ct)
    f3 = exchange(g0, "tensor", 3)

    projs, gains, smalls = (proj_a, proj_b), wa[4], (wa[5], wb[5])
    more = (x, mixed_a, gains, wa[2:4], wb[2:4])
    states_b, resid, nh, nl = run_mixer(me, proj_b, seg, segrow, wb[5], taps, more)
    n = (nh, nl)
    out, fng, feed_g = run_feed(me, n, ct, resid, resid, w0, 1, True)
    (f3,) = after((f3,), fng)
    w3 = gathered(f3)
    out, fng = run_feed(me, n, ct, out, fng, w12, 2, False)
    theirs, out_halves, fng = run_feed(me, n, ct, out, fng, w3, 1, False, True)
    feed_g = lax.psum_scatter(feed_g, plane, scatter_dimension=0, tiled=True)
    came = exchange(theirs, "ctx", 1)
    theirs, halves, keep, send = run_mixer_back(
        me, fng, resid, x, ct, projs, (states_a, states_b), mixed_a, seg, segrow, smalls, gains,
        wa[2:4], wb[2:4], wa[:2], wb[:2], taps,
    )
    layer_output = run_leave(me, out_halves, came)
    core = lax.axis_index("ctx")
    came_send = exchange(send, "ctx", 1)
    diagonal = keep[:, 3] + came_send[:, 3]
    keep, came_send = after((keep, came_send), diagonal)
    diagonal = corner(diagonal)
    came = exchange(theirs, "ctx", 1)
    to_own, to_x, to_y = (keep[:, i] + came_send[:, i] for i in range(3))
    diagonal, to_own, to_x, to_y, came = after((diagonal, to_own, to_x, to_y, came))
    came_x = exchange(jnp.where(core == 0, to_x + diagonal, to_x), "dp", 1)
    came_y = exchange(jnp.where(core == 0, to_y, to_y + diagonal), "dp", 2)
    input_grad = run_leave(me, halves, came)
    mixer_g = (to_own + came_x + came_y)[0]
    few_g, mixer_g = mixer_g[rows:], mixer_g[:rows]
    hidden = up_weight.shape[1]
    return (
        layer_output,
        input_grad,
        few_g[0, :rows],
        mixer_g[:, :own],
        mixer_g[:, own : 2 * own],
        mixer_g[:, 2 * own : 3 * own],
        few_g[2 : 2 + taps, :few],
        mixer_g[:, 3 * own :].T,
        few_g[1, :rows],
        feed_g[:, :hidden],
        feed_g[:, hidden:].T,
    )


def solution(mesh):
    shape = mesh.shape

    def chosen(*arrays):
        rows, length, model = arrays[0].shape
        heads, width = arrays[7].shape
        fits = (
            (shape["dp"], shape["ctx"], shape["tensor"]) == (4, 2, 4)
            and (rows, length) == (2, 2 * TILE)
            and PAIR * width == LANES
            and 2 * heads * width % LANES == 0
        )
        return (by_sequence if fits else on_device)(*arrays)

    return jax.shard_map(
        chosen,
        mesh=mesh,
        in_specs=(
            P("dp", "ctx", None),
            P("dp", "ctx"),
            P(("dp", "ctx")),
            P(("dp", "ctx"), "tensor"),
            P(("dp", "ctx"), "tensor"),
            P(("dp", "ctx"), "tensor"),
            P(None, ("tensor", "dp", "ctx")),
            P("tensor", None),
            P("tensor", ("dp", "ctx")),
            P(("dp", "ctx")),
            P(("dp", "ctx"), "tensor"),
            P("tensor", ("dp", "ctx")),
            P("dp", "ctx", None),
        ),
        out_specs=(
            P("dp", "ctx", None),
            P("dp", "ctx", None),
            P(("dp", "ctx")),
            P(("dp", "ctx"), "tensor"),
            P(("dp", "ctx"), "tensor"),
            P(("dp", "ctx"), "tensor"),
            P(None, ("tensor", "dp", "ctx")),
            P("tensor", ("dp", "ctx")),
            P(("dp", "ctx")),
            P(("dp", "ctx"), "tensor"),
            P("tensor", ("dp", "ctx")),
        ),
        check_vma=False,
    )
```

```python
from functools import partial

import jax
import jax.numpy as jnp
from jax import lax
from jax.experimental import pallas as pl
from jax.experimental.pallas import tpu as pltpu
from jax.sharding import PartitionSpec as P

SUBBLOCK = 64


eps = 1e-05
precise = lax.Precision.HIGHEST


def passed_along(value, axis, steps):
    count = lax.axis_size(axis)
    leading, last = (max(0, -steps), min(count, count - steps))
    return lax.ppermute(value, axis, [(source, source + steps) for source in range(leading, last)])


def carried_in(value, axis, join, neutral, backward):
    count, mine = (lax.axis_size(axis), lax.axis_index(axis))
    pieces = jax.tree.map(lambda part: lax.all_gather(part, axis), value)
    if backward:
        pieces = jax.tree.map(lambda part: part[::-1], pieces)
        mine = count - 1 - mine
    subtotal = jax.tree.map(
        lambda part, zero: jnp.full_like(part, 0) + jnp.asarray(zero, part.dtype), value, neutral
    )

    def step(position, subtotal):
        longer = join(subtotal, jax.tree.map(lambda part: part[position], pieces))
        return jax.tree.map(lambda new, old: jnp.where(position < mine, new, old), longer, subtotal)

    return lax.fori_loop(0, count - 1, step, subtotal)


def normalize(inputs, gain):
    centered = inputs - jnp.mean(inputs, axis=-1, keepdims=True)
    scaled = centered * lax.rsqrt(jnp.mean(centered * centered, axis=-1, keepdims=True) + eps)
    return scaled * gain


def project(left, right):
    return jnp.einsum(
        "btd,df->btf", left, right, precision=precise, preferred_element_type=jnp.float32
    )


def outer_sum(left, right):
    return jnp.einsum(
        "btd,btf->df", left, right, precision=precise, preferred_element_type=jnp.float32
    )


def smooth_gate(inputs):
    return jax.nn.gelu(inputs, approximate=True)


def shift_keys(extended, kernel, seg_ext):
    taps = kernel.shape[0]
    length = extended.shape[1] - taps + 1
    current = seg_ext[:, taps - 1 :]
    summed = jnp.zeros((extended.shape[0], length, extended.shape[2]), jnp.float32)
    for offset in range(taps):
        begin = taps - 1 - offset
        joined = (seg_ext[:, begin : begin + length] == current).astype(jnp.float32)
        summed = summed + kernel[offset] * extended[:, begin : begin + length] * joined[:, :, None]
    return summed


def compose(earlier, later):
    return (earlier[0] * later[0], later[0][..., None] * earlier[1] + later[1])


def geometry(segments, before_block, log_decay):
    rows, length = segments.shape
    pieces = length // SUBBLOCK
    grouped = segments.reshape(rows, pieces, SUBBLOCK)
    before = jnp.concatenate([before_block[:, None], grouped[:, :-1, -1]], axis=1)
    living = (grouped == before[:, :, None]).astype(jnp.float32)
    retained = (grouped == grouped[:, :, -1:]).astype(jnp.float32)
    position = jnp.arange(SUBBLOCK, dtype=jnp.float32)
    causal = position[:, None] >= position[None, :]
    allowed = jnp.logical_and(grouped[:, :, :, None] == grouped[:, :, None, :], causal).astype(
        jnp.float32
    )
    growing = jnp.exp(position[:, None, None] * log_decay)
    shrinking = jnp.exp(-position[:, None, None] * log_decay)
    step_in = growing * jnp.exp(log_decay)
    closing = jnp.exp((SUBBLOCK - 1.0 - position)[:, None, None] * log_decay)
    whole_decay = jnp.exp(SUBBLOCK * log_decay)[None, None] * living[:, :, -1][:, :, None, None]
    running = jnp.ones((rows,) + log_decay.shape, jnp.float32)
    carried = []
    for index in range(pieces):
        carried.append(running)
        running = running * whole_decay[:, index]
    return (
        living,
        retained,
        allowed,
        growing,
        shrinking,
        step_in,
        closing,
        whole_decay,
        jnp.stack(carried, axis=1),
        running,
    )


def local_part(queries, shifted, values, shape_info):
    (
        living,
        retained,
        allowed,
        growing,
        shrinking,
        step_in,
        closing,
        whole_decay,
        carried,
        block_decay,
    ) = shape_info
    scores = jnp.einsum(
        "bncgi,bnsgi->bngcs", queries * growing, shifted * shrinking, precision=precise
    )
    scores = scores * allowed[:, :, None]
    within = jnp.einsum("bngcs,bnsgj->bncgj", scores, values, precision=precise)
    update = jnp.einsum(
        "bncgi,bncgj->bngij",
        shifted * closing * retained[..., None, None],
        values,
        precision=precise,
    )
    running = jnp.zeros_like(update[:, 0])
    starts = []
    for index in range(update.shape[1]):
        starts.append(running)
        running = whole_decay[:, index][..., None] * running + update[:, index]
    return (within, jnp.stack(starts, axis=1), running)


def across(queries, starts, state_in, shape_info):
    (
        living,
        retained,
        allowed,
        growing,
        shrinking,
        step_in,
        closing,
        whole_decay,
        carried,
        block_decay,
    ) = shape_info
    entries = starts + carried[..., None] * state_in[:, None]
    weighted = queries * step_in * living[..., None, None]
    return jnp.einsum("bncgi,bngij->bncgj", weighted, entries, precision=precise)


def on_device(
    layer_input,
    segment_ids,
    mixer_gain,
    query_weight,
    key_weight,
    value_weight,
    shift_kernel,
    state_decay,
    mixer_weight,
    feed_gain,
    up_weight,
    down_weight,
    cotangent,
):
    (
        mixer_gain_all,
        query_all,
        key_all,
        value_all,
        kernel_all,
        mixer_all,
        feed_gain_all,
        up_all,
        down_all,
    ) = (
        lax.all_gather(mixer_gain, ("dp", "ctx"), axis=0, tiled=True),
        lax.all_gather(query_weight, ("dp", "ctx"), axis=0, tiled=True),
        lax.all_gather(key_weight, ("dp", "ctx"), axis=0, tiled=True),
        lax.all_gather(value_weight, ("dp", "ctx"), axis=0, tiled=True),
        lax.all_gather(shift_kernel, ("dp", "ctx"), axis=1, tiled=True),
        lax.all_gather(mixer_weight, ("dp", "ctx"), axis=1, tiled=True),
        lax.all_gather(feed_gain, ("dp", "ctx"), axis=0, tiled=True),
        lax.all_gather(up_weight, ("dp", "ctx"), axis=0, tiled=True),
        lax.all_gather(down_weight, ("dp", "ctx"), axis=1, tiled=True),
    )
    heads, width = state_decay.shape
    log_decay = jnp.log(state_decay)
    taps = kernel_all.shape[0]
    rows, length, model = layer_input.shape
    pieces = length // SUBBLOCK
    features = heads * width
    seg_float = segment_ids.astype(jnp.float32)
    joint_weight = jnp.concatenate([query_all, key_all, value_all], axis=1)
    normed = normalize(layer_input, mixer_gain_all)
    projected = project(normed, joint_weight)
    queries = projected[:, :, :features]
    keys_raw = projected[:, :, features : 2 * features]
    values = projected[:, :, 2 * features :]
    tail_keys, tail_segs = passed_along(
        (keys_raw[:, length - taps + 1 :], seg_float[:, length - taps + 1 :]), "ctx", 1
    )
    extended = jnp.concatenate([tail_keys, keys_raw], axis=1)
    seg_ext = jnp.concatenate([tail_segs, seg_float], axis=1)
    shift_fixed = partial(shift_keys, seg_ext=seg_ext)
    shifted = shift_fixed(extended, kernel_all)
    info = geometry(seg_float, tail_segs[:, -1], log_decay)
    block_decay = info[-1]
    head_q = queries.reshape(rows, pieces, SUBBLOCK, heads, width)
    head_k = shifted.reshape(rows, pieces, SUBBLOCK, heads, width)
    head_v = values.reshape(rows, pieces, SUBBLOCK, heads, width)
    within, starts, local_end = local_part(head_q, head_k, head_v, info)
    identity = (jnp.ones_like(block_decay), jnp.zeros_like(local_end))
    state_in = carried_in((block_decay, local_end), "ctx", compose, identity, False)[1]
    mixed = (within + across(head_q, starts, state_in, info)).reshape(rows, length, features)
    branch = lax.psum(project(mixed, mixer_all), "tensor")
    resid = layer_input + branch
    normed_feed = normalize(resid, feed_gain_all)
    pre_act = project(normed_feed, up_all)
    activated, gelu_back = jax.vjp(smooth_gate, pre_act)
    feed = lax.psum(project(activated, down_all), "tensor")
    layer_output = resid + feed
    act_grad = project(cotangent, down_all.T)
    down_grad = outer_sum(activated, cotangent)
    (pre_grad,) = gelu_back(act_grad)
    up_grad = outer_sum(normed_feed, pre_grad)
    feed_normed_grad = lax.psum(project(pre_grad, up_all.T), "tensor")
    _, feed_norm_back = jax.vjp(normalize, resid, feed_gain_all)
    resid_ln_grad, feed_gain_grad = feed_norm_back(feed_normed_grad)
    resid_grad = cotangent + resid_ln_grad
    mixed_grad = project(resid_grad, mixer_all.T)
    mixer_weight_grad = outer_sum(mixed, resid_grad)
    head_du = mixed_grad.reshape(rows, pieces, SUBBLOCK, heads, width)
    (
        living,
        retained,
        allowed,
        growing,
        shrinking,
        step_in,
        closing,
        whole_decay,
        carried,
        block_decay,
    ) = info
    own_grad = jnp.einsum(
        "bncgi,bncgj,bngi->bgij",
        head_q * step_in * living[..., None, None],
        head_du,
        carried,
        precision=precise,
    )
    identity_grad = (jnp.ones_like(block_decay), jnp.zeros_like(own_grad))
    after = carried_in((block_decay, own_grad), "ctx", compose, identity_grad, True)[1]

    def mixer_full(query_in, key_in, value_in, entering):
        inner, begins, ending = local_part(query_in, key_in, value_in, info)
        output = inner + across(query_in, begins, entering, info)
        return (output, ending + block_decay[..., None] * entering)

    _, mixer_vjp = jax.vjp(mixer_full, head_q, head_k, head_v, state_in)
    query_act_grad, shifted_grad, value_act_grad, _ = mixer_vjp((head_du, after))
    _, shift_back = jax.vjp(shift_fixed, extended, kernel_all)
    ext_grad, kernel_grad = shift_back(shifted_grad.reshape(rows, length, features))
    returned = passed_along(ext_grad[:, : taps - 1], "ctx", -1)
    key_act_grad = ext_grad[:, taps - 1 :] + jnp.pad(
        returned, ((0, 0), (length - taps + 1, 0), (0, 0))
    )
    joint_grad = jnp.concatenate(
        [
            query_act_grad.reshape(rows, length, features),
            key_act_grad,
            value_act_grad.reshape(rows, length, features),
        ],
        axis=2,
    )
    joint_weight_grad = outer_sum(normed, joint_grad)
    normed_grad = lax.psum(project(joint_grad, joint_weight.T), "tensor")
    _, mixer_norm_back = jax.vjp(normalize, layer_input, mixer_gain_all)
    input_ln_grad, mixer_gain_grad = mixer_norm_back(normed_grad)
    input_grad = resid_grad + input_ln_grad
    query_grad = joint_weight_grad[:, :features]
    key_grad = joint_weight_grad[:, features : 2 * features]
    value_grad = joint_weight_grad[:, 2 * features :]
    all_parts = tuple(
        (
            lax.psum_scatter(mixer_gain_grad, ("dp", "ctx"), scatter_dimension=0, tiled=True),
            lax.psum_scatter(query_grad, ("dp", "ctx"), scatter_dimension=0, tiled=True),
            lax.psum_scatter(key_grad, ("dp", "ctx"), scatter_dimension=0, tiled=True),
            lax.psum_scatter(value_grad, ("dp", "ctx"), scatter_dimension=0, tiled=True),
            lax.psum_scatter(kernel_grad, ("dp", "ctx"), scatter_dimension=1, tiled=True),
            lax.psum_scatter(mixer_weight_grad, ("dp", "ctx"), scatter_dimension=1, tiled=True),
            lax.psum_scatter(feed_gain_grad, ("dp", "ctx"), scatter_dimension=0, tiled=True),
            lax.psum_scatter(up_grad, ("dp", "ctx"), scatter_dimension=0, tiled=True),
            lax.psum_scatter(down_grad, ("dp", "ctx"), scatter_dimension=1, tiled=True),
        )
    )
    return (layer_output, input_grad) + all_parts


PAIR = 2
BLOCK = 128
LANES = 128
LIMIT = 60
TILE = 256
C_GELU = 0.7978845608028654
NN = ((1,), (0,))
NT = ((1,), (1,))
TN = ((0,), (0,))
f32, bf16 = jnp.float32, jnp.bfloat16


def params(limit=LIMIT):
    return pltpu.CompilerParams(vmem_limit_bytes=limit * 2**20)


def cost(flops, moved):
    return pl.CostEstimate(flops=int(flops), bytes_accessed=int(moved), transcendentals=0)


def shaped(shape, dtype=jnp.float32):
    return jax.ShapeDtypeStruct(shape, dtype)


def split(a):
    high = a.astype(bf16)
    return high, (a - high.astype(f32)).astype(bf16)


def d3(left, right, dims):
    dot = partial(lax.dot_general, dimension_numbers=(dims, ((), ())), preferred_element_type=f32)
    if dims == TN:
        joined_left = jnp.concatenate([left[0], left[1], left[0]], axis=0)
        return dot(joined_left, jnp.concatenate([right[0], right[0], right[1]], axis=0))
    rows = left[0].shape[0]
    both = dot(jnp.concatenate(left, axis=0), right[0])
    return both[:rows] + both[rows:] + dot(left[0], right[1])


def tied(arrays):
    specs = [
        pl.BlockSpec((1,) * (a.ndim - 2) + (8, 128), lambda *_, n=a.ndim: (0,) * n) for a in arrays
    ]
    return specs, list(arrays)


def norm_parts(v):
    centered = v - jnp.mean(v, axis=-1, keepdims=True)
    r = lax.rsqrt(jnp.mean(centered * centered, axis=-1, keepdims=True) + eps)
    return centered * r, r


def whole(shape):
    return pl.BlockSpec(
        shape, lambda *_: (0,) * len(shape), pipeline_mode=pl.Buffered(buffer_count=1)
    )


def scalar():
    return pl.BlockSpec(memory_space=pltpu.SMEM)


def pack_mixer_kernel(me_ref, q_ref, k_ref, v_ref, m_ref, mg_ref, fg_ref, kern_ref, decay_ref, o_ref):
    rows, own = q_ref.shape
    taps, few = kern_ref.shape
    heads, width = decay_ref.shape
    o_ref[0:rows, 0:own] = q_ref[...]
    o_ref[0:rows, own : 2 * own] = k_ref[...]
    o_ref[0:rows, 2 * own : 3 * own] = v_ref[...]
    o_ref[0:rows, 3 * own :] = jnp.transpose(m_ref[...])
    o_ref[rows:, :] = jnp.zeros((8, o_ref.shape[1]), f32)
    for b in range(8):

        @pl.when(me_ref[0] == b)
        def _():
            o_ref[rows : rows + 1, b * rows : (b + 1) * rows] = mg_ref[...]
            o_ref[rows + 1 : rows + 2, b * rows : (b + 1) * rows] = fg_ref[...]
            o_ref[rows + 2 : rows + 2 + taps, b * few : (b + 1) * few] = kern_ref[...]

    @pl.when(me_ref[0] == 0)
    def _():
        for h in range(heads):
            at = rows + 2 + taps
            o_ref[at : at + 1, h * width : (h + 1) * width] = decay_ref[h : h + 1, :]


def run_pack_mixer(me, q, k, v, m, mg, fg, kern, decay):
    rows, own = q.shape
    args = (q, k, v, m, mg[None], fg[None], kern, decay)
    return pl.pallas_call(
        pack_mixer_kernel,
        grid=(1,),
        in_specs=[scalar()] + [whole(a.shape) for a in args],
        out_specs=whole((rows + 8, 4 * own)),
        out_shape=shaped((rows + 8, 4 * own)),
        compiler_params=params(),
        cost_estimate=cost(1e6, 2**20),
        name="pack_mixer",
    )(me, *args)


def pack_feed_kernel(up_ref, down_ref, o_ref):
    hidden = up_ref.shape[1]
    o_ref[:, :hidden] = up_ref[...]
    o_ref[:, hidden:] = jnp.transpose(down_ref[...])


def run_pack_feed(up, down):
    return pl.pallas_call(
        pack_feed_kernel,
        grid=(1,),
        in_specs=[whole(up.shape), whole(down.shape)],
        out_specs=whole((up.shape[0], 2 * up.shape[1])),
        out_shape=shaped((up.shape[0], 2 * up.shape[1])),
        compiler_params=params(),
        cost_estimate=cost(1e6, 2 * 2**20),
        name="pack_feed",
    )(up, down)


def sequence_specs(model, order):
    def mine(i, m):
        return (m[0] & 1, order(i, m) % 2, 0)

    return [pl.BlockSpec((1, TILE, model), mine)] * 2


def sequence_tile(tile, me_ref, mine_ref, came_ref):
    own = tile // 2 == (me_ref[0] & 1)
    return jnp.where(own, mine_ref[0], came_ref[0])


def project_kernel(me_ref, x_ref, xr_ref, *refs):
    first, second = refs[0:8], refs[8:16]
    o_ref, wh_ref, wl_ref, mh_ref, ml_ref, gains_ref, small_ref = refs[-7:]
    own = first[0].shape[1] // 4
    rows = wh_ref.shape[0] // 8

    @pl.when(pl.program_id(0) == 0)
    def _():
        for r in range(8):
            at = pl.ds(pl.multiple_of((me_ref[0] ^ r) * rows, rows), rows)
            a, b = first[r][0:rows, :], second[r][0:rows, :]
            for i in range(4):
                both = jnp.concatenate(
                    [a[:, i * own : (i + 1) * own], b[:, i * own : (i + 1) * own]], axis=1
                )
                high, low = split(both)
                if i < 3:
                    wh_ref[at, i * 2 * own : (i + 1) * 2 * own] = high
                    wl_ref[at, i * 2 * own : (i + 1) * 2 * own] = low
                else:
                    mh_ref[at, :] = high
                    ml_ref[at, :] = low
        sums = []
        for pieces in (first, second):
            total = pieces[0][rows:, :]
            for r in range(1, 8):
                total = total + pieces[r][rows:, :]
            sums.append(total)
        gains_ref[...] = sums[0]
        small_ref[...] = jnp.concatenate([s[:, :own] for s in sums], axis=1)

    x = sequence_tile(pl.program_id(0), me_ref, x_ref, xr_ref)
    n = split(norm_parts(x)[0] * gains_ref[0:1, :])
    o_ref[...] = d3(n, (wh_ref[...], wl_ref[...]), NN)


def run_project(me, x, first, second, ties=()):
    rows, half, model = x[0].shape
    tokens = rows * half
    own = first[0].shape[1] // 4
    wide = 6 * own
    piece = whole(first[0].shape)
    weights = [(model, wide)] * 2 + [(model, 2 * own)] * 2
    few = [(8, model), (8, 2 * own)]
    tie_specs, tie_args = tied(ties)
    return pl.pallas_call(
        project_kernel,
        grid_spec=pltpu.PrefetchScalarGridSpec(
            num_scalar_prefetch=1,
            grid=(tokens // TILE,),
            in_specs=sequence_specs(model, lambda i, m: i) + [piece] * 16 + tie_specs,
            out_specs=[pl.BlockSpec((TILE, wide), lambda i, m: (i, 0))]
            + [whole(s) for s in weights + few],
        ),
        out_shape=[shaped((tokens, wide))]
        + [shaped(s, bf16) for s in weights]
        + [shaped(s) for s in few],
        compiler_params=params(),
        cost_estimate=cost(6 * tokens * model * wide, 20 * 2**20),
        name="project",
    )(me, *x, *first, *second, *tie_args)


def spread(parts, masks):
    return tuple(jnp.concatenate([p * m for m in masks], axis=0) for p in parts)


def lane_masks(lanes):
    which = lax.broadcasted_iota(jnp.int32, (1, lanes), 1) // (lanes // PAIR)
    return [jnp.where(which == h, 1.0, 0.0).astype(bf16) for h in range(PAIR)]


def square_mask(lanes):
    a = lax.broadcasted_iota(jnp.int32, (lanes, lanes), 0) // (lanes // PAIR)
    b = lax.broadcasted_iota(jnp.int32, (lanes, lanes), 1) // (lanes // PAIR)
    return jnp.where(a == b, 1.0, 0.0)


def fill_tables(decay, grow, shrink, dec, end, full):
    size, model = grow.shape
    lanes = dec.shape[0]
    rates = jnp.log(decay)
    position = lax.broadcasted_iota(jnp.int32, (size, model), 0).astype(f32)
    grow[...] = jnp.exp(position * rates)
    shrink[...] = jnp.exp(-position * rates)
    for p in range(model // lanes):
        s = slice(p * lanes, (p + 1) * lanes)
        column = jnp.transpose(jnp.broadcast_to(rates[:, s], (lanes, lanes)))
        dec[:, s] = jnp.exp(column)
        end[:, s] = jnp.exp((size - 1.0) * column)
        full[:, s] = jnp.exp(float(size) * column)


def joined(extended, size, taps):
    now = extended[8:]
    return [jnp.where(extended[8 - j : 8 - j + size] == now, 1.0, 0.0) for j in range(1, taps)]


def shift_forward(keys, before, kern, same, taps):
    extended = jnp.concatenate([before, keys], axis=0)
    size = keys.shape[0]
    moved = [keys]
    for j in range(1, taps):
        moved.append(extended[8 - j : 8 - j + size] * same[j - 1])
    total = kern[0:1, :] * keys
    for j in range(1, taps):
        total = total + kern[j : j + 1, :] * moved[j]
    return total, moved


def allowed_masks(seg, row):
    size, wide = seg.shape[0], row.shape[1]
    rows = lax.broadcasted_iota(jnp.int32, (size, wide), 0)
    cols = lax.broadcasted_iota(jnp.int32, (size, wide), 1) % size
    same = seg == row
    return (
        jnp.where(jnp.logical_and(rows >= cols, same), 1.0, 0.0),
        jnp.where(jnp.logical_and(rows <= cols, same), 1.0, 0.0),
    )


def pair(a_ref, b_ref):
    return jnp.concatenate([a_ref[...], b_ref[...]], axis=1)


def third_of(refs, rows, i):
    wide = refs[0].shape[1] // 3
    return jnp.concatenate([r[rows, i * wide : (i + 1) * wide] for r in refs], axis=1)


def mixer_kernel(taps, last, me_ref, proj_ref, seg_ref, segrow_ref, small_ref, *refs):
    if last:
        x_ref, xr_ref, other_ref, gains_ref, ah_ref, al_ref, bh_ref, bl_ref = refs[:8]
        state_out_ref, resid_ref, nh_ref, nl_ref = refs[8:12]
    else:
        state_out_ref, mixed_ref = refs[:2]
    state, tail, segtail, grow, shrink, dec, end, full, mixed = refs[-9:]
    size, lanes = grow.shape[0], dec.shape[0]
    projs = (proj_ref,)

    @pl.when(pl.program_id(0) == 0)
    def _():
        state[...] = jnp.zeros_like(state)
        tail[...] = jnp.zeros_like(tail)
        segtail[...] = jnp.full_like(segtail, -1.0)
        fill_tables(small_ref[2 + taps : 3 + taps], grow, shrink, dec, end, full)

    kern = small_ref[2 : 2 + taps]
    masks = lane_masks(lanes)
    square = square_mask(lanes)
    groups = [slice(g * lanes, (g + 1) * lanes) for g in range(state.shape[1] // lanes)]
    before_keys, before = tail[...], segtail[...]
    for chunk in range(proj_ref.shape[0] // size):
        here = slice(chunk * size, (chunk + 1) * size)
        seg = seg_ref[here, :]
        extended = jnp.concatenate([before, seg], axis=0)
        living = jnp.where(seg == before[7:8], 1.0, 0.0)
        kept = jnp.where(seg == seg[size - 1 :], 1.0, 0.0)
        goes_on = living[size - 1 :]
        q_all, keys, v_all = (third_of(projs, here, i) for i in range(3))
        shifted, _ = shift_forward(keys, before_keys, kern, joined(extended, size, taps), taps)
        before_keys, before = keys[size - 8 :, :], seg[size - 8 :]
        allowed, _ = allowed_masks(seg, segrow_ref[chunk])
        state_out_ref[chunk] = state[...]
        qg, kf, v, scores = [], [], [], []
        for s in groups:
            qg.append(split(q_all[:, s] * grow[:, s]))
            kf.append(shifted[:, s] * shrink[:, s])
            v.append(split(v_all[:, s]))
            scores.append(d3(qg[-1], spread(split(kf[-1]), masks), NT))
        updates = [d3(split(k * kept), w, TN) * square for k, w in zip(kf, v)]
        weights = [split(score * allowed) for score in scores]
        for g, s in enumerate(groups):
            part = d3(weights[g], spread(v[g], masks), NN)
            mixed[here, s] = part + living * d3(qg[g], split(state[:, s] * dec[:, s]), NN)
        for g, s in enumerate(groups):
            state[:, s] = state[:, s] * (full[:, s] * goes_on) + end[:, s] * updates[g]
    tail[...] = before_keys
    segtail[...] = before
    if not last:
        mixed_ref[...] = mixed[...]
        return
    resid = (
        sequence_tile(pl.program_id(0), me_ref, x_ref, xr_ref)
        + d3(split(other_ref[...]), (ah_ref[...], al_ref[...]), NT)
        + d3(split(mixed[...]), (bh_ref[...], bl_ref[...]), NT)
    )
    resid_ref[...] = resid
    nh_ref[...], nl_ref[...] = split(norm_parts(resid)[0] * gains_ref[1:2, :])


def mixer_scratch(model):
    return [pltpu.VMEM((BLOCK, model), f32)] * 2 + [pltpu.VMEM((LANES, model), f32)] * 3


def run_mixer(me, proj, seg, segrow, small, taps, more=(), ties=()):
    tokens, third = proj.shape[0], proj.shape[1] // 3
    chunks = TILE // BLOCK

    def row(width):
        return pl.BlockSpec((TILE, width), lambda c, m: (c, 0))

    extra_specs, extra = [], []
    outs = [(row(third), shaped((tokens, third)))]
    if more:
        x, other, gains, a, b = more
        model = x[0].shape[2]
        extra_specs = sequence_specs(model, lambda i, m: i) + [row(third), whole(gains.shape)]
        extra_specs = extra_specs + [whole(a[0].shape)] * 4
        extra = [*x, other, gains, *a, *b]
        outs = [(row(model), shaped((tokens, model), t)) for t in (f32, bf16, bf16)]
    states = pl.BlockSpec((chunks, LANES, third), lambda c, m: (c, 0, 0))
    tie_specs, tie_args = tied(ties)
    return pl.pallas_call(
        partial(mixer_kernel, taps, bool(more)),
        grid_spec=pltpu.PrefetchScalarGridSpec(
            num_scalar_prefetch=1,
            grid=(tokens // TILE,),
            in_specs=[
                row(3 * third),
                row(1),
                pl.BlockSpec((chunks, 1, segrow.shape[2]), lambda c, m: (c, 0, 0)),
                whole(small.shape),
            ]
            + extra_specs
            + tie_specs,
            out_specs=[states] + [spec for spec, _ in outs],
            scratch_shapes=[
                pltpu.VMEM((LANES, third), f32),
                pltpu.VMEM((8, third), f32),
                pltpu.VMEM((8, 1), f32),
            ]
            + mixer_scratch(third)
            + [pltpu.VMEM((TILE, third), f32)],
        ),
        out_shape=[shaped((tokens // BLOCK, LANES, third))] + [shape for _, shape in outs],
        compiler_params=params(),
        cost_estimate=cost(6e9 + (7e9 if more else 0), 10 * 2**20),
        name="mixer_out" if more else "mixer",
    )(me, proj, seg, segrow, small, *extra, *tie_args)


def mixer_back_kernel(
    taps, me_ref, fng_ref, resid_ref, x_ref, xr_ref, ct_ref, cr_ref, pa_ref, pb_ref, ba_ref, bb_ref,
    ta_ref, tb_ref, mixed_ref, seg_ref, segb_ref, segrow_ref, sa_ref, sb_ref, gains_ref,
    ah_ref, al_ref, bh_ref, bl_ref, qah_ref, qal_ref, qbh_ref, qbl_ref, *refs,
):
    (
        theirs_ref, ig_ref, keep_ref, send_ref, gg, g2, dkern,
        grad, head, grow, shrink, dec, end, full, du_all, da, db, wg,
    ) = refs[-18:]
    size, lanes = grow.shape[0], dec.shape[0]
    step, steps = pl.program_id(0), pl.num_programs(0)
    projs = (pa_ref, pb_ref)

    @pl.when(step == 0)
    def _():
        grad[...] = jnp.zeros_like(grad)
        head[...] = jnp.zeros_like(head)
        dkern[...] = jnp.zeros_like(dkern)
        gg[...] = jnp.zeros_like(gg)
        g2[...] = jnp.zeros_like(g2)
        wg[...] = jnp.zeros_like(wg)
        fill_tables(pair(sa_ref, sb_ref)[2 + taps : 3 + taps], grow, shrink, dec, end, full)

    third = ah_ref.shape[1]
    tile = steps - 1 - step
    back, gain_grad, _ = norm_back(resid_ref[...], gains_ref[1:2, :], fng_ref[...])
    rg = sequence_tile(tile, me_ref, ct_ref, cr_ref) + back
    g2[...] += gain_grad
    r2 = split(rg)
    du_all[:, :third] = d3(r2, (ah_ref[...], al_ref[...]), NN)
    du_all[:, third:] = d3(r2, (bh_ref[...], bl_ref[...]), NN)

    kern = pair(sa_ref, sb_ref)[2 : 2 + taps]
    masks = lane_masks(lanes)
    square = square_mask(lanes)
    model = grad.shape[1]
    groups = [slice(g * lanes, (g + 1) * lanes) for g in range(model // lanes)]
    count = len(groups)
    chunks = rg.shape[0] // size
    for chunk in reversed(range(chunks)):
        here = slice(chunk * size, (chunk + 1) * size)
        seg = seg_ref[here, :]
        q_all, keys, v_all = (third_of(projs, here, i) for i in range(3))
        if chunk:
            just = slice(chunk * size - 8, chunk * size)
            before, before_keys = seg_ref[just, :], third_of(projs, just, 1)
        else:
            before = jnp.where(step == steps - 1, -1.0, segb_ref[...])
            before_keys = pair(ba_ref, bb_ref)
        extended = jnp.concatenate([before, seg], axis=0)
        living = jnp.where(seg == before[7:8], 1.0, 0.0)
        kept = jnp.where(seg == seg[size - 1 :], 1.0, 0.0)
        goes_on = living[size - 1 :]
        same = joined(extended, size, taps)
        shifted, moved = shift_forward(keys, before_keys, kern, same, taps)
        allowed, allowed_t = allowed_masks(seg, segrow_ref[chunk])
        qf = [q_all[:, s] * grow[:, s] for s in groups]
        qg = [split(q) for q in qf]
        kg = [split(shifted[:, s] * shrink[:, s]) for s in groups]
        v = [split(v_all[:, s]) for s in groups]
        du = [split(du_all[here, s]) for s in groups]
        p_t = [d3(kg[g], spread(qg[g], masks), NT) for g in range(count)]
        dp = [d3(du[g], spread(v[g], masks), NT) for g in range(count)]
        dp_t = [d3(v[g], spread(du[g], masks), NT) for g in range(count)]
        updates = [d3(split(qf[g] * living), du[g], TN) * square for g in range(count)]
        p_t = [split(p * allowed_t) for p in p_t]
        dp = [split(p * allowed) for p in dp]
        dp_t = [split(p * allowed_t) for p in dp_t]
        for g, s in enumerate(groups):
            first = s.start < third
            at = s.start - (0 if first else third)
            to = da if first else db
            states = (ta_ref if first else tb_ref)[chunk, :, at : at + lanes]
            entering = split(states * dec[:, s])
            leaving = split(grad[:, s] * end[:, s])
            dqg = d3(dp[g], spread(kg[g], masks), NN) + living * d3(du[g], entering, NT)
            dkg = d3(dp_t[g], spread(qg[g], masks), NN) + kept * d3(v[g], leaving, NT)
            dv = d3(p_t[g], spread(du[g], masks), NN) + kept * d3(kg[g], leaving, NN)
            to[here, 2 * third + at : 2 * third + at + lanes] = dv
            to[here, at : at + lanes] = dqg * grow[:, s]
            dshift = dkg * shrink[:, s]
            grad[:, s] = grad[:, s] * (full[:, s] * goes_on) + dec[:, s] * updates[g]
            total = kern[0:1, s] * dshift
            for j in range(1, taps):
                part = dshift * same[j - 1]
                longer = jnp.concatenate([part, head[j - 1, :, s]], axis=0)
                total = total + kern[j : j + 1, s] * longer[j : j + size]
                head[j - 1, :, s] = part[0:8]
            to[here, third + at : third + at + lanes] = total
            if g < 2:
                for j in range(taps):
                    dkern[j : j + 1, s] += jnp.sum(
                        dshift * moved[j][:, s], axis=0, keepdims=True
                    )

    own = keep_ref.shape[-1] // 4
    x = sequence_tile(tile, me_ref, x_ref, xr_ref)
    left, right = split(da[...]), split(db[...])
    incoming = d3(left, (qah_ref[...], qal_ref[...]), NT)
    incoming = incoming + d3(right, (qbh_ref[...], qbl_ref[...]), NT)
    back, gain_grad, xhat = norm_back(x, gains_ref[0:1, :], incoming)
    ig_ref[0] = rg + back
    gg[...] += gain_grad
    n = split(xhat * gains_ref[0:1, :])
    joint = tuple(
        jnp.concatenate([p[:, i * third : i * third + own] for i in range(3)], axis=1) for p in left
    )
    wg[:, : 3 * own] += d3(n, joint, TN)
    wg[:, 3 * own :] += d3(r2, split(mixed_ref[:, :own]), TN)

    @pl.when(tile // 2 != (me_ref[0] & 1))
    def _():
        theirs_ref[...] = ig_ref[0]

    @pl.when(step == steps - 1)
    def _():
        few = (gg[...], g2[...], dkern[:, :own])
        store_blocks(me_ref[0], wg, few, keep_ref, send_ref)


def run_mixer_back(
    me, fng, resid, x, ct, projs, states, mixed, seg, segrow, smalls, gains, a, b, qa, qb, taps
):
    tokens, model = resid.shape
    third = projs[0].shape[1] // 3
    own = third // 2
    chunks = TILE // BLOCK
    last = tokens // TILE - 1
    blocks = (1, 4, model // 8 + 8, 4 * own)

    def prior(c):
        return jnp.maximum((last - c) * (TILE // 8) - 1, 0)

    row = pl.BlockSpec((TILE, model), lambda c, m: (last - c, 0))
    proj = pl.BlockSpec((TILE, 3 * third), lambda c, m: (last - c, 0))
    before = pl.BlockSpec((8, third), lambda c, m: (prior(c), 1))
    state = pl.BlockSpec((chunks, LANES, third), lambda c, m: (last - c, 0, 0))
    halves = pl.BlockSpec((1, TILE, model), lambda c, m: ((last - c) // 2, (last - c) % 2, 0))

    def for_other(c, m):
        core, tile = m[0] & 1, last - c
        return (jnp.where(tile // 2 == 1 - core, tile % 2, core), 0)

    theirs = pl.BlockSpec((TILE, model), for_other)
    return pl.pallas_call(
        partial(mixer_back_kernel, taps),
        grid_spec=pltpu.PrefetchScalarGridSpec(
            num_scalar_prefetch=1,
            grid=(last + 1,),
            in_specs=[row, row]
            + sequence_specs(model, lambda c, m: last - c) * 2
            + [proj, proj, before, before, state, state]
            + [
                pl.BlockSpec((TILE, third), lambda c, m: (last - c, 0)),
                pl.BlockSpec((TILE, 1), lambda c, m: (last - c, 0)),
                pl.BlockSpec((8, 1), lambda c, m: (prior(c), 0)),
                pl.BlockSpec((chunks, 1, segrow.shape[2]), lambda c, m: (last - c, 0, 0)),
                whole(smalls[0].shape),
                whole(smalls[1].shape),
                whole(gains.shape),
            ]
            + [whole(a[0].shape)] * 4
            + [whole(qa[0].shape)] * 4,
            out_specs=[theirs, halves, whole(blocks), whole(blocks)],
            scratch_shapes=[
                pltpu.VMEM((1, model), f32),
                pltpu.VMEM((1, model), f32),
                pltpu.VMEM((taps, model), f32),
                pltpu.VMEM((LANES, model), f32),
                pltpu.VMEM((taps - 1, 8, model), f32),
            ]
            + mixer_scratch(model)
            + [pltpu.VMEM((TILE, model), f32)]
            + [pltpu.VMEM((TILE, 3 * third), f32)] * 2
            + [pltpu.VMEM((model, 4 * own), f32)],
        ),
        out_shape=[shaped((tokens // 2, model)), shaped((2, tokens // 2, model))]
        + [shaped(blocks), shaped(blocks)],
        compiler_params=params(),
        cost_estimate=cost(1e11, 60 * 2**20),
        name="mixer_back",
    )(
        me, fng, resid, *x, *ct, *projs, *projs, *states, mixed, seg, seg, segrow, *smalls, gains,
        *a, *b, *qa, *qb,
    )


def gelu_parts(pre, back):
    th = jnp.tanh(pre * (C_GELU + (C_GELU * 0.044715) * (pre * pre)))
    half = 0.5 + 0.5 * th
    act = pre * half
    slope = half + (1.0 - th) * act * (C_GELU + (3 * C_GELU * 0.044715) * (pre * pre))
    return act, back * slope


def store_blocks(me, g, few, keep_ref, send_ref):
    rows = g.shape[0] // 8
    for b in range(8):
        r = me ^ b
        where = r // 2
        short = [f[:, b * (f.shape[1] // 8) : (b + 1) * (f.shape[1] // 8)] for f in few]

        def put(ref):
            ref[0, where, 0:rows, :] = g[b * rows : (b + 1) * rows]
            ref[0, where, rows:, :] = jnp.zeros((ref.shape[2] - rows, ref.shape[3]), f32)
            at = rows
            for part in short:
                ref[0, where, at : at + part.shape[0], 0 : part.shape[1]] = part
                at = at + part.shape[0]

        @pl.when((r & 1) == 0)
        def _():
            put(keep_ref)

        @pl.when((r & 1) == 1)
        def _():
            put(send_ref)


def feed_kernel(own, slots, final, me_ref, nh_ref, nl_ref, ct_ref, cr_ref, out_in, fng_in, w_in, *refs):
    if own:
        out_ref, fng_ref, wg, w = refs[-4:]
    else:
        out_ref, fng_ref, w = refs[-3:]
    step = pl.program_id(0)
    hidden = w.shape[2] // (2 * slots)

    @pl.when(step == 0)
    def _():
        w[0], w[1] = split(w_in[...])
        if own:
            wg[...] = jnp.zeros_like(wg)

    tile = theirs_first(step, me_ref)
    n = (nh_ref[...], nl_ref[...])
    ct = split(sequence_tile(tile, me_ref, ct_ref, cr_ref))
    out, fng = out_in[...], None if own else fng_in[...]
    for t in range(slots):
        a, b = (slice((2 * t + i) * hidden, (2 * t + i + 1) * hidden) for i in range(2))
        u, d = (w[0, :, a], w[1, :, a]), (w[0, :, b], w[1, :, b])
        act, grad = gelu_parts(d3(n, u, NN), d3(ct, d, NN))
        act, grad = split(act), split(grad)
        out = out + d3(act, d, NT)
        more = d3(grad, u, NT)
        fng = more if fng is None else fng + more
    out_ref[...] = out.reshape(out_ref.shape)
    fng_ref[...] = fng
    if own:
        wg[:, :hidden] += d3(n, grad, TN)
        wg[:, hidden:] += d3(ct, act, TN)
    if final:

        @pl.when(step < 2)
        def _():
            refs[0][...] = out_ref[0]


def theirs_first(step, me):
    core = me[0] & 1
    return jnp.where(step < 2, 1 - core, core) * 2 + (step & 1)


def run_feed(me, n, ct, out, fng, w, slots, own, final=False):
    tokens, model = n[0].shape
    wide = w.shape[1]
    row = pl.BlockSpec((TILE, model), lambda i, m: (theirs_first(i, m), 0))
    full = shaped((tokens, model))
    last = pl.BlockSpec((1, TILE, model), lambda i, m: (theirs_first(i, m) // 2, i % 2, 0))
    theirs = pl.BlockSpec((TILE, model), lambda i, m: (jnp.minimum(i, 1), 0))
    return pl.pallas_call(
        partial(feed_kernel, own, slots, final),
        grid_spec=pltpu.PrefetchScalarGridSpec(
            num_scalar_prefetch=1,
            grid=(tokens // TILE,),
            in_specs=[row] * 2
            + sequence_specs(model, theirs_first)
            + [row] * 2
            + [whole(w.shape)],
            out_specs=[theirs] * final
            + [last if final else row, row]
            + ([whole((model, wide))] if own else []),
            scratch_shapes=[pltpu.VMEM((2, model, wide), bf16)],
        ),
        out_shape=[shaped((tokens // 2, model))] * final
        + [shaped((2, tokens // 2, model)) if final else full, full]
        + ([shaped((model, wide))] if own else []),
        compiler_params=params(),
        cost_estimate=cost((6 if own else 4) * 3 * tokens * model * wide, 30 * 2**20),
        name="feed_own" if own else "feed",
    )(me, *n, *ct, out, fng, w)


def norm_back(v, gain, incoming):
    xhat, r = norm_parts(v)
    scaled = incoming * gain
    grad = r * (
        scaled
        - jnp.mean(scaled, axis=-1, keepdims=True)
        - xhat * jnp.mean(scaled * xhat, axis=-1, keepdims=True)
    )
    return grad, jnp.sum(incoming * xhat, axis=0, keepdims=True), xhat


def leave_kernel(me_ref, came_ref, whole_ref, o_ref):
    o_ref[0] = came_ref[...]


def run_leave(me, mine, came):
    half, model = came.shape
    return pl.pallas_call(
        leave_kernel,
        grid_spec=pltpu.PrefetchScalarGridSpec(
            num_scalar_prefetch=1,
            grid=(half // TILE,),
            in_specs=[
                pl.BlockSpec((TILE, model), lambda t, m: (t, 0)),
                pl.BlockSpec(memory_space=pl.ANY),
            ],
            out_specs=pl.BlockSpec((1, TILE, model), lambda t, m: (1 - (m[0] & 1), t, 0)),
        ),
        out_shape=shaped((2, half, model)),
        input_output_aliases={2: 0},
        compiler_params=params(),
        cost_estimate=cost(1e6, 4 * 2**20),
        name="leave",
    )(me, came, mine)


def exchange(value, axis, flip):
    count = lax.axis_size(axis)
    return lax.ppermute(value, axis, [(i, i ^ flip) for i in range(count)])


def corner(value):
    pairs = []
    for d in range(4):
        for c in range(2):
            pairs.append((d * 2 + c, (d ^ (2 if c == 0 else 1)) * 2 + c))
    return lax.ppermute(value, ("dp", "ctx"), pairs)


def after(values, *earlier):
    return lax.optimization_barrier((tuple(values), earlier))[0]


def sides(block):
    return [exchange(block, "dp", 1), exchange(block, "dp", 2), exchange(block, "ctx", 1)]


def far(from_x, from_y):
    return corner(jnp.where(lax.axis_index("ctx") == 0, from_x, from_y))


def across_cores(*values):
    return [exchange(v, "ctx", 1) for v in values]


def by_distance(block, near, near_other, diagonal, diagonal_other):
    from_x, from_y, other = near
    return [
        block, other, from_x, near_other[0], from_y, near_other[1], diagonal, diagonal_other
    ]


def scatter_core(keep, send):
    return keep + exchange(send, "ctx", 1)


def scatter_corner(mine):
    core = lax.axis_index("ctx")
    own, to_x, to_y, to_d = (mine[:, i] for i in range(4))
    came = corner(to_d)
    return (
        own,
        jnp.where(core == 0, to_x + came, to_x),
        jnp.where(core == 0, to_y, to_y + came),
    )


def scatter_sides(own, to_x, to_y):
    return own + exchange(to_x, "dp", 1) + exchange(to_y, "dp", 2)


def swap_in(block):
    me = lax.axis_index("ctx")
    mine = lax.dynamic_index_in_dim(block, me, 0, keepdims=False)
    came = lax.dynamic_index_in_dim(exchange(block, "ctx", 1), me, 0, keepdims=False)
    return jnp.where(
        me == 0, jnp.concatenate([mine, came], axis=0), jnp.concatenate([came, mine], axis=0)
    )


def by_sequence(
    layer_input, segment_ids, mixer_gain, query_weight, key_weight, value_weight, shift_kernel,
    state_decay, mixer_weight, feed_gain, up_weight, down_weight, cotangent,
):
    plane = ("dp", "ctx")
    position = lax.axis_index("dp") * 2 + lax.axis_index("ctx")
    me = position.astype(jnp.int32).reshape(1)
    rows, own = query_weight.shape
    taps, few = shift_kernel.shape

    def gathered(block):
        return lax.all_gather(block, plane, axis=0, tiled=True)

    a0 = run_pack_mixer(
        me, query_weight, key_weight, value_weight, mixer_weight, mixer_gain, feed_gain,
        shift_kernel, state_decay,
    )
    a1 = exchange(a0, "tensor", 1)
    near0 = sides(a0)
    f0 = run_pack_feed(*after((up_weight, down_weight), a0))
    x_came = exchange(after((layer_input,), a0)[0], "ctx", 1)
    seg = swap_in(segment_ids).astype(f32)

    b0, b1, near0 = after((a0, a1, near0), f0)
    a2 = exchange(b0, "tensor", 2)
    far0 = far(*near0[:2])
    near1 = exchange(b1, "dp", 1), exchange(b1, "dp", 2)
    inner = after((*near0[:2], b1), far0)
    other0 = across_cores(*inner[:2], far0)
    other1 = exchange(inner[2], "ctx", 1)

    b0, b2, near1, seg = after((a0, a2, near1, seg), far0, other0, x_came)
    a3 = exchange(b0, "tensor", 3)
    far1 = far(*near1)
    near2 = exchange(b2, "dp", 1), exchange(b2, "dp", 2)
    inner = after((*near1, b2), far1)
    near1 = (*near1, other1)
    other1 = across_cores(*inner[:2], far1)
    other2 = exchange(inner[2], "ctx", 1)

    g0, b3, near2 = after((f0, a3, near2), far1, other1)
    w0 = gathered(g0)
    far2 = far(*near2)
    near3 = exchange(b3, "dp", 1), exchange(b3, "dp", 2)
    f1 = exchange(g0, "tensor", 1)
    f2 = exchange(g0, "tensor", 2)
    first0 = by_distance(a0, near0, other0[:2], far0, other0[2])
    first1 = by_distance(a1, near1, other1[:2], far1, other1[2])
    x = (layer_input, x_came)
    proj_a, *wa = run_project(me, x, first0, first1)
    inner = after((*near2, b3, far2), proj_a, near3)
    near2 = (*near2, other2)
    other2 = across_cores(*inner[:2], inner[3])
    other3 = exchange(inner[2], "ctx", 1)

    near3, late = after((near3, cotangent), far2, proj_a)
    far3 = far(*near3)
    ct = (cotangent, exchange(late, "ctx", 1))
    segrow = jnp.tile(seg.reshape(-1, 1, BLOCK), (1, 1, PAIR))
    seg = seg[:, None]
    states_a, mixed_a = run_mixer(me, proj_a, seg, segrow, wa[5], taps)
    f1, f2, far3, g0 = after((f1, f2, far3, f0), mixed_a)
    w12 = gathered(jnp.concatenate([f1, f2], axis=1))
    inner = after(near3, far3)
    near3 = (*near3, other3)
    other3 = across_cores(*inner, far3)
    first2 = by_distance(a2, near2, other2[:2], far2, other2[2])
    first3 = by_distance(a3, near3, other3[:2], far3, other3[2])
    proj_b, *wb = run_project(me, x, first2, first3)
    (g0,) = after((g0,), proj_b, ct)
    f3 = exchange(g0, "tensor", 3)

    projs, gains, smalls = (proj_a, proj_b), wa[4], (wa[5], wb[5])
    more = (x, mixed_a, gains, wa[2:4], wb[2:4])
    states_b, resid, nh, nl = run_mixer(me, proj_b, seg, segrow, wb[5], taps, more)
    n = (nh, nl)
    out, fng, feed_g = run_feed(me, n, ct, resid, resid, w0, 1, True)
    (f3,) = after((f3,), fng)
    w3 = gathered(f3)
    out, fng = run_feed(me, n, ct, out, fng, w12, 2, False)
    theirs, out_halves, fng = run_feed(me, n, ct, out, fng, w3, 1, False, True)
    feed_g = lax.psum_scatter(feed_g, plane, scatter_dimension=0, tiled=True)
    came = exchange(theirs, "ctx", 1)
    theirs, halves, keep, send = run_mixer_back(
        me, fng, resid, x, ct, projs, (states_a, states_b), mixed_a, seg, segrow, smalls, gains,
        wa[2:4], wb[2:4], wa[:2], wb[:2], taps,
    )
    layer_output = run_leave(me, out_halves, came)
    core = lax.axis_index("ctx")
    came_send = exchange(send, "ctx", 1)
    diagonal = keep[:, 3] + came_send[:, 3]
    keep, came_send = after((keep, came_send), diagonal)
    diagonal = corner(diagonal)
    came = exchange(theirs, "ctx", 1)
    to_own, to_x, to_y = (keep[:, i] + came_send[:, i] for i in range(3))
    diagonal, to_own, to_x, to_y, came = after((diagonal, to_own, to_x, to_y, came))
    came_x = exchange(jnp.where(core == 0, to_x + diagonal, to_x), "dp", 1)
    came_y = exchange(jnp.where(core == 0, to_y, to_y + diagonal), "dp", 2)
    input_grad = run_leave(me, halves, came)
    mixer_g = (to_own + came_x + came_y)[0]
    few_g, mixer_g = mixer_g[rows:], mixer_g[:rows]
    hidden = up_weight.shape[1]
    return (
        layer_output,
        input_grad,
        few_g[0, :rows],
        mixer_g[:, :own],
        mixer_g[:, own : 2 * own],
        mixer_g[:, 2 * own : 3 * own],
        few_g[2 : 2 + taps, :few],
        mixer_g[:, 3 * own :].T,
        few_g[1, :rows],
        feed_g[:, :hidden],
        feed_g[:, hidden:].T,
    )


def solution(mesh):
    shape = mesh.shape

    def chosen(*arrays):
        rows, length, model = arrays[0].shape
        heads, width = arrays[7].shape
        fits = (
            (shape["dp"], shape["ctx"], shape["tensor"]) == (4, 2, 4)
            and (rows, length) == (2, 2 * TILE)
            and PAIR * width == LANES
            and 2 * heads * width % LANES == 0
        )
        return (by_sequence if fits else on_device)(*arrays)

    return jax.shard_map(
        chosen,
        mesh=mesh,
        in_specs=(
            P("dp", "ctx", None),
            P("dp", "ctx"),
            P(("dp", "ctx")),
            P(("dp", "ctx"), "tensor"),
            P(("dp", "ctx"), "tensor"),
            P(("dp", "ctx"), "tensor"),
            P(None, ("tensor", "dp", "ctx")),
            P("tensor", None),
            P("tensor", ("dp", "ctx")),
            P(("dp", "ctx")),
            P(("dp", "ctx"), "tensor"),
            P("tensor", ("dp", "ctx")),
            P("dp", "ctx", None),
        ),
        out_specs=(
            P("dp", "ctx", None),
            P("dp", "ctx", None),
            P(("dp", "ctx")),
            P(("dp", "ctx"), "tensor"),
            P(("dp", "ctx"), "tensor"),
            P(("dp", "ctx"), "tensor"),
            P(None, ("tensor", "dp", "ctx")),
            P("tensor", ("dp", "ctx")),
            P(("dp", "ctx")),
            P(("dp", "ctx"), "tensor"),
            P("tensor", ("dp", "ctx")),
        ),
        check_vma=False,
    )
```

```python
from functools import partial

import jax
import jax.numpy as jnp
from jax import lax
from jax.experimental import pallas as pl
from jax.experimental.pallas import tpu as pltpu
from jax.sharding import PartitionSpec as P

SUBBLOCK = 64


eps = 1e-05
precise = lax.Precision.HIGHEST


def passed_along(value, axis, steps):
    count = lax.axis_size(axis)
    leading, last = (max(0, -steps), min(count, count - steps))
    return lax.ppermute(value, axis, [(source, source + steps) for source in range(leading, last)])


def carried_in(value, axis, join, neutral, backward):
    count, mine = (lax.axis_size(axis), lax.axis_index(axis))
    pieces = jax.tree.map(lambda part: lax.all_gather(part, axis), value)
    if backward:
        pieces = jax.tree.map(lambda part: part[::-1], pieces)
        mine = count - 1 - mine
    subtotal = jax.tree.map(
        lambda part, zero: jnp.full_like(part, 0) + jnp.asarray(zero, part.dtype), value, neutral
    )

    def step(position, subtotal):
        longer = join(subtotal, jax.tree.map(lambda part: part[position], pieces))
        return jax.tree.map(lambda new, old: jnp.where(position < mine, new, old), longer, subtotal)

    return lax.fori_loop(0, count - 1, step, subtotal)


def normalize(inputs, gain):
    centered = inputs - jnp.mean(inputs, axis=-1, keepdims=True)
    scaled = centered * lax.rsqrt(jnp.mean(centered * centered, axis=-1, keepdims=True) + eps)
    return scaled * gain


def project(left, right):
    return jnp.einsum(
        "btd,df->btf", left, right, precision=precise, preferred_element_type=jnp.float32
    )


def outer_sum(left, right):
    return jnp.einsum(
        "btd,btf->df", left, right, precision=precise, preferred_element_type=jnp.float32
    )


def smooth_gate(inputs):
    return jax.nn.gelu(inputs, approximate=True)


def shift_keys(extended, kernel, seg_ext):
    taps = kernel.shape[0]
    length = extended.shape[1] - taps + 1
    current = seg_ext[:, taps - 1 :]
    summed = jnp.zeros((extended.shape[0], length, extended.shape[2]), jnp.float32)
    for offset in range(taps):
        begin = taps - 1 - offset
        joined = (seg_ext[:, begin : begin + length] == current).astype(jnp.float32)
        summed = summed + kernel[offset] * extended[:, begin : begin + length] * joined[:, :, None]
    return summed


def compose(earlier, later):
    return (earlier[0] * later[0], later[0][..., None] * earlier[1] + later[1])


def geometry(segments, before_block, log_decay):
    rows, length = segments.shape
    pieces = length // SUBBLOCK
    grouped = segments.reshape(rows, pieces, SUBBLOCK)
    before = jnp.concatenate([before_block[:, None], grouped[:, :-1, -1]], axis=1)
    living = (grouped == before[:, :, None]).astype(jnp.float32)
    retained = (grouped == grouped[:, :, -1:]).astype(jnp.float32)
    position = jnp.arange(SUBBLOCK, dtype=jnp.float32)
    causal = position[:, None] >= position[None, :]
    allowed = jnp.logical_and(grouped[:, :, :, None] == grouped[:, :, None, :], causal).astype(
        jnp.float32
    )
    growing = jnp.exp(position[:, None, None] * log_decay)
    shrinking = jnp.exp(-position[:, None, None] * log_decay)
    step_in = growing * jnp.exp(log_decay)
    closing = jnp.exp((SUBBLOCK - 1.0 - position)[:, None, None] * log_decay)
    whole_decay = jnp.exp(SUBBLOCK * log_decay)[None, None] * living[:, :, -1][:, :, None, None]
    running = jnp.ones((rows,) + log_decay.shape, jnp.float32)
    carried = []
    for index in range(pieces):
        carried.append(running)
        running = running * whole_decay[:, index]
    return (
        living,
        retained,
        allowed,
        growing,
        shrinking,
        step_in,
        closing,
        whole_decay,
        jnp.stack(carried, axis=1),
        running,
    )


def local_part(queries, shifted, values, shape_info):
    (
        living,
        retained,
        allowed,
        growing,
        shrinking,
        step_in,
        closing,
        whole_decay,
        carried,
        block_decay,
    ) = shape_info
    scores = jnp.einsum(
        "bncgi,bnsgi->bngcs", queries * growing, shifted * shrinking, precision=precise
    )
    scores = scores * allowed[:, :, None]
    within = jnp.einsum("bngcs,bnsgj->bncgj", scores, values, precision=precise)
    update = jnp.einsum(
        "bncgi,bncgj->bngij",
        shifted * closing * retained[..., None, None],
        values,
        precision=precise,
    )
    running = jnp.zeros_like(update[:, 0])
    starts = []
    for index in range(update.shape[1]):
        starts.append(running)
        running = whole_decay[:, index][..., None] * running + update[:, index]
    return (within, jnp.stack(starts, axis=1), running)


def across(queries, starts, state_in, shape_info):
    (
        living,
        retained,
        allowed,
        growing,
        shrinking,
        step_in,
        closing,
        whole_decay,
        carried,
        block_decay,
    ) = shape_info
    entries = starts + carried[..., None] * state_in[:, None]
    weighted = queries * step_in * living[..., None, None]
    return jnp.einsum("bncgi,bngij->bncgj", weighted, entries, precision=precise)


def on_device(
    layer_input,
    segment_ids,
    mixer_gain,
    query_weight,
    key_weight,
    value_weight,
    shift_kernel,
    state_decay,
    mixer_weight,
    feed_gain,
    up_weight,
    down_weight,
    cotangent,
):
    (
        mixer_gain_all,
        query_all,
        key_all,
        value_all,
        kernel_all,
        mixer_all,
        feed_gain_all,
        up_all,
        down_all,
    ) = (
        lax.all_gather(mixer_gain, ("dp", "ctx"), axis=0, tiled=True),
        lax.all_gather(query_weight, ("dp", "ctx"), axis=0, tiled=True),
        lax.all_gather(key_weight, ("dp", "ctx"), axis=0, tiled=True),
        lax.all_gather(value_weight, ("dp", "ctx"), axis=0, tiled=True),
        lax.all_gather(shift_kernel, ("dp", "ctx"), axis=1, tiled=True),
        lax.all_gather(mixer_weight, ("dp", "ctx"), axis=1, tiled=True),
        lax.all_gather(feed_gain, ("dp", "ctx"), axis=0, tiled=True),
        lax.all_gather(up_weight, ("dp", "ctx"), axis=0, tiled=True),
        lax.all_gather(down_weight, ("dp", "ctx"), axis=1, tiled=True),
    )
    heads, width = state_decay.shape
    log_decay = jnp.log(state_decay)
    taps = kernel_all.shape[0]
    rows, length, model = layer_input.shape
    pieces = length // SUBBLOCK
    features = heads * width
    seg_float = segment_ids.astype(jnp.float32)
    joint_weight = jnp.concatenate([query_all, key_all, value_all], axis=1)
    normed = normalize(layer_input, mixer_gain_all)
    projected = project(normed, joint_weight)
    queries = projected[:, :, :features]
    keys_raw = projected[:, :, features : 2 * features]
    values = projected[:, :, 2 * features :]
    tail_keys, tail_segs = passed_along(
        (keys_raw[:, length - taps + 1 :], seg_float[:, length - taps + 1 :]), "ctx", 1
    )
    extended = jnp.concatenate([tail_keys, keys_raw], axis=1)
    seg_ext = jnp.concatenate([tail_segs, seg_float], axis=1)
    shift_fixed = partial(shift_keys, seg_ext=seg_ext)
    shifted = shift_fixed(extended, kernel_all)
    info = geometry(seg_float, tail_segs[:, -1], log_decay)
    block_decay = info[-1]
    head_q = queries.reshape(rows, pieces, SUBBLOCK, heads, width)
    head_k = shifted.reshape(rows, pieces, SUBBLOCK, heads, width)
    head_v = values.reshape(rows, pieces, SUBBLOCK, heads, width)
    within, starts, local_end = local_part(head_q, head_k, head_v, info)
    identity = (jnp.ones_like(block_decay), jnp.zeros_like(local_end))
    state_in = carried_in((block_decay, local_end), "ctx", compose, identity, False)[1]
    mixed = (within + across(head_q, starts, state_in, info)).reshape(rows, length, features)
    branch = lax.psum(project(mixed, mixer_all), "tensor")
    resid = layer_input + branch
    normed_feed = normalize(resid, feed_gain_all)
    pre_act = project(normed_feed, up_all)
    activated, gelu_back = jax.vjp(smooth_gate, pre_act)
    feed = lax.psum(project(activated, down_all), "tensor")
    layer_output = resid + feed
    act_grad = project(cotangent, down_all.T)
    down_grad = outer_sum(activated, cotangent)
    (pre_grad,) = gelu_back(act_grad)
    up_grad = outer_sum(normed_feed, pre_grad)
    feed_normed_grad = lax.psum(project(pre_grad, up_all.T), "tensor")
    _, feed_norm_back = jax.vjp(normalize, resid, feed_gain_all)
    resid_ln_grad, feed_gain_grad = feed_norm_back(feed_normed_grad)
    resid_grad = cotangent + resid_ln_grad
    mixed_grad = project(resid_grad, mixer_all.T)
    mixer_weight_grad = outer_sum(mixed, resid_grad)
    head_du = mixed_grad.reshape(rows, pieces, SUBBLOCK, heads, width)
    (
        living,
        retained,
        allowed,
        growing,
        shrinking,
        step_in,
        closing,
        whole_decay,
        carried,
        block_decay,
    ) = info
    own_grad = jnp.einsum(
        "bncgi,bncgj,bngi->bgij",
        head_q * step_in * living[..., None, None],
        head_du,
        carried,
        precision=precise,
    )
    identity_grad = (jnp.ones_like(block_decay), jnp.zeros_like(own_grad))
    after = carried_in((block_decay, own_grad), "ctx", compose, identity_grad, True)[1]

    def mixer_full(query_in, key_in, value_in, entering):
        inner, begins, ending = local_part(query_in, key_in, value_in, info)
        output = inner + across(query_in, begins, entering, info)
        return (output, ending + block_decay[..., None] * entering)

    _, mixer_vjp = jax.vjp(mixer_full, head_q, head_k, head_v, state_in)
    query_act_grad, shifted_grad, value_act_grad, _ = mixer_vjp((head_du, after))
    _, shift_back = jax.vjp(shift_fixed, extended, kernel_all)
    ext_grad, kernel_grad = shift_back(shifted_grad.reshape(rows, length, features))
    returned = passed_along(ext_grad[:, : taps - 1], "ctx", -1)
    key_act_grad = ext_grad[:, taps - 1 :] + jnp.pad(
        returned, ((0, 0), (length - taps + 1, 0), (0, 0))
    )
    joint_grad = jnp.concatenate(
        [
            query_act_grad.reshape(rows, length, features),
            key_act_grad,
            value_act_grad.reshape(rows, length, features),
        ],
        axis=2,
    )
    joint_weight_grad = outer_sum(normed, joint_grad)
    normed_grad = lax.psum(project(joint_grad, joint_weight.T), "tensor")
    _, mixer_norm_back = jax.vjp(normalize, layer_input, mixer_gain_all)
    input_ln_grad, mixer_gain_grad = mixer_norm_back(normed_grad)
    input_grad = resid_grad + input_ln_grad
    query_grad = joint_weight_grad[:, :features]
    key_grad = joint_weight_grad[:, features : 2 * features]
    value_grad = joint_weight_grad[:, 2 * features :]
    all_parts = tuple(
        (
            lax.psum_scatter(mixer_gain_grad, ("dp", "ctx"), scatter_dimension=0, tiled=True),
            lax.psum_scatter(query_grad, ("dp", "ctx"), scatter_dimension=0, tiled=True),
            lax.psum_scatter(key_grad, ("dp", "ctx"), scatter_dimension=0, tiled=True),
            lax.psum_scatter(value_grad, ("dp", "ctx"), scatter_dimension=0, tiled=True),
            lax.psum_scatter(kernel_grad, ("dp", "ctx"), scatter_dimension=1, tiled=True),
            lax.psum_scatter(mixer_weight_grad, ("dp", "ctx"), scatter_dimension=1, tiled=True),
            lax.psum_scatter(feed_gain_grad, ("dp", "ctx"), scatter_dimension=0, tiled=True),
            lax.psum_scatter(up_grad, ("dp", "ctx"), scatter_dimension=0, tiled=True),
            lax.psum_scatter(down_grad, ("dp", "ctx"), scatter_dimension=1, tiled=True),
        )
    )
    return (layer_output, input_grad) + all_parts


PAIR = 2
BLOCK = 128
LANES = 128
LIMIT = 63
TILE = 256
C_GELU = 0.7978845608028654
NN = ((1,), (0,))
NT = ((1,), (1,))
TN = ((0,), (0,))
f32, bf16 = jnp.float32, jnp.bfloat16


def params(limit=LIMIT):
    return pltpu.CompilerParams(vmem_limit_bytes=limit * 2**20)


def cost(flops, moved):
    return pl.CostEstimate(flops=int(flops), bytes_accessed=int(moved), transcendentals=0)


def shaped(shape, dtype=jnp.float32):
    return jax.ShapeDtypeStruct(shape, dtype)


def split(a):
    high = a.astype(bf16)
    return high, (a - high.astype(f32)).astype(bf16)


def d3(left, right, dims):
    dot = partial(lax.dot_general, dimension_numbers=(dims, ((), ())), preferred_element_type=f32)
    if dims == TN:
        joined_left = jnp.concatenate([left[0], left[1], left[0]], axis=0)
        return dot(joined_left, jnp.concatenate([right[0], right[0], right[1]], axis=0))
    rows = left[0].shape[0]
    both = dot(jnp.concatenate(left, axis=0), right[0])
    return both[:rows] + both[rows:] + dot(left[0], right[1])


def tied(arrays):
    specs = [
        pl.BlockSpec((1,) * (a.ndim - 2) + (8, 128), lambda *_, n=a.ndim: (0,) * n) for a in arrays
    ]
    return specs, list(arrays)


def norm_parts(v):
    centered = v - jnp.mean(v, axis=-1, keepdims=True)
    r = lax.rsqrt(jnp.mean(centered * centered, axis=-1, keepdims=True) + eps)
    return centered * r, r


def whole(shape):
    return pl.BlockSpec(
        shape, lambda *_: (0,) * len(shape), pipeline_mode=pl.Buffered(buffer_count=1)
    )


def scalar():
    return pl.BlockSpec(memory_space=pltpu.SMEM)


def pack_mixer_kernel(me_ref, q_ref, k_ref, v_ref, m_ref, mg_ref, fg_ref, kern_ref, decay_ref, o_ref):
    rows, own = q_ref.shape
    taps, few = kern_ref.shape
    heads, width = decay_ref.shape
    o_ref[0:rows, 0:own] = q_ref[...]
    o_ref[0:rows, own : 2 * own] = k_ref[...]
    o_ref[0:rows, 2 * own : 3 * own] = v_ref[...]
    o_ref[0:rows, 3 * own :] = jnp.transpose(m_ref[...])
    o_ref[rows:, :] = jnp.zeros((8, o_ref.shape[1]), f32)
    for b in range(8):

        @pl.when(me_ref[0] == b)
        def _():
            o_ref[rows : rows + 1, b * rows : (b + 1) * rows] = mg_ref[...]
            o_ref[rows + 1 : rows + 2, b * rows : (b + 1) * rows] = fg_ref[...]
            o_ref[rows + 2 : rows + 2 + taps, b * few : (b + 1) * few] = kern_ref[...]

    @pl.when(me_ref[0] == 0)
    def _():
        for h in range(heads):
            at = rows + 2 + taps
            o_ref[at : at + 1, h * width : (h + 1) * width] = decay_ref[h : h + 1, :]


def run_pack_mixer(me, q, k, v, m, mg, fg, kern, decay):
    rows, own = q.shape
    args = (q, k, v, m, mg[None], fg[None], kern, decay)
    return pl.pallas_call(
        pack_mixer_kernel,
        grid=(1,),
        in_specs=[scalar()] + [whole(a.shape) for a in args],
        out_specs=whole((rows + 8, 4 * own)),
        out_shape=shaped((rows + 8, 4 * own)),
        compiler_params=params(),
        cost_estimate=cost(1e6, 2**20),
        name="pack_mixer",
    )(me, *args)


def pack_feed_kernel(up_ref, down_ref, o_ref):
    hidden = up_ref.shape[1]
    o_ref[:, :hidden] = up_ref[...]
    o_ref[:, hidden:] = jnp.transpose(down_ref[...])


def run_pack_feed(up, down):
    return pl.pallas_call(
        pack_feed_kernel,
        grid=(1,),
        in_specs=[whole(up.shape), whole(down.shape)],
        out_specs=whole((up.shape[0], 2 * up.shape[1])),
        out_shape=shaped((up.shape[0], 2 * up.shape[1])),
        compiler_params=params(),
        cost_estimate=cost(1e6, 2 * 2**20),
        name="pack_feed",
    )(up, down)


def sequence_specs(model, order):
    def mine(i, m):
        return (m[0] & 1, order(i, m) % 2, 0)

    return [pl.BlockSpec((1, TILE, model), mine)] * 2


def sequence_tile(tile, me_ref, mine_ref, came_ref):
    own = tile // 2 == (me_ref[0] & 1)
    return jnp.where(own, mine_ref[0], came_ref[0])


def project_kernel(me_ref, x_ref, xr_ref, *refs):
    first, second = refs[0:8], refs[8:16]
    o_ref, wh_ref, wl_ref, mh_ref, ml_ref, gains_ref, small_ref = refs[-7:]
    own = first[0].shape[1] // 4
    rows = wh_ref.shape[0] // 8

    @pl.when(pl.program_id(0) == 0)
    def _():
        for r in range(8):
            at = pl.ds(pl.multiple_of((me_ref[0] ^ r) * rows, rows), rows)
            a, b = first[r][0:rows, :], second[r][0:rows, :]
            for i in range(4):
                both = jnp.concatenate(
                    [a[:, i * own : (i + 1) * own], b[:, i * own : (i + 1) * own]], axis=1
                )
                high, low = split(both)
                if i < 3:
                    wh_ref[at, i * 2 * own : (i + 1) * 2 * own] = high
                    wl_ref[at, i * 2 * own : (i + 1) * 2 * own] = low
                else:
                    mh_ref[at, :] = high
                    ml_ref[at, :] = low
        sums = []
        for pieces in (first, second):
            total = pieces[0][rows:, :]
            for r in range(1, 8):
                total = total + pieces[r][rows:, :]
            sums.append(total)
        gains_ref[...] = sums[0]
        small_ref[...] = jnp.concatenate([s[:, :own] for s in sums], axis=1)

    x = sequence_tile(pl.program_id(0), me_ref, x_ref, xr_ref)
    n = split(norm_parts(x)[0] * gains_ref[0:1, :])
    o_ref[...] = d3(n, (wh_ref[...], wl_ref[...]), NN)


def run_project(me, x, first, second, ties=()):
    rows, half, model = x[0].shape
    tokens = rows * half
    own = first[0].shape[1] // 4
    wide = 6 * own
    piece = whole(first[0].shape)
    weights = [(model, wide)] * 2 + [(model, 2 * own)] * 2
    few = [(8, model), (8, 2 * own)]
    tie_specs, tie_args = tied(ties)
    return pl.pallas_call(
        project_kernel,
        grid_spec=pltpu.PrefetchScalarGridSpec(
            num_scalar_prefetch=1,
            grid=(tokens // TILE,),
            in_specs=sequence_specs(model, lambda i, m: i) + [piece] * 16 + tie_specs,
            out_specs=[pl.BlockSpec((TILE, wide), lambda i, m: (i, 0))]
            + [whole(s) for s in weights + few],
        ),
        out_shape=[shaped((tokens, wide))]
        + [shaped(s, bf16) for s in weights]
        + [shaped(s) for s in few],
        compiler_params=params(),
        cost_estimate=cost(6 * tokens * model * wide, 20 * 2**20),
        name="project",
    )(me, *x, *first, *second, *tie_args)


def spread(parts, masks):
    return tuple(jnp.concatenate([p * m for m in masks], axis=0) for p in parts)


def lane_masks(lanes):
    which = lax.broadcasted_iota(jnp.int32, (1, lanes), 1) // (lanes // PAIR)
    return [jnp.where(which == h, 1.0, 0.0).astype(bf16) for h in range(PAIR)]


def square_mask(lanes):
    a = lax.broadcasted_iota(jnp.int32, (lanes, lanes), 0) // (lanes // PAIR)
    b = lax.broadcasted_iota(jnp.int32, (lanes, lanes), 1) // (lanes // PAIR)
    return jnp.where(a == b, 1.0, 0.0)


def fill_tables(decay, grow, shrink, dec, end, full):
    size, model = grow.shape
    lanes = dec.shape[0]
    rates = jnp.log(decay)
    position = lax.broadcasted_iota(jnp.int32, (size, model), 0).astype(f32)
    grow[...] = jnp.exp(position * rates)
    shrink[...] = jnp.exp(-position * rates)
    for p in range(model // lanes):
        s = slice(p * lanes, (p + 1) * lanes)
        column = jnp.transpose(jnp.broadcast_to(rates[:, s], (lanes, lanes)))
        dec[:, s] = jnp.exp(column)
        end[:, s] = jnp.exp((size - 1.0) * column)
        full[:, s] = jnp.exp(float(size) * column)


def joined(extended, size, taps):
    now = extended[8:]
    return [jnp.where(extended[8 - j : 8 - j + size] == now, 1.0, 0.0) for j in range(1, taps)]


def shift_forward(keys, before, kern, same, taps):
    extended = jnp.concatenate([before, keys], axis=0)
    size = keys.shape[0]
    moved = [keys]
    for j in range(1, taps):
        moved.append(extended[8 - j : 8 - j + size] * same[j - 1])
    total = kern[0:1, :] * keys
    for j in range(1, taps):
        total = total + kern[j : j + 1, :] * moved[j]
    return total, moved


def allowed_masks(seg, row):
    size, wide = seg.shape[0], row.shape[1]
    rows = lax.broadcasted_iota(jnp.int32, (size, wide), 0)
    cols = lax.broadcasted_iota(jnp.int32, (size, wide), 1) % size
    same = seg == row
    return (
        jnp.where(jnp.logical_and(rows >= cols, same), 1.0, 0.0),
        jnp.where(jnp.logical_and(rows <= cols, same), 1.0, 0.0),
    )


def pair(a_ref, b_ref):
    return jnp.concatenate([a_ref[...], b_ref[...]], axis=1)


def third_of(refs, rows, i):
    wide = refs[0].shape[1] // 3
    return jnp.concatenate([r[rows, i * wide : (i + 1) * wide] for r in refs], axis=1)


def mixer_kernel(taps, last, me_ref, proj_ref, seg_ref, segrow_ref, small_ref, *refs):
    if last:
        x_ref, xr_ref, other_ref, gains_ref, ah_ref, al_ref, bh_ref, bl_ref = refs[:8]
        state_out_ref, resid_ref, nh_ref, nl_ref = refs[8:12]
    else:
        state_out_ref, mixed_ref = refs[:2]
    state, tail, segtail, grow, shrink, dec, end, full, mixed = refs[-9:]
    size, lanes = grow.shape[0], dec.shape[0]
    projs = (proj_ref,)

    @pl.when(pl.program_id(0) == 0)
    def _():
        state[...] = jnp.zeros_like(state)
        tail[...] = jnp.zeros_like(tail)
        segtail[...] = jnp.full_like(segtail, -1.0)
        fill_tables(small_ref[2 + taps : 3 + taps], grow, shrink, dec, end, full)

    kern = small_ref[2 : 2 + taps]
    masks = lane_masks(lanes)
    square = square_mask(lanes)
    groups = [slice(g * lanes, (g + 1) * lanes) for g in range(state.shape[1] // lanes)]
    before_keys, before = tail[...], segtail[...]
    for chunk in range(proj_ref.shape[0] // size):
        here = slice(chunk * size, (chunk + 1) * size)
        seg = seg_ref[here, :]
        extended = jnp.concatenate([before, seg], axis=0)
        living = jnp.where(seg == before[7:8], 1.0, 0.0)
        kept = jnp.where(seg == seg[size - 1 :], 1.0, 0.0)
        goes_on = living[size - 1 :]
        q_all, keys, v_all = (third_of(projs, here, i) for i in range(3))
        shifted, _ = shift_forward(keys, before_keys, kern, joined(extended, size, taps), taps)
        before_keys, before = keys[size - 8 :, :], seg[size - 8 :]
        allowed, _ = allowed_masks(seg, segrow_ref[chunk])
        state_out_ref[chunk] = state[...]
        qg, kf, v, scores = [], [], [], []
        for s in groups:
            qg.append(split(q_all[:, s] * grow[:, s]))
            kf.append(shifted[:, s] * shrink[:, s])
            v.append(split(v_all[:, s]))
            scores.append(d3(qg[-1], spread(split(kf[-1]), masks), NT))
        updates = [d3(split(k * kept), w, TN) * square for k, w in zip(kf, v)]
        weights = [split(score * allowed) for score in scores]
        for g, s in enumerate(groups):
            part = d3(weights[g], spread(v[g], masks), NN)
            mixed[here, s] = part + living * d3(qg[g], split(state[:, s] * dec[:, s]), NN)
        for g, s in enumerate(groups):
            state[:, s] = state[:, s] * (full[:, s] * goes_on) + end[:, s] * updates[g]
    tail[...] = before_keys
    segtail[...] = before
    if not last:
        mixed_ref[...] = mixed[...]
        return
    resid = (
        sequence_tile(pl.program_id(0), me_ref, x_ref, xr_ref)
        + d3(split(other_ref[...]), (ah_ref[...], al_ref[...]), NT)
        + d3(split(mixed[...]), (bh_ref[...], bl_ref[...]), NT)
    )
    resid_ref[...] = resid
    nh_ref[...], nl_ref[...] = split(norm_parts(resid)[0] * gains_ref[1:2, :])


def mixer_scratch(model):
    return [pltpu.VMEM((BLOCK, model), f32)] * 2 + [pltpu.VMEM((LANES, model), f32)] * 3


def run_mixer(me, proj, seg, segrow, small, taps, more=(), ties=()):
    tokens, third = proj.shape[0], proj.shape[1] // 3
    chunks = TILE // BLOCK

    def row(width):
        return pl.BlockSpec((TILE, width), lambda c, m: (c, 0))

    extra_specs, extra = [], []
    outs = [(row(third), shaped((tokens, third)))]
    if more:
        x, other, gains, a, b = more
        model = x[0].shape[2]
        extra_specs = sequence_specs(model, lambda i, m: i) + [row(third), whole(gains.shape)]
        extra_specs = extra_specs + [whole(a[0].shape)] * 4
        extra = [*x, other, gains, *a, *b]
        outs = [(row(model), shaped((tokens, model), t)) for t in (f32, bf16, bf16)]
    states = pl.BlockSpec((chunks, LANES, third), lambda c, m: (c, 0, 0))
    tie_specs, tie_args = tied(ties)
    return pl.pallas_call(
        partial(mixer_kernel, taps, bool(more)),
        grid_spec=pltpu.PrefetchScalarGridSpec(
            num_scalar_prefetch=1,
            grid=(tokens // TILE,),
            in_specs=[
                row(3 * third),
                row(1),
                pl.BlockSpec((chunks, 1, segrow.shape[2]), lambda c, m: (c, 0, 0)),
                whole(small.shape),
            ]
            + extra_specs
            + tie_specs,
            out_specs=[states] + [spec for spec, _ in outs],
            scratch_shapes=[
                pltpu.VMEM((LANES, third), f32),
                pltpu.VMEM((8, third), f32),
                pltpu.VMEM((8, 1), f32),
            ]
            + mixer_scratch(third)
            + [pltpu.VMEM((TILE, third), f32)],
        ),
        out_shape=[shaped((tokens // BLOCK, LANES, third))] + [shape for _, shape in outs],
        compiler_params=params(),
        cost_estimate=cost(6e9 + (7e9 if more else 0), 10 * 2**20),
        name="mixer_out" if more else "mixer",
    )(me, proj, seg, segrow, small, *extra, *tie_args)


def mixer_back_kernel(
    taps, me_ref, fng_ref, resid_ref, x_ref, xr_ref, ct_ref, cr_ref, pa_ref, pb_ref, ba_ref, bb_ref,
    ta_ref, tb_ref, mixed_ref, seg_ref, segb_ref, segrow_ref, sa_ref, sb_ref, gains_ref,
    ah_ref, al_ref, bh_ref, bl_ref, qah_ref, qal_ref, qbh_ref, qbl_ref, *refs,
):
    (
        theirs_ref, ig_ref, keep_ref, send_ref, gg, g2, dkern,
        grad, head, grow, shrink, dec, end, full, du_all, da, db, wg,
    ) = refs[-18:]
    size, lanes = grow.shape[0], dec.shape[0]
    step, steps = pl.program_id(0), pl.num_programs(0)
    projs = (pa_ref, pb_ref)

    @pl.when(step == 0)
    def _():
        grad[...] = jnp.zeros_like(grad)
        head[...] = jnp.zeros_like(head)
        dkern[...] = jnp.zeros_like(dkern)
        gg[...] = jnp.zeros_like(gg)
        g2[...] = jnp.zeros_like(g2)
        wg[...] = jnp.zeros_like(wg)
        fill_tables(pair(sa_ref, sb_ref)[2 + taps : 3 + taps], grow, shrink, dec, end, full)

    third = ah_ref.shape[1]
    tile = steps - 1 - step
    back, gain_grad, _ = norm_back(resid_ref[...], gains_ref[1:2, :], fng_ref[...])
    rg = sequence_tile(tile, me_ref, ct_ref, cr_ref) + back
    g2[...] += gain_grad
    r2 = split(rg)
    du_all[:, :third] = d3(r2, (ah_ref[...], al_ref[...]), NN)
    du_all[:, third:] = d3(r2, (bh_ref[...], bl_ref[...]), NN)

    kern = pair(sa_ref, sb_ref)[2 : 2 + taps]
    masks = lane_masks(lanes)
    square = square_mask(lanes)
    model = grad.shape[1]
    groups = [slice(g * lanes, (g + 1) * lanes) for g in range(model // lanes)]
    count = len(groups)
    chunks = rg.shape[0] // size
    for chunk in reversed(range(chunks)):
        here = slice(chunk * size, (chunk + 1) * size)
        seg = seg_ref[here, :]
        q_all, keys, v_all = (third_of(projs, here, i) for i in range(3))
        if chunk:
            just = slice(chunk * size - 8, chunk * size)
            before, before_keys = seg_ref[just, :], third_of(projs, just, 1)
        else:
            before = jnp.where(step == steps - 1, -1.0, segb_ref[...])
            before_keys = pair(ba_ref, bb_ref)
        extended = jnp.concatenate([before, seg], axis=0)
        living = jnp.where(seg == before[7:8], 1.0, 0.0)
        kept = jnp.where(seg == seg[size - 1 :], 1.0, 0.0)
        goes_on = living[size - 1 :]
        same = joined(extended, size, taps)
        shifted, moved = shift_forward(keys, before_keys, kern, same, taps)
        allowed, allowed_t = allowed_masks(seg, segrow_ref[chunk])
        qf = [q_all[:, s] * grow[:, s] for s in groups]
        qg = [split(q) for q in qf]
        kg = [split(shifted[:, s] * shrink[:, s]) for s in groups]
        v = [split(v_all[:, s]) for s in groups]
        du = [split(du_all[here, s]) for s in groups]
        p_t = [d3(kg[g], spread(qg[g], masks), NT) for g in range(count)]
        dp = [d3(du[g], spread(v[g], masks), NT) for g in range(count)]
        dp_t = [d3(v[g], spread(du[g], masks), NT) for g in range(count)]
        updates = [d3(split(qf[g] * living), du[g], TN) * square for g in range(count)]
        p_t = [split(p * allowed_t) for p in p_t]
        dp = [split(p * allowed) for p in dp]
        dp_t = [split(p * allowed_t) for p in dp_t]
        for g, s in enumerate(groups):
            first = s.start < third
            at = s.start - (0 if first else third)
            to = da if first else db
            states = (ta_ref if first else tb_ref)[chunk, :, at : at + lanes]
            entering = split(states * dec[:, s])
            leaving = split(grad[:, s] * end[:, s])
            dqg = d3(dp[g], spread(kg[g], masks), NN) + living * d3(du[g], entering, NT)
            dkg = d3(dp_t[g], spread(qg[g], masks), NN) + kept * d3(v[g], leaving, NT)
            dv = d3(p_t[g], spread(du[g], masks), NN) + kept * d3(kg[g], leaving, NN)
            to[here, 2 * third + at : 2 * third + at + lanes] = dv
            to[here, at : at + lanes] = dqg * grow[:, s]
            dshift = dkg * shrink[:, s]
            grad[:, s] = grad[:, s] * (full[:, s] * goes_on) + dec[:, s] * updates[g]
            total = kern[0:1, s] * dshift
            for j in range(1, taps):
                part = dshift * same[j - 1]
                longer = jnp.concatenate([part, head[j - 1, :, s]], axis=0)
                total = total + kern[j : j + 1, s] * longer[j : j + size]
                head[j - 1, :, s] = part[0:8]
            to[here, third + at : third + at + lanes] = total
            if g < 2:
                for j in range(taps):
                    dkern[j : j + 1, s] += jnp.sum(
                        dshift * moved[j][:, s], axis=0, keepdims=True
                    )

    own = keep_ref.shape[-1] // 4
    x = sequence_tile(tile, me_ref, x_ref, xr_ref)
    left, right = split(da[...]), split(db[...])
    incoming = d3(left, (qah_ref[...], qal_ref[...]), NT)
    incoming = incoming + d3(right, (qbh_ref[...], qbl_ref[...]), NT)
    back, gain_grad, xhat = norm_back(x, gains_ref[0:1, :], incoming)
    ig_ref[0] = rg + back
    gg[...] += gain_grad
    n = split(xhat * gains_ref[0:1, :])
    joint = tuple(
        jnp.concatenate([p[:, i * third : i * third + own] for i in range(3)], axis=1) for p in left
    )
    wg[:, : 3 * own] += d3(n, joint, TN)
    wg[:, 3 * own :] += d3(r2, split(mixed_ref[:, :own]), TN)

    @pl.when(tile // 2 != (me_ref[0] & 1))
    def _():
        theirs_ref[...] = ig_ref[0]

    @pl.when(step == steps - 1)
    def _():
        few = (gg[...], g2[...], dkern[:, :own])
        store_blocks(me_ref[0], wg, few, keep_ref, send_ref)


def run_mixer_back(
    me, fng, resid, x, ct, projs, states, mixed, seg, segrow, smalls, gains, a, b, qa, qb, taps
):
    tokens, model = resid.shape
    third = projs[0].shape[1] // 3
    own = third // 2
    chunks = TILE // BLOCK
    last = tokens // TILE - 1
    blocks = (1, 4, model // 8 + 8, 4 * own)

    def prior(c):
        return jnp.maximum((last - c) * (TILE // 8) - 1, 0)

    row = pl.BlockSpec((TILE, model), lambda c, m: (last - c, 0))
    proj = pl.BlockSpec((TILE, 3 * third), lambda c, m: (last - c, 0))
    before = pl.BlockSpec((8, third), lambda c, m: (prior(c), 1))
    state = pl.BlockSpec((chunks, LANES, third), lambda c, m: (last - c, 0, 0))
    halves = pl.BlockSpec((1, TILE, model), lambda c, m: ((last - c) // 2, (last - c) % 2, 0))

    def for_other(c, m):
        core, tile = m[0] & 1, last - c
        return (jnp.where(tile // 2 == 1 - core, tile % 2, core), 0)

    theirs = pl.BlockSpec((TILE, model), for_other)
    return pl.pallas_call(
        partial(mixer_back_kernel, taps),
        grid_spec=pltpu.PrefetchScalarGridSpec(
            num_scalar_prefetch=1,
            grid=(last + 1,),
            in_specs=[row, row]
            + sequence_specs(model, lambda c, m: last - c) * 2
            + [proj, proj, before, before, state, state]
            + [
                pl.BlockSpec((TILE, third), lambda c, m: (last - c, 0)),
                pl.BlockSpec((TILE, 1), lambda c, m: (last - c, 0)),
                pl.BlockSpec((8, 1), lambda c, m: (prior(c), 0)),
                pl.BlockSpec((chunks, 1, segrow.shape[2]), lambda c, m: (last - c, 0, 0)),
                whole(smalls[0].shape),
                whole(smalls[1].shape),
                whole(gains.shape),
            ]
            + [whole(a[0].shape)] * 4
            + [whole(qa[0].shape)] * 4,
            out_specs=[theirs, halves, whole(blocks), whole(blocks)],
            scratch_shapes=[
                pltpu.VMEM((1, model), f32),
                pltpu.VMEM((1, model), f32),
                pltpu.VMEM((taps, model), f32),
                pltpu.VMEM((LANES, model), f32),
                pltpu.VMEM((taps - 1, 8, model), f32),
            ]
            + mixer_scratch(model)
            + [pltpu.VMEM((TILE, model), f32)]
            + [pltpu.VMEM((TILE, 3 * third), f32)] * 2
            + [pltpu.VMEM((model, 4 * own), f32)],
        ),
        out_shape=[shaped((tokens // 2, model)), shaped((2, tokens // 2, model))]
        + [shaped(blocks), shaped(blocks)],
        compiler_params=params(),
        cost_estimate=cost(1e11, 60 * 2**20),
        name="mixer_back",
    )(
        me, fng, resid, *x, *ct, *projs, *projs, *states, mixed, seg, seg, segrow, *smalls, gains,
        *a, *b, *qa, *qb,
    )


def gelu_parts(pre, back):
    th = jnp.tanh(pre * (C_GELU + (C_GELU * 0.044715) * (pre * pre)))
    half = 0.5 + 0.5 * th
    act = pre * half
    slope = half + (1.0 - th) * act * (C_GELU + (3 * C_GELU * 0.044715) * (pre * pre))
    return act, back * slope


def store_blocks(me, g, few, keep_ref, send_ref):
    rows = g.shape[0] // 8
    for b in range(8):
        r = me ^ b
        where = r // 2
        short = [f[:, b * (f.shape[1] // 8) : (b + 1) * (f.shape[1] // 8)] for f in few]

        def put(ref):
            ref[0, where, 0:rows, :] = g[b * rows : (b + 1) * rows]
            ref[0, where, rows:, :] = jnp.zeros((ref.shape[2] - rows, ref.shape[3]), f32)
            at = rows
            for part in short:
                ref[0, where, at : at + part.shape[0], 0 : part.shape[1]] = part
                at = at + part.shape[0]

        @pl.when((r & 1) == 0)
        def _():
            put(keep_ref)

        @pl.when((r & 1) == 1)
        def _():
            put(send_ref)


def feed_kernel(own, slots, final, me_ref, nh_ref, nl_ref, ct_ref, cr_ref, out_in, fng_in, w_in, *refs):
    if own:
        out_ref, fng_ref, wg, w = refs[-4:]
    else:
        out_ref, fng_ref, w = refs[-3:]
    step = pl.program_id(0)
    hidden = w.shape[2] // (2 * slots)

    @pl.when(step == 0)
    def _():
        w[0], w[1] = split(w_in[...])
        if own:
            wg[...] = jnp.zeros_like(wg)

    tile = theirs_first(step, me_ref)
    n = (nh_ref[...], nl_ref[...])
    ct = split(sequence_tile(tile, me_ref, ct_ref, cr_ref))
    out, fng = out_in[...], None if own else fng_in[...]
    for t in range(slots):
        a, b = (slice((2 * t + i) * hidden, (2 * t + i + 1) * hidden) for i in range(2))
        u, d = (w[0, :, a], w[1, :, a]), (w[0, :, b], w[1, :, b])
        act, grad = gelu_parts(d3(n, u, NN), d3(ct, d, NN))
        act, grad = split(act), split(grad)
        out = out + d3(act, d, NT)
        more = d3(grad, u, NT)
        fng = more if fng is None else fng + more
    out_ref[...] = out.reshape(out_ref.shape)
    fng_ref[...] = fng
    if own:
        wg[:, :hidden] += d3(n, grad, TN)
        wg[:, hidden:] += d3(ct, act, TN)
    if final:

        @pl.when(step < 2)
        def _():
            refs[0][...] = out_ref[0]


def theirs_first(step, me):
    core = me[0] & 1
    return jnp.where(step < 2, 1 - core, core) * 2 + (step & 1)


def run_feed(me, n, ct, out, fng, w, slots, own, final=False):
    tokens, model = n[0].shape
    wide = w.shape[1]
    row = pl.BlockSpec((TILE, model), lambda i, m: (theirs_first(i, m), 0))
    full = shaped((tokens, model))
    last = pl.BlockSpec((1, TILE, model), lambda i, m: (theirs_first(i, m) // 2, i % 2, 0))
    theirs = pl.BlockSpec((TILE, model), lambda i, m: (jnp.minimum(i, 1), 0))
    return pl.pallas_call(
        partial(feed_kernel, own, slots, final),
        grid_spec=pltpu.PrefetchScalarGridSpec(
            num_scalar_prefetch=1,
            grid=(tokens // TILE,),
            in_specs=[row] * 2
            + sequence_specs(model, theirs_first)
            + [row] * 2
            + [whole(w.shape)],
            out_specs=[theirs] * final
            + [last if final else row, row]
            + ([whole((model, wide))] if own else []),
            scratch_shapes=[pltpu.VMEM((2, model, wide), bf16)],
        ),
        out_shape=[shaped((tokens // 2, model))] * final
        + [shaped((2, tokens // 2, model)) if final else full, full]
        + ([shaped((model, wide))] if own else []),
        compiler_params=params(),
        cost_estimate=cost((6 if own else 4) * 3 * tokens * model * wide, 30 * 2**20),
        name="feed_own" if own else "feed",
    )(me, *n, *ct, out, fng, w)


def norm_back(v, gain, incoming):
    xhat, r = norm_parts(v)
    scaled = incoming * gain
    grad = r * (
        scaled
        - jnp.mean(scaled, axis=-1, keepdims=True)
        - xhat * jnp.mean(scaled * xhat, axis=-1, keepdims=True)
    )
    return grad, jnp.sum(incoming * xhat, axis=0, keepdims=True), xhat


def leave_kernel(me_ref, came_ref, whole_ref, o_ref):
    o_ref[0] = came_ref[...]


def run_leave(me, mine, came):
    half, model = came.shape
    return pl.pallas_call(
        leave_kernel,
        grid_spec=pltpu.PrefetchScalarGridSpec(
            num_scalar_prefetch=1,
            grid=(half // TILE,),
            in_specs=[
                pl.BlockSpec((TILE, model), lambda t, m: (t, 0)),
                pl.BlockSpec(memory_space=pl.ANY),
            ],
            out_specs=pl.BlockSpec((1, TILE, model), lambda t, m: (1 - (m[0] & 1), t, 0)),
        ),
        out_shape=shaped((2, half, model)),
        input_output_aliases={2: 0},
        compiler_params=params(),
        cost_estimate=cost(1e6, 4 * 2**20),
        name="leave",
    )(me, came, mine)


def exchange(value, axis, flip):
    count = lax.axis_size(axis)
    return lax.ppermute(value, axis, [(i, i ^ flip) for i in range(count)])


def corner(value):
    pairs = []
    for d in range(4):
        for c in range(2):
            pairs.append((d * 2 + c, (d ^ (2 if c == 0 else 1)) * 2 + c))
    return lax.ppermute(value, ("dp", "ctx"), pairs)


def after(values, *earlier):
    return lax.optimization_barrier((tuple(values), earlier))[0]


def sides(block):
    return [exchange(block, "dp", 1), exchange(block, "dp", 2), exchange(block, "ctx", 1)]


def far(from_x, from_y):
    return corner(jnp.where(lax.axis_index("ctx") == 0, from_x, from_y))


def across_cores(*values):
    return [exchange(v, "ctx", 1) for v in values]


def by_distance(block, near, near_other, diagonal, diagonal_other):
    from_x, from_y, other = near
    return [
        block, other, from_x, near_other[0], from_y, near_other[1], diagonal, diagonal_other
    ]


def scatter_core(keep, send):
    return keep + exchange(send, "ctx", 1)


def scatter_corner(mine):
    core = lax.axis_index("ctx")
    own, to_x, to_y, to_d = (mine[:, i] for i in range(4))
    came = corner(to_d)
    return (
        own,
        jnp.where(core == 0, to_x + came, to_x),
        jnp.where(core == 0, to_y, to_y + came),
    )


def scatter_sides(own, to_x, to_y):
    return own + exchange(to_x, "dp", 1) + exchange(to_y, "dp", 2)


def swap_in(block):
    me = lax.axis_index("ctx")
    mine = lax.dynamic_index_in_dim(block, me, 0, keepdims=False)
    came = lax.dynamic_index_in_dim(exchange(block, "ctx", 1), me, 0, keepdims=False)
    return jnp.where(
        me == 0, jnp.concatenate([mine, came], axis=0), jnp.concatenate([came, mine], axis=0)
    )


def by_sequence(
    layer_input, segment_ids, mixer_gain, query_weight, key_weight, value_weight, shift_kernel,
    state_decay, mixer_weight, feed_gain, up_weight, down_weight, cotangent,
):
    plane = ("dp", "ctx")
    position = lax.axis_index("dp") * 2 + lax.axis_index("ctx")
    me = position.astype(jnp.int32).reshape(1)
    rows, own = query_weight.shape
    taps, few = shift_kernel.shape

    def gathered(block):
        return lax.all_gather(block, plane, axis=0, tiled=True)

    a0 = run_pack_mixer(
        me, query_weight, key_weight, value_weight, mixer_weight, mixer_gain, feed_gain,
        shift_kernel, state_decay,
    )
    a1 = exchange(a0, "tensor", 1)
    near0 = sides(a0)
    f0 = run_pack_feed(*after((up_weight, down_weight), a0))
    x_came = exchange(after((layer_input,), a0)[0], "ctx", 1)
    seg = swap_in(segment_ids).astype(f32)

    b0, b1, near0 = after((a0, a1, near0), f0)
    a2 = exchange(b0, "tensor", 2)
    far0 = far(*near0[:2])
    near1 = exchange(b1, "dp", 1), exchange(b1, "dp", 2)
    inner = after((*near0[:2], b1), far0)
    other0 = across_cores(*inner[:2], far0)
    other1 = exchange(inner[2], "ctx", 1)

    b0, b2, near1, seg = after((a0, a2, near1, seg), far0, other0, x_came)
    a3 = exchange(b0, "tensor", 3)
    far1 = far(*near1)
    near2 = exchange(b2, "dp", 1), exchange(b2, "dp", 2)
    inner = after((*near1, b2), far1)
    near1 = (*near1, other1)
    other1 = across_cores(*inner[:2], far1)
    other2 = exchange(inner[2], "ctx", 1)

    g0, b3, near2 = after((f0, a3, near2), far1, other1)
    w0 = gathered(g0)
    far2 = far(*near2)
    near3 = exchange(b3, "dp", 1), exchange(b3, "dp", 2)
    f1 = exchange(g0, "tensor", 1)
    f2 = exchange(g0, "tensor", 2)
    first0 = by_distance(a0, near0, other0[:2], far0, other0[2])
    first1 = by_distance(a1, near1, other1[:2], far1, other1[2])
    x = (layer_input, x_came)
    proj_a, *wa = run_project(me, x, first0, first1)
    inner = after((*near2, b3, far2), proj_a, near3)
    near2 = (*near2, other2)
    other2 = across_cores(*inner[:2], inner[3])
    other3 = exchange(inner[2], "ctx", 1)

    near3, late = after((near3, cotangent), far2, proj_a)
    far3 = far(*near3)
    ct = (cotangent, exchange(late, "ctx", 1))
    segrow = jnp.tile(seg.reshape(-1, 1, BLOCK), (1, 1, PAIR))
    seg = seg[:, None]
    states_a, mixed_a = run_mixer(me, proj_a, seg, segrow, wa[5], taps)
    f1, f2, far3, g0 = after((f1, f2, far3, f0), mixed_a)
    w12 = gathered(jnp.concatenate([f1, f2], axis=1))
    inner = after(near3, far3)
    near3 = (*near3, other3)
    other3 = across_cores(*inner, far3)
    first2 = by_distance(a2, near2, other2[:2], far2, other2[2])
    first3 = by_distance(a3, near3, other3[:2], far3, other3[2])
    proj_b, *wb = run_project(me, x, first2, first3)
    (g0,) = after((g0,), proj_b, ct)
    f3 = exchange(g0, "tensor", 3)

    projs, gains, smalls = (proj_a, proj_b), wa[4], (wa[5], wb[5])
    more = (x, mixed_a, gains, wa[2:4], wb[2:4])
    states_b, resid, nh, nl = run_mixer(me, proj_b, seg, segrow, wb[5], taps, more)
    n = (nh, nl)
    out, fng, feed_g = run_feed(me, n, ct, resid, resid, w0, 1, True)
    (f3,) = after((f3,), fng)
    w3 = gathered(f3)
    out, fng = run_feed(me, n, ct, out, fng, w12, 2, False)
    theirs, out_halves, fng = run_feed(me, n, ct, out, fng, w3, 1, False, True)
    feed_g = lax.psum_scatter(feed_g, plane, scatter_dimension=0, tiled=True)
    came = exchange(theirs, "ctx", 1)
    theirs, halves, keep, send = run_mixer_back(
        me, fng, resid, x, ct, projs, (states_a, states_b), mixed_a, seg, segrow, smalls, gains,
        wa[2:4], wb[2:4], wa[:2], wb[:2], taps,
    )
    layer_output = run_leave(me, out_halves, came)
    core = lax.axis_index("ctx")
    came_send = exchange(send, "ctx", 1)
    diagonal = keep[:, 3] + came_send[:, 3]
    keep, came_send = after((keep, came_send), diagonal)
    diagonal = corner(diagonal)
    came = exchange(theirs, "ctx", 1)
    to_own, to_x, to_y = (keep[:, i] + came_send[:, i] for i in range(3))
    diagonal, to_own, to_x, to_y, came = after((diagonal, to_own, to_x, to_y, came))
    came_x = exchange(jnp.where(core == 0, to_x + diagonal, to_x), "dp", 1)
    came_y = exchange(jnp.where(core == 0, to_y, to_y + diagonal), "dp", 2)
    input_grad = run_leave(me, halves, came)
    mixer_g = (to_own + came_x + came_y)[0]
    few_g, mixer_g = mixer_g[rows:], mixer_g[:rows]
    hidden = up_weight.shape[1]
    return (
        layer_output,
        input_grad,
        few_g[0, :rows],
        mixer_g[:, :own],
        mixer_g[:, own : 2 * own],
        mixer_g[:, 2 * own : 3 * own],
        few_g[2 : 2 + taps, :few],
        mixer_g[:, 3 * own :].T,
        few_g[1, :rows],
        feed_g[:, :hidden],
        feed_g[:, hidden:].T,
    )


def solution(mesh):
    shape = mesh.shape

    def chosen(*arrays):
        rows, length, model = arrays[0].shape
        heads, width = arrays[7].shape
        fits = (
            (shape["dp"], shape["ctx"], shape["tensor"]) == (4, 2, 4)
            and (rows, length) == (2, 2 * TILE)
            and PAIR * width == LANES
            and 2 * heads * width % LANES == 0
        )
        return (by_sequence if fits else on_device)(*arrays)

    return jax.shard_map(
        chosen,
        mesh=mesh,
        in_specs=(
            P("dp", "ctx", None),
            P("dp", "ctx"),
            P(("dp", "ctx")),
            P(("dp", "ctx"), "tensor"),
            P(("dp", "ctx"), "tensor"),
            P(("dp", "ctx"), "tensor"),
            P(None, ("tensor", "dp", "ctx")),
            P("tensor", None),
            P("tensor", ("dp", "ctx")),
            P(("dp", "ctx")),
            P(("dp", "ctx"), "tensor"),
            P("tensor", ("dp", "ctx")),
            P("dp", "ctx", None),
        ),
        out_specs=(
            P("dp", "ctx", None),
            P("dp", "ctx", None),
            P(("dp", "ctx")),
            P(("dp", "ctx"), "tensor"),
            P(("dp", "ctx"), "tensor"),
            P(("dp", "ctx"), "tensor"),
            P(None, ("tensor", "dp", "ctx")),
            P("tensor", ("dp", "ctx")),
            P(("dp", "ctx")),
            P(("dp", "ctx"), "tensor"),
            P("tensor", ("dp", "ctx")),
        ),
        check_vma=False,
    )
```
